128 devices in a mesh: fsdp: 128 (over x, z, y, core).
Axes of the slice: x: 4, y: 4, z: 4, core: 2. Of those that a mesh axis runs over, the one named last changes fastest.
Arguments:
- tokens: bfloat16 [32768, 1024], P('fsdp'), may hold values from -6 to 6
- segments: int32 [256, 128], P('fsdp'), may hold values from -1 to 3, as said below
- grad_out: bfloat16 [32768, 1024], P('fsdp'), may hold values from -24 to 24
- ln1_gain: bfloat16 [1024], P('fsdp'), may hold values from 0.099609375 to 1.8984375
- ln1_bias: bfloat16 [1024], P('fsdp'), may hold values from -4 to 4
- ln2_gain: bfloat16 [1024], P('fsdp'), may hold values from 0.099609375 to 1.8984375
- ln2_bias: bfloat16 [1024], P('fsdp'), may hold values from -4 to 4
- w_qkv: bfloat16 [1024, 3072], P('fsdp'), may hold values from -0.1875 to 0.1875
- b_qkv: bfloat16 [3072], P('fsdp'), may hold values from -4 to 4
- w_dense: bfloat16 [1024, 1024], P('fsdp'), may hold values from -0.75 to 0.75
- b_dense: bfloat16 [1024], P('fsdp'), may hold values from -4 to 4
- w_fc1: bfloat16 [1024, 4096], P('fsdp'), may hold values from -0.1875 to 0.1875
- b_fc1: bfloat16 [4096], P('fsdp'), may hold values from -4 to 4
- w_fc2: bfloat16 [4096, 1024], P('fsdp'), may hold values from -0.09375 to 0.09375
- b_fc2: bfloat16 [1024], P('fsdp'), may hold values from -4 to 4
Outputs:
- out: bfloat16 [32768, 1024], P('fsdp')
- grad_tokens: bfloat16 [32768, 1024], P('fsdp')
- grad_ln1_gain: float32 [1024], P('fsdp')
- grad_ln1_bias: float32 [1024], P('fsdp')
- grad_ln2_gain: float32 [1024], P('fsdp')
- grad_ln2_bias: float32 [1024], P('fsdp')
- grad_w_qkv: float32 [1024, 3072], P('fsdp')
- grad_b_qkv: float32 [3072], P('fsdp')
- grad_w_dense: float32 [1024, 1024], P('fsdp')
- grad_b_dense: float32 [1024], P('fsdp')
- grad_w_fc1: float32 [1024, 4096], P('fsdp')
- grad_b_fc1: float32 [4096], P('fsdp')
- grad_w_fc2: float32 [4096, 1024], P('fsdp')
- grad_b_fc2: float32 [1024], P('fsdp')
The draws below stay inside these ranges and needn't reach their ends.
Inputs may be any that keep to these rules, and one draw needn't show every extreme that they name: `segments`: in each block of 128 rows (one device's micro-batch) the live rows come first with segment numbers that never fall, and padding rows (-1) follow; at least 64 rows of each block are live, and some block has exactly 64; some block, drawn from the seed, holds one sequence of all 128 rows.
All inputs are finite; a program needn't handle non-finite values.
Results may differ from the reference program's by a relative error of at most 0.0096.
Values may be sent and summed in bfloat16 or wider, within the bound.
A program may use at most 192 MiB of HBM per device.

```python
import math
import jax
import jax.numpy as jnp
from jax import lax

D = 1024
HEAD_DIM = 64
ROT = 16
FF = 4096
ROWS = 128
SEQS = 4
BLOCKS = 256
TOKENS = 32768


def draw_segments(key, part):
    key = jax.random.fold_in(key, 7)
    key_live, key_cuts, key_full, key_half = jax.random.split(key, 4)
    block_ids = jnp.arange(BLOCKS, dtype=jnp.int32)
    live_count = jax.random.randint(key_live, (BLOCKS,), ROWS // 2, ROWS + 1)
    full_block = jax.random.randint(key_full, (), 0, BLOCKS)
    half_block = (full_block + 1 + jax.random.randint(key_half, (), 0, BLOCKS - 1)) % BLOCKS
    live_count = jnp.where(block_ids == full_block, ROWS, live_count)
    live_count = jnp.where(block_ids == half_block, ROWS // 2, live_count)
    raw_cuts = jax.random.randint(key_cuts, (BLOCKS, SEQS - 1), 0, ROWS)
    cut_rows = 1 + raw_cuts % (live_count[:, None] - 1)
    cut_rows = jnp.where((block_ids == full_block)[:, None], ROWS, cut_rows)
    row_ids = jnp.arange(ROWS, dtype=jnp.int32)
    seg_ids = jnp.sum((cut_rows[:, None, :] <= row_ids[None, :, None]).astype(jnp.int32), -1)
    return jnp.where(row_ids[None, :] < live_count[:, None], seg_ids, -1).astype(jnp.int32)


def with_spikes(result, rng, source, target, blocks, factor):
    def block_of(axis_at):
        return (jnp.arange(result.shape[axis_at]) // (result.shape[axis_at] // blocks)).reshape((-1,) + (1,) * (result.ndim - 1 - axis_at))

    near = jax.random.permutation(rng, blocks)[block_of(target)]
    other_side = (block_of(target) + blocks // 2) % blocks
    return jnp.where((block_of(source) == near) | (block_of(source) == other_side), factor * result, result)


def block_scale(rng, extent, cuts, low, high):
    def one(dim, shards_of):
        steps = jax.random.uniform(jax.random.fold_in(jax.random.fold_in(rng, 6), dim), (shards_of,), jnp.float32, low / len(cuts), high / len(cuts))
        return jnp.repeat(jnp.exp(steps), extent[dim] // shards_of).reshape((-1,) + (1,) * (len(extent) - dim - 1))

    factor_of = one(*cuts[0])
    for cut in cuts[1:]:
        factor_of = factor_of * one(*cut)
    return factor_of


def normal_values(rng, shape, width, bound, pieces=(), kind=jnp.bfloat16):
    factor_of = block_scale(rng, shape, pieces, -0.22, 0.18) if pieces else 1.0
    values = jax.random.normal(rng, shape, jnp.float32) * width * factor_of
    return jnp.minimum(jnp.maximum(values, -bound), bound).astype(kind)


def heavy_noise(own_key, shape, scale, most, pieces, heavy, kind=jnp.bfloat16):
    array = scale * jax.random.normal(own_key, shape, jnp.float32)
    if pieces:
        array = array * block_scale(own_key, shape, pieces, -0.22, 0.18)
    return jnp.clip(with_spikes(array, jax.random.fold_in(own_key, 3), *heavy), -most, most).astype(kind)


def setup_inputs(seed: int = 0) -> dict:
    arg_keys = jax.random.split(jax.random.key(seed), 16)
    tokens = normal_values(arg_keys[0], (TOKENS, D), 1.0, 6.0, ((0, 128),))
    segments = draw_segments(jax.random.fold_in(arg_keys[15], 71), 0)
    grad_out = heavy_noise(arg_keys[2], (TOKENS, D), 1.0, 24.0, ((0, 128),), (0, 1, 128, 5.5))
    ln1_gain = jnp.clip(1.0 + 0.18 * jax.random.normal(arg_keys[3], (D,), jnp.float32), 0.099609375, 1.8984375).astype(jnp.bfloat16)
    ln1_bias = normal_values(arg_keys[4], (D,), 0.3, 4.0, ((0, 128),))
    ln2_gain = jnp.clip(1.0 + 0.18 * jax.random.normal(arg_keys[5], (D,), jnp.float32), 0.099609375, 1.8984375).astype(jnp.bfloat16)
    ln2_bias = normal_values(arg_keys[6], (D,), 0.3, 4.0, ((0, 128),))
    w_qkv = normal_values(arg_keys[7], (D, 3 * D), D ** -0.5, 0.1875, ((0, 128),))
    b_qkv = normal_values(arg_keys[8], (3 * D,), 0.3, 4.0, ((0, 128),))
    w_dense = normal_values(arg_keys[9], (D, D), (D // 16) ** -0.5, 0.75, ((0, 128),))
    b_dense = normal_values(arg_keys[10], (D,), 0.3, 4.0, ((0, 128),))
    w_fc1 = normal_values(arg_keys[11], (D, FF), D ** -0.5, 0.1875, ((0, 128),))
    b_fc1 = normal_values(arg_keys[12], (FF,), 0.3, 4.0, ((0, 128),))
    w_fc2 = normal_values(arg_keys[13], (FF, D), FF ** -0.5, 0.09375, ((0, 128),))
    b_fc2 = normal_values(arg_keys[14], (D,), 0.3, 4.0, ((0, 128),))
    return {"tokens": tokens, "segments": segments, "grad_out": grad_out, "ln1_gain": ln1_gain, "ln1_bias": ln1_bias, "ln2_gain": ln2_gain, "ln2_bias": ln2_bias, "w_qkv": w_qkv, "b_qkv": b_qkv, "w_dense": w_dense, "b_dense": b_dense, "w_fc1": w_fc1, "b_fc1": b_fc1, "w_fc2": w_fc2, "b_fc2": b_fc2}


@jax.custom_vjp
def low(v):
    return lax.optimization_barrier(v.astype(jnp.bfloat16)).astype(jnp.float32)

@jax.custom_vjp
def low_back(v):
    return v

def low_keep(v):
    return (low(v), None)

def low_pass(kept, grad):
    return (grad,)

def back_keep(v):
    return (v, None)

def back_low(kept, grad):
    return (low(grad),)
low.defvjp(low_keep, low_pass)
low_back.defvjp(back_keep, back_low)
PRECISE = lax.Precision.HIGHEST
NORM_EPS = 1e-05
MASKED = -1e+30

def product(left, right):
    return jnp.dot(left, right, precision=PRECISE, preferred_element_type=jnp.float32)

def layer_norm(values, norm_gain, norm_shift):
    centre = values - lax.optimization_barrier(jnp.mean(values, -1, keepdims=True))
    spread = lax.optimization_barrier(jnp.mean(centre * centre, -1, keepdims=True))
    return centre * lax.rsqrt(spread + NORM_EPS) * norm_gain + norm_shift

def positions_allowed(segment_row):
    row_count = segment_row.shape[0]
    order = jnp.arange(row_count, dtype=jnp.int32)
    allowed = (segment_row[:, None] == segment_row[None, :]) & (order[None, :] <= order[:, None])
    position = lax.optimization_barrier(jnp.sum(allowed.astype(jnp.int32), 1)) - 1
    return (position, allowed)

def rotate(tensor, position, rot_dims):
    half_dims = rot_dims // 2
    inverse_freq = jnp.exp(jnp.arange(half_dims, dtype=jnp.float32) * (-2.0 * math.log(10000.0) / rot_dims))
    angles = position.astype(jnp.float32)[:, None] * inverse_freq[None, :]
    cosine = jnp.cos(angles)[:, None, :]
    sine_wave = jnp.sin(angles)[:, None, :]
    first_half = tensor[..., :half_dims]
    second_half = tensor[..., half_dims:rot_dims]
    return jnp.concatenate([first_half * cosine - second_half * sine_wave, second_half * cosine + first_half * sine_wave, tensor[..., rot_dims:]], -1)

def block_forward(x_rows, segment_row, params):
    gain_one, shift_one, gain_two, shift_two, w_qkv, b_qkv, w_dense, b_dense, w_fc1, b_fc1, w_fc2, b_fc2 = params
    row_count, model_width = x_rows.shape
    head_count = model_width // HEAD_DIM
    shape_heads = (row_count, head_count, HEAD_DIM)
    position, allowed = positions_allowed(segment_row)
    live_rows = (segment_row >= 0).astype(jnp.float32)[:, None]
    normed_one = low(layer_norm(x_rows, gain_one, shift_one))
    normed_two = low(layer_norm(x_rows, gain_two, shift_two))
    joined_qkv = low_back(product(normed_one, w_qkv)) + b_qkv
    queries = low(rotate(joined_qkv[:, :model_width].reshape(shape_heads), position, ROT))
    keys_rot = low(rotate(joined_qkv[:, model_width:2 * model_width].reshape(shape_heads), position, ROT))
    values_in = low(joined_qkv[:, 2 * model_width:].reshape(shape_heads))
    scores = low_back(jnp.einsum('qhd,khd->hqk', queries, keys_rot, precision=PRECISE) * HEAD_DIM ** (-0.5))
    scores = jnp.where(allowed[None], scores, MASKED)
    exp_scores = jnp.exp(scores - lax.optimization_barrier(jnp.max(scores, -1, keepdims=True)))
    attn_probs = exp_scores / lax.optimization_barrier(jnp.sum(exp_scores, -1, keepdims=True))
    context = jnp.einsum('hqk,khd->qhd', low(attn_probs), values_in, precision=PRECISE).reshape(row_count, model_width)
    context = low(low_back(context))
    attention = product(context, w_dense) + b_dense
    hidden = low_back(product(normed_two, w_fc1)) + b_fc1
    active = low(jax.nn.gelu(hidden, approximate=False))
    feed_out = product(active, w_fc2) + b_fc2
    return x_rows + live_rows * (attention + feed_out)

def forward(x_all, segments, params):
    group_size = math.gcd(BLOCKS, max(1, 4096 // ROWS))
    group_count = BLOCKS // group_size
    x_groups = x_all.reshape(group_count, group_size, ROWS, x_all.shape[-1])
    seg_groups = segments.reshape(group_count, group_size, ROWS)
    group_fn = jax.checkpoint(lambda group_x, group_seg, group_params: jax.vmap(block_forward, (0, 0, None))(group_x, group_seg, group_params))
    outputs = lax.map(lambda pair_items: group_fn(pair_items[0], pair_items[1], params), (x_groups, seg_groups))
    return outputs.reshape(x_all.shape)

def reference(tokens, segments, grad_out, ln1_gain, ln1_bias, ln2_gain, ln2_bias, w_qkv, b_qkv, w_dense, b_dense, w_fc1, b_fc1, w_fc2, b_fc2):
    params = tuple((member.astype(jnp.float32) for member in (ln1_gain, ln1_bias, ln2_gain, ln2_bias, w_qkv, b_qkv, w_dense, b_dense, w_fc1, b_fc1, w_fc2, b_fc2)))
    x_all = tokens.astype(jnp.float32)
    out_all, pull_back = jax.vjp(lambda x_in, *weights_in: forward(x_in, segments, weights_in), x_all, *params)
    grads = pull_back(grad_out.astype(jnp.float32))
    return (out_all.astype(jnp.bfloat16), grads[0].astype(jnp.bfloat16), grads[1], grads[2], grads[3], grads[4], grads[5], grads[6], grads[7], grads[8], grads[9], grads[10], grads[11], grads[12])
```

```python
import functools
import math

import jax
import jax.numpy as jnp
import numpy as np
from jax import lax
from jax.experimental import pallas as pl
from jax.experimental.pallas import tpu as pltpu
from jax.sharding import PartitionSpec as P

NORM_EPS = 1e-05
MASKED = -1e30
MESH = pl.DeviceIdType.MESH
BF = jnp.bfloat16
F32 = jnp.float32
VMEM_LIMIT = 60 * 1024 * 1024


def coords():
    i = lax.axis_index("fsdp")
    core = lax.rem(i, 2)
    y = lax.rem(i // 2, 4)
    z = lax.rem(i // 8, 4)
    x = i // 32
    return x, z, y, core


def ident(x, z, y, core):
    return ((x * 4 + z) * 4 + y) * 2 + core


class Ring:
    def __init__(self, at, core):
        step = 1 + 2 * core
        self.own = at
        self.fwd = lax.rem(at + step, 4)
        self.bwd = lax.rem(at + 4 - step, 4)
        self.opp = lax.rem(at + 2, 4)


class Messages:
    def __init__(self, send_sem, recv_sem):
        self.send_sem, self.recv_sem = send_sem, recv_sem
        self.sent, self.landed = {}, set()

    def send(self, name, src, dst, target):
        n = len(self.sent)
        copy = pltpu.make_async_remote_copy(
            src_ref=src,
            dst_ref=dst,
            send_sem=self.send_sem.at[n],
            recv_sem=self.recv_sem.at[n],
            device_id=(target,),
            device_id_type=MESH,
        )
        copy.start()
        self.sent[name] = copy

    def land(self, name):
        assert name not in self.landed
        self.landed.add(name)
        self.sent[name].wait_recv()

    def finish(self):
        for name, copy in self.sent.items():
            if name not in self.landed:
                copy.wait_recv()
        for copy in self.sent.values():
            copy.wait_send()


def enter(targets):
    barrier = pltpu.get_barrier_semaphore()
    for target in targets:
        pl.semaphore_signal(barrier, inc=1, device_id=(target,), device_id_type=MESH)
    pl.semaphore_wait(barrier, len(targets))


def group_member(x, z, t):
    return ident(x, z, 0, 0) + t


GATHER_MESSAGES = 7 + 7 + 2 * 7 + 2 * (3 + 12)
PARTS = (("a", 0, 7), ("b", 7, 13))


def gather_kernel(x_ref, dy_ref, seg_ref, wl_ref, rest_ref, X, DY, SEG, WB, send_sem, recv_sem, local_sem):
    x, z, y, core = coords()
    t = y * 2 + core
    ring_y, ring_x, ring_z = Ring(y, core), Ring(x, core), Ring(z, core)
    y_dev = lambda to: ident(x, z, to, core)
    x_dev = lambda to: ident(to, z, y, core)
    z_dev = lambda to: ident(x, to, y, core)
    sibling = ident(x, z, y, 1 - core)
    others = [lax.rem(t + k, 8) for k in range(1, 8)]

    enter(
        [group_member(x, z, o) for o in others]
        + [x_dev(ring_x.fwd), x_dev(ring_x.bwd), z_dev(ring_z.fwd), z_dev(ring_z.bwd)]
    )
    msgs = Messages(send_sem, recv_sem)

    local = [
        pltpu.make_async_copy(wl_ref.at[t], WB.at[x, z, t], local_sem.at[0]),
        pltpu.make_async_copy(rest_ref, WB.at[x, z, pl.ds(8, 5)], local_sem.at[1]),
        pltpu.make_async_copy(x_ref, X.at[t], local_sem.at[2]),
        pltpu.make_async_copy(dy_ref, DY.at[t], local_sem.at[3]),
        pltpu.make_async_copy(seg_ref, SEG.at[t], local_sem.at[4]),
    ]
    for copy in local:
        copy.start()
    for k, o in enumerate(others):
        msgs.send(("w", k), wl_ref.at[o], WB.at[x, z, t], group_member(x, z, o))
    rows = (("x", x_ref, X), ("d", dy_ref, DY))

    def own_rows(name, src, dst):
        msgs.send((name, 0), src, dst.at[t], y_dev(ring_y.fwd))
        msgs.send((name, 1), src, dst.at[t], y_dev(ring_y.bwd))
        msgs.send((name, 2), src, dst.at[t], sibling)

    own_rows(*rows[0])
    for k, o in enumerate(others):
        msgs.send(("s", k), seg_ref, SEG.at[t], group_member(x, z, o))
    own_rows(*rows[1])
    for copy in local:
        copy.wait()
    for k in range(7):
        msgs.land(("w", k))

    def piece(half, p, q):
        name, lo, hi = half
        if name == "a":
            return WB.at[p, q, pl.ds(lo, hi - lo)]
        return WB.at[q, p, pl.ds(lo, hi - lo)]

    def axes(half):
        if half[0] == "a":
            return ring_x, x_dev, ring_z, z_dev
        return ring_z, z_dev, ring_x, x_dev

    def first(half, k, at, to):
        one, one_dev, two, _ = axes(half)
        ref = piece(half, at, two.own)
        msgs.send((half[0], "p", k), ref, ref, one_dev(to))

    def second(half, sub, k, at, frm, to):
        _, _, two, two_dev = axes(half)
        ref = piece(half, at, frm)
        msgs.send((half[0], sub, k), ref, ref, two_dev(to))

    def spread(half, sub, at):
        two = axes(half)[2]
        second(half, sub, 0, at, two.own, two.fwd)
        second(half, sub, 1, at, two.own, two.bwd)

    def pass_on(half, sub):
        one, _, two, _ = axes(half)
        msgs.land((half[0], sub, 0))
        second(half, sub, 2, getattr(one, sub), two.bwd, two.fwd)

    for half in PARTS:
        one = axes(half)[0]
        first(half, 0, one.own, one.fwd)
        first(half, 1, one.own, one.bwd)
        spread(half, "own", one.own)
    for half in PARTS:
        one = axes(half)[0]
        msgs.land((half[0], "p", 0))
        first(half, 2, one.bwd, one.fwd)
        spread(half, "bwd", one.bwd)
    for half in PARTS:
        msgs.land((half[0], "p", 1))
        spread(half, "fwd", axes(half)[0].fwd)
    for half in PARTS:
        msgs.land((half[0], "p", 2))
        spread(half, "opp", axes(half)[0].opp)
    for half in PARTS:
        pass_on(half, "own")

    slot = lambda at: at * 2 + core

    def rows_on(name, dst):
        msgs.land((name, 0))
        ref = dst.at[slot(ring_y.bwd)]
        msgs.send((name, 3), ref, ref, y_dev(ring_y.fwd))
        msgs.send((name, 4), ref, ref, sibling)
        msgs.land((name, 1))
        ref = dst.at[slot(ring_y.fwd)]
        msgs.send((name, 5), ref, ref, sibling)

    def rows_last(name, dst):
        msgs.land((name, 3))
        ref = dst.at[slot(ring_y.opp)]
        msgs.send((name, 6), ref, ref, sibling)

    rows_on("x", X)
    for sub in ("bwd", "fwd", "opp"):
        for half in PARTS:
            pass_on(half, sub)
    rows_on("d", DY)
    rows_last("x", X)
    rows_last("d", DY)
    msgs.finish()


def gather(x, dy, seg, wl, rest):
    any_spec = pl.BlockSpec(memory_space=pl.ANY)
    return pl.pallas_call(
        gather_kernel,
        out_shape=(
            jax.ShapeDtypeStruct((8, 256, 1024), BF),
            jax.ShapeDtypeStruct((8, 256, 1024), BF),
            jax.ShapeDtypeStruct((8, 2, 128), jnp.int32),
            jax.ShapeDtypeStruct((4, 4, 13, 8, 1024), BF),
        ),
        in_specs=[any_spec] * 5,
        out_specs=(any_spec,) * 4,
        scratch_shapes=[
            pltpu.SemaphoreType.DMA((GATHER_MESSAGES,)),
            pltpu.SemaphoreType.DMA((GATHER_MESSAGES,)),
            pltpu.SemaphoreType.DMA((5,)),
        ],
        compiler_params=pltpu.CompilerParams(collective_id=0, has_side_effects=True),
        name="gather_rows_and_weights",
    )(x, dy, seg, wl, rest)


def dot(a, b):
    return jnp.dot(a, b, preferred_element_type=F32)


def dot_nt(a, b):
    return lax.dot_general(a, b, (((1,), (1,)), ((), ())), preferred_element_type=F32)


def dot_tn(a, b):
    return lax.dot_general(a, b, (((0,), (0,)), ((), ())), preferred_element_type=F32)


def turn(u, cosine, sine, low_lanes):
    moved = jnp.where(low_lanes, pltpu.roll(u, 120, 1), pltpu.roll(u, 8, 1))
    return u * cosine + moved * sine


def block_kernel(x_ref, dy_ref, seg_ref, w1_ref, w2_ref, ln_ref, bias_ref, table_ref,
                 out_ref, g_ref, grad_ref, sum_ref, acc_n, acc_c, acc_s):
    step = pl.program_id(0)
    first, last = step == 0, step == pl.num_programs(0) - 1

    @pl.when(first)
    def _():
        acc_n[...] = jnp.zeros_like(acc_n)
        acc_c[...] = jnp.zeros_like(acc_c)
        acc_s[...] = jnp.zeros_like(acc_s)

    x = x_ref[0].astype(F32)
    centre = x - jnp.mean(x, 1, keepdims=True)
    spread = jnp.mean(centre * centre, 1, keepdims=True)
    normed = centre * lax.rsqrt(spread + NORM_EPS)
    g1, g2 = ln_ref[0:1, :], ln_ref[2:3, :]
    a1 = (normed * g1 + ln_ref[1:2, :]).astype(BF)
    a2 = (normed * g2 + ln_ref[3:4, :]).astype(BF)
    normed_b = normed.astype(BF)
    joined = dot(a1, w1_ref[:, 0:384]) + bias_ref[:, 0:384]
    hidden = dot(a2, w1_ref[:, 384:896]) + bias_ref[:, 384:896]
    phi_cdf = 0.5 + 0.5 * lax.erf(hidden * math.sqrt(0.5))
    active = (hidden * phi_cdf).astype(BF)
    slope = phi_cdf + hidden * (jnp.exp(hidden * hidden * -0.5) * (1.0 / math.sqrt(2.0 * math.pi)))

    row = lax.broadcasted_iota(jnp.int32, (128, 128), 0)
    col = lax.broadcasted_iota(jnp.int32, (128, 128), 1)
    masks, lives, tables = [], [], []
    for b in range(2):
        seg_c = jnp.broadcast_to(seg_ref[0, b : b + 1, :].astype(F32), (128, 128))
        seg_r = seg_c.T
        allowed = (seg_c == seg_r) & (col <= row)
        position = jnp.sum(allowed.astype(F32), 1, keepdims=True) - 1.0
        onehot = (col == position.astype(jnp.int32)).astype(BF)
        tables.append(dot(onehot, table_ref[...]))
        masks.append(allowed)
        lives.append((seg_r[:, 0:1] >= 0.0).astype(F32))
    dy = dy_ref[0].astype(F32) * jnp.concatenate(lives, 0)
    branch = dy.astype(BF)
    d_cat = dot_nt(branch, w2_ref[...])
    d_hidden = d_cat[:, 128:640] * slope
    d_context = d_cat[:, 0:128].astype(BF)

    lane = lax.broadcasted_iota(jnp.int32, (128, 128), 1)
    low_lanes = lax.rem(lane, 64) < 8
    head0 = lane < 64

    def stacked(u):
        zero = jnp.zeros_like(u)
        return jnp.concatenate([jnp.where(head0, u, zero), jnp.where(head0, zero, u)], 0)

    contexts, d_joined = [], []
    for b in range(2):
        part = slice(b * 128, b * 128 + 128)
        cosine = tables[b][:, 0:128] + tables[b][:, 128:256]
        sine = tables[b][:, 256:384] + tables[b][:, 384:512]
        q = turn(joined[part, 0:128], cosine, sine, low_lanes).astype(BF)
        k = turn(joined[part, 128:256], cosine, sine, low_lanes).astype(BF)
        v = joined[part, 256:384].astype(BF)
        q2 = stacked(q)
        allowed = jnp.concatenate([masks[b], masks[b]], 0)
        scores = jnp.where(allowed, dot_nt(q2, k) * 0.125, MASKED)
        e = jnp.exp(scores - jnp.max(scores, 1, keepdims=True))
        probs = e / jnp.sum(e, 1, keepdims=True)
        probs_b = probs.astype(BF)
        ctx = dot(probs_b, v)
        contexts.append(jnp.where(head0, ctx[0:128], ctx[128:256]).astype(BF))
        dc2 = stacked(d_context[part])
        d_probs = dot_nt(dc2, v)
        d_v = dot_tn(probs_b, dc2)
        d_scores = probs * (d_probs - jnp.sum(probs * d_probs, 1, keepdims=True))
        d_scores = d_scores.astype(BF)
        dq2 = dot(d_scores, k) * 0.125
        d_q = jnp.where(head0, dq2[0:128], dq2[128:256])
        d_k = dot_tn(d_scores, q2) * 0.125
        d_joined.append(
            jnp.concatenate(
                [turn(d_q, cosine, -sine, low_lanes), turn(d_k, cosine, -sine, low_lanes), d_v], 1
            )
        )
    cat = jnp.concatenate([jnp.concatenate(contexts, 0), active], 1)
    out_ref[0] = dot(cat, w2_ref[...]).astype(BF)
    acc_c[...] += dot_tn(cat, branch)
    d_all = jnp.concatenate([jnp.concatenate(d_joined, 0), d_hidden], 1)
    acc_s[0:1, 0:896] += jnp.sum(d_all, 0, keepdims=True)
    acc_s[1:2, :] += jnp.sum(dy, 0, keepdims=True)
    d_all_b = d_all.astype(BF)
    acc_n[...] += dot_tn(normed_b, d_all_b)
    g = g1 * dot_nt(d_all_b[:, 0:384], w1_ref[:, 0:384]) + g2 * dot_nt(d_all_b[:, 384:896], w1_ref[:, 384:896])
    g_ref[0] = g.astype(BF)

    @pl.when(last)
    def _():
        grad_ref[:, 0:64, 0:896] = acc_n[...].reshape(16, 64, 896).astype(BF)
        grad_ref[:, 64:96, :] = acc_c[128:640, :].reshape(16, 32, 1024).astype(BF)
        dense = acc_c[0:128, :].reshape(16, 8, 1024)
        for j in range(4):
            pair = [dense[:, :, i * 128 : i * 128 + 128] for i in (2 * j, 2 * j + 1)]
            grad_ref[:, 16 * j : 16 * j + 16, 896:1024] = jnp.concatenate(pair, 1).astype(BF)
        sum_ref[...] = acc_s[...]


def rotary_table():
    m = 8
    angle = np.arange(128, dtype=np.float64)[:, None] * (10000.0 ** (-2.0 * np.arange(m) / 16.0))[None, :]
    cosine = np.ones((128, 128), np.float32)
    sine = np.zeros((128, 128), np.float32)
    for head in (0, 64):
        cosine[:, head : head + m] = np.cos(angle)
        cosine[:, head + m : head + 2 * m] = np.cos(angle)
        sine[:, head : head + m] = -np.sin(angle)
        sine[:, head + m : head + 2 * m] = np.sin(angle)
    parts = []
    for table in (cosine, sine):
        high = table.astype(jnp.bfloat16)
        parts += [high, (table - high.astype(np.float32)).astype(jnp.bfloat16)]
    return np.concatenate(parts, 1)


def block(x, dy, seg, w1, w2, ln, bias):
    whole = lambda shape: pl.BlockSpec(shape, lambda s: (0,) * len(shape))
    rows = pl.BlockSpec((1, 256, 1024), lambda s: (s, 0, 0))
    return pl.pallas_call(
        block_kernel,
        grid=(8,),
        out_shape=(
            jax.ShapeDtypeStruct((8, 256, 1024), BF),
            jax.ShapeDtypeStruct((8, 256, 1024), BF),
            jax.ShapeDtypeStruct((16, 96, 1024), BF),
            jax.ShapeDtypeStruct((8, 1024), F32),
        ),
        in_specs=[
            rows, rows, pl.BlockSpec((1, 2, 128), lambda s: (s, 0, 0)),
            whole((1024, 1024)), whole((640, 1024)), whole((4, 1024)), whole((1, 896)), whole((128, 512)),
        ],
        out_specs=(rows, rows, whole((16, 96, 1024)), whole((8, 1024))),
        scratch_shapes=[
            pltpu.VMEM((1024, 896), F32),
            pltpu.VMEM((640, 1024), F32),
            pltpu.VMEM((8, 1024), F32),
        ],
        compiler_params=pltpu.CompilerParams(
            dimension_semantics=("arbitrary",), vmem_limit_bytes=VMEM_LIMIT
        ),
        cost_estimate=pl.CostEstimate(flops=20_000_000_000, bytes_accessed=25_000_000, transcendentals=3_000_000),
        name="block_forward_backward",
    )(x, dy, seg, w1, w2, ln, bias, jnp.asarray(rotary_table()))


def slabs(rows, step, fn):
    def one(i, carry):
        fn(pl.ds(pl.multiple_of(i * step, step), step))
        return carry

    lax.fori_loop(0, rows // step, one, 0)


SUM_MESSAGES = 3 + 3 + 7 + 2 * (4 + 3) + 2 * 6 + 7


def sum_kernel(out_ref, g_ref, blob_ref, vec_ref,
               out_sum, g_sum, all_ref, own_ref, vec_all,
               sib, held, from_y, from_one, held_one, from_two, held_two, held_last, vec_one, vec_sum, vec_two,
               send_sem, recv_sem):
    x, z, y, core = coords()
    t = y * 2 + core
    ring_y, ring_x, ring_z = Ring(y, core), Ring(x, core), Ring(z, core)
    y_dev = lambda to: ident(x, z, to, core)
    x_dev = lambda to: ident(to, z, y, core)
    z_dev = lambda to: ident(x, to, y, core)
    sibling = ident(x, z, y, 1 - core)
    others = [lax.rem(t + k, 8) for k in range(1, 8)]
    x_others = [lax.rem(x + k, 4) for k in range(1, 4)]
    z_others = [lax.rem(z + k, 4) for k in range(1, 4)]
    enter(
        [group_member(x, z, o) for o in others]
        + [x_dev(o) for o in x_others]
        + [z_dev(o) for o in z_others]
    )
    msgs = Messages(send_sem, recv_sem)
    mine = lambda at: at * 2 + core
    hers = lambda at: at * 2 + 1 - core

    arrays = ((0, out_ref, out_sum), (1, g_ref, g_sum))

    def to_sibling(a, src, role):
        at = getattr(ring_y, role)
        msgs.send(("sib", a, role), src.at[hers(at)], sib.at[a, at], sibling)

    for a, src, _ in arrays:
        to_sibling(a, src, "opp")

    def half(name):
        if name == "a":
            return ring_x, x_dev, ring_z, z_dev, (lambda p: blob_ref.at[p, :, pl.ds(0, 48)]), 0
        return ring_z, z_dev, ring_x, x_dev, (lambda p: blob_ref.at[:, p, pl.ds(48, 48)]), 1

    for k, o in enumerate(x_others):
        msgs.send(("v1", k), vec_ref, vec_one.at[k], x_dev(o))
    for name in "ab":
        one, one_dev, _, _, part, h = half(name)
        msgs.send((name, "one", 0), part(one.opp), from_one.at[h, 0], one_dev(one.fwd))
        msgs.send((name, "one", 1), part(one.bwd), from_one.at[h, 1], one_dev(one.bwd))
    for role in ("fwd", "bwd", "own"):
        for a, src, _ in arrays:
            to_sibling(a, src, role)

    def gathered(a, src, role, slot, extra=None):
        at = getattr(ring_y, role)

        def add(r):
            v = src[mine(at), r, :].astype(F32) + sib[a, at, r, :].astype(F32)
            if extra is not None:
                v = v + from_y[a, extra, r, :].astype(F32)
            held[a, slot, r, :] = v.astype(BF)

        slabs(256, 32, add)

    for a, src, _ in arrays:
        msgs.land(("sib", a, "opp"))
        gathered(a, src, "opp", 0)
        msgs.send(("y", a, 0), held.at[a, 0], from_y.at[a, 0], y_dev(ring_y.fwd))
    for a, src, _ in arrays:
        msgs.land(("sib", a, "fwd"))
        gathered(a, src, "bwd", 1)
        msgs.send(("y", a, 1), held.at[a, 1], from_y.at[a, 1], y_dev(ring_y.bwd))

    def first_forward(name):
        one, one_dev, _, _, part, h = half(name)
        msgs.land((name, "one", 0))
        block_of = part(one.fwd)

        def add(r):
            held_one[h, :, r, :] = (block_of[:, r, :].astype(F32) + from_one[h, 0, :, r, :].astype(F32)).astype(BF)

        slabs(48, 16, add)
        msgs.send((name, "one", 2), held_one.at[h], from_one.at[h, 2], one_dev(one.fwd))

    for name in "ab":
        first_forward(name)

    for k in range(3):
        msgs.land(("v1", k))
    vec_sum[...] = vec_ref[...] + vec_one[0] + vec_one[1] + vec_one[2]
    for k, o in enumerate(z_others):
        msgs.send(("v2", k), vec_sum, vec_two.at[k], z_dev(o))

    for a, src, _ in arrays:
        msgs.land(("sib", a, "bwd"))
        msgs.land(("y", a, 0))
        gathered(a, src, "fwd", 2, extra=0)
        msgs.send(("y", a, 2), held.at[a, 2], from_y.at[a, 2], y_dev(ring_y.fwd))

    def first_total(name):
        one, _, two, two_dev, part, h = half(name)
        msgs.land((name, "one", 1))
        msgs.land((name, "one", 2))
        block_of = part(one.own)

        def add(r):
            v = block_of[:, r, :].astype(F32) + from_one[h, 1, :, r, :].astype(F32)
            held_two[h, :, r, :] = (v + from_one[h, 2, :, r, :].astype(F32)).astype(BF)

        slabs(48, 16, add)
        msgs.send((name, "two", 0), held_two.at[h, two.opp], from_two.at[h, 0], two_dev(two.fwd))
        msgs.send((name, "two", 1), held_two.at[h, two.bwd], from_two.at[h, 1], two_dev(two.bwd))

    for name in "ab":
        first_total(name)

    for k in range(3):
        msgs.land(("v2", k))
    vec_all[t] = vec_sum[...] + vec_two[0] + vec_two[1] + vec_two[2]
    for k, o in enumerate(others):
        msgs.send(("v3", k), vec_all.at[t], vec_all.at[t], group_member(x, z, o))

    for name in "ab":
        _, _, two, two_dev, _, h = half(name)
        msgs.land((name, "two", 0))
        held_last[h] = (held_two[h, two.fwd].astype(F32) + from_two[h, 0].astype(F32)).astype(BF)
        msgs.send((name, "two", 2), held_last.at[h], from_two.at[h, 2], two_dev(two.fwd))

    for a, src, dst in arrays:
        msgs.land(("sib", a, "own"))
        msgs.land(("y", a, 1))
        msgs.land(("y", a, 2))

        def add(r, a=a, src=src, dst=dst):
            v = src[mine(y), r, :].astype(F32) + sib[a, y, r, :].astype(F32)
            dst[r, :] = v + from_y[a, 1, r, :].astype(F32) + from_y[a, 2, r, :].astype(F32)

        slabs(256, 32, add)

    for name in "ab":
        _, _, two, _, _, h = half(name)
        msgs.land((name, "two", 1))
        msgs.land((name, "two", 2))
        v = held_two[h, two.own].astype(F32) + from_two[h, 1].astype(F32) + from_two[h, 2].astype(F32)
        own_ref[h * 6 : h * 6 + 6] = v.reshape(6, 8, 1024)
    for k, o in enumerate(others):
        msgs.send(("n", k), own_ref.at[o], all_ref.at[t], group_member(x, z, o))
    all_ref[t] = own_ref[t]
    msgs.finish()


def add_up(out_part, g_part, blob, vec):
    vmem = pl.BlockSpec(memory_space=pltpu.VMEM)
    return pl.pallas_call(
        sum_kernel,
        out_shape=(
            jax.ShapeDtypeStruct((256, 1024), F32),
            jax.ShapeDtypeStruct((256, 1024), F32),
            jax.ShapeDtypeStruct((8, 8, 1024), F32),
            jax.ShapeDtypeStruct((12, 8, 1024), F32),
            jax.ShapeDtypeStruct((8, 8, 256), F32),
        ),
        in_specs=[vmem] * 4,
        out_specs=(vmem,) * 5,
        scratch_shapes=[
            pltpu.VMEM((2, 4, 256, 1024), BF),
            pltpu.VMEM((2, 3, 256, 1024), BF),
            pltpu.VMEM((2, 3, 256, 1024), BF),
            pltpu.VMEM((2, 3, 4, 48, 1024), BF),
            pltpu.VMEM((2, 4, 48, 1024), BF),
            pltpu.VMEM((2, 3, 48, 1024), BF),
            pltpu.VMEM((2, 4, 48, 1024), BF),
            pltpu.VMEM((2, 48, 1024), BF),
            pltpu.VMEM((3, 8, 256), F32),
            pltpu.VMEM((8, 256), F32),
            pltpu.VMEM((3, 8, 256), F32),
            pltpu.SemaphoreType.DMA((SUM_MESSAGES,)),
            pltpu.SemaphoreType.DMA((SUM_MESSAGES,)),
        ],
        compiler_params=pltpu.CompilerParams(
            collective_id=1, has_side_effects=True, vmem_limit_bytes=VMEM_LIMIT
        ),
        name="sum_rows_and_gradients",
    )(out_part, g_part, blob, vec)


def body(tokens, segments, grad_out, ln1_gain, ln1_bias, ln2_gain, ln2_bias, w_qkv, b_qkv,
         w_dense, b_dense, w_fc1, b_fc1, w_fc2, b_fc2):
    me = lax.axis_index("fsdp")
    t = lax.rem(me, 8)

    dense = lax.ppermute(w_dense, "fsdp", [(d, (d % 16) * 8 + d // 16) for d in range(128)])
    small = jnp.concatenate(
        [ln1_gain, ln1_bias, ln2_gain, ln2_bias, b_qkv, b_fc1, b_dense, b_fc2, jnp.zeros((24,), BF)]
    )
    qkv_parts = w_qkv.reshape(8, 3, 8, 128).transpose(2, 0, 1, 3).reshape(8, 8, 384)
    fc1_parts = w_fc1.reshape(8, 16, 8, 32).transpose(2, 0, 1, 3).reshape(8, 8, 512)
    wl = jnp.concatenate([qkv_parts, fc1_parts, jnp.broadcast_to(small, (8, 8, 128))], -1)
    rest = jnp.concatenate([dense[None], w_fc2.reshape(4, 8, 1024)], 0)
    x_all, dy_all, seg_all, blob = gather(tokens, grad_out, segments, wl, rest)

    blob = blob.reshape(16, 13, 8, 1024)
    w1 = blob[:, 0:8].reshape(1024, 1024)
    w2 = jnp.concatenate([blob[:, 8].reshape(128, 1024), blob[:, 9:13].reshape(512, 1024)], 0)
    small = blob[:, 0:8, 0, 896:1000].reshape(128, 104)
    ln = small[:, 0:32].reshape(128, 4, 8).transpose(1, 0, 2).reshape(4, 1024).astype(F32)
    b_one = lax.dynamic_index_in_dim(small[:, 32:56].reshape(3, 8, 128), t, 1, False).reshape(384)
    b_two = lax.dynamic_index_in_dim(small[:, 56:88].reshape(16, 8, 32), t, 1, False).reshape(512)
    bias = jnp.concatenate([b_one, b_two])[None].astype(F32)
    b_out = (small[:, 88:96].astype(F32) + small[:, 96:104].astype(F32)).reshape(1024)

    out_part, g_part, grads, sums = block(x_all, dy_all, seg_all, w1, w2, ln, bias)
    out_sum, g_sum, n_all, own, sums = add_up(
        out_part, g_part, grads.reshape(4, 4, 96, 1024), sums[0:2].reshape(8, 256)
    )

    live = (segments.reshape(256, 1) >= 0).astype(F32)
    x = tokens.astype(F32)
    out = (x + live * (out_sum + b_out)).astype(BF)
    centre = x - jnp.mean(x, -1, keepdims=True)
    scale = lax.rsqrt(jnp.mean(centre * centre, -1, keepdims=True) + NORM_EPS)
    normed = centre * scale
    dx = (g_sum - jnp.mean(g_sum, -1, keepdims=True) - normed * jnp.mean(g_sum * normed, -1, keepdims=True)) * scale
    grad_tokens = (grad_out.astype(F32) + dx).astype(BF)

    sums = sums.reshape(8, 2, 1024)
    sum_qkv = sums[:, 0, 0:384].reshape(8, 3, 128).transpose(1, 0, 2).reshape(3072)
    sum_fc1 = sums[:, 0, 384:896].reshape(8, 16, 32).transpose(1, 0, 2).reshape(4096)
    n_qkv = n_all[:, :, 0:384].reshape(8, 8, 3, 128).transpose(1, 2, 0, 3).reshape(8, 3072)
    n_fc1 = n_all[:, :, 384:896].reshape(8, 8, 16, 32).transpose(1, 2, 0, 3).reshape(8, 4096)

    def norm_grads(weight, n, s, gain, bias_of):
        weight = weight.astype(F32)
        grad_w = gain.astype(F32)[:, None] * n + bias_of.astype(F32)[:, None] * s
        return jnp.sum(weight * n, 1), jnp.sum(weight * s, 1), grad_w

    g1_gain, g1_bias, grad_qkv = norm_grads(w_qkv, n_qkv, sum_qkv, ln1_gain, ln1_bias)
    g2_gain, g2_bias, grad_fc1 = norm_grads(w_fc1, n_fc1, sum_fc1, ln2_gain, ln2_bias)
    grad_b_qkv = lax.dynamic_slice(sum_qkv, (me * 24,), (24,))
    grad_b_fc1 = lax.dynamic_slice(sum_fc1, (me * 32,), (32,))
    grad_b_out = lax.dynamic_slice(sums[0, 1], (me * 8,), (8,))
    grad_dense = lax.ppermute(own[0:8, :, 896:1024], "fsdp", [(d, (d % 8) * 16 + d // 8) for d in range(128)])
    grad_dense = grad_dense.transpose(1, 0, 2).reshape(8, 1024)
    grad_fc2 = own[8:12].reshape(32, 1024)
    return (out, grad_tokens, g1_gain, g1_bias, g2_gain, g2_bias, grad_qkv, grad_b_qkv,
            grad_dense, grad_b_out, grad_fc1, grad_b_fc1, grad_fc2, grad_b_out)


def solution(mesh):
    rows, flat = P("fsdp", None), P("fsdp")
    return jax.shard_map(
        body,
        mesh=mesh,
        in_specs=(rows, rows, rows, flat, flat, flat, flat, rows, flat, rows, flat, rows, flat, rows, flat),
        out_specs=(rows, rows, flat, flat, flat, flat, rows, flat, rows, flat, rows, flat, rows, flat),
        check_vma=False,
    )
```

```python
import functools
import math

import jax
import jax.numpy as jnp
import numpy as np
from jax import lax
from jax.experimental import pallas as pl
from jax.experimental.pallas import tpu as pltpu
from jax.sharding import PartitionSpec as P

NORM_EPS = 1e-05
MASKED = -1e30
MESH = pl.DeviceIdType.MESH
BF = jnp.bfloat16
F32 = jnp.float32
VMEM_LIMIT = 60 * 1024 * 1024


def coords():
    i = lax.axis_index("fsdp")
    core = lax.rem(i, 2)
    y = lax.rem(i // 2, 4)
    z = lax.rem(i // 8, 4)
    x = i // 32
    return x, z, y, core


def ident(x, z, y, core):
    return ((x * 4 + z) * 4 + y) * 2 + core


class Ring:
    def __init__(self, at, core):
        step = 1 + 2 * core
        self.own = at
        self.fwd = lax.rem(at + step, 4)
        self.bwd = lax.rem(at + 4 - step, 4)
        self.opp = lax.rem(at + 2, 4)


class Messages:
    def __init__(self, send_sem, recv_sem):
        self.send_sem, self.recv_sem = send_sem, recv_sem
        self.sent, self.landed = {}, set()

    def plan(self, name, src, dst, target):
        n = len(self.sent)
        copy = pltpu.make_async_remote_copy(
            src_ref=src,
            dst_ref=dst,
            send_sem=self.send_sem.at[n],
            recv_sem=self.recv_sem.at[n],
            device_id=(target,),
            device_id_type=MESH,
        )
        self.sent[name] = copy

    def send(self, name, src, dst, target):
        self.plan(name, src, dst, target)
        self.sent[name].start()

    def land(self, name):
        assert name not in self.landed
        self.landed.add(name)
        self.sent[name].wait_recv()

    def finish(self):
        for name, copy in self.sent.items():
            if name not in self.landed:
                copy.wait_recv()
        for copy in self.sent.values():
            copy.wait_send()


def enter(targets):
    barrier = pltpu.get_barrier_semaphore()
    for target in targets:
        pl.semaphore_signal(barrier, inc=1, device_id=(target,), device_id_type=MESH)
    pl.semaphore_wait(barrier, len(targets))


def group_member(x, z, t):
    return ident(x, z, 0, 0) + t


def dot(a, b):
    return jnp.dot(a, b, preferred_element_type=F32)


def dot_nt(a, b):
    return lax.dot_general(a, b, (((1,), (1,)), ((), ())), preferred_element_type=F32)


def dot_tn(a, b):
    return lax.dot_general(a, b, (((0,), (0,)), ((), ())), preferred_element_type=F32)


def turn(u, cosine, sine, low_lanes):
    moved = jnp.where(low_lanes, pltpu.roll(u, 120, 1), pltpu.roll(u, 8, 1))
    return u * cosine + moved * sine


def rotary_table():
    m = 8
    angle = np.arange(128, dtype=np.float64)[:, None] * (10000.0 ** (-2.0 * np.arange(m) / 16.0))[None, :]
    cosine = np.ones((128, 128), np.float32)
    sine = np.zeros((128, 128), np.float32)
    for head in (0, 64):
        cosine[:, head : head + m] = np.cos(angle)
        cosine[:, head + m : head + 2 * m] = np.cos(angle)
        sine[:, head : head + m] = -np.sin(angle)
        sine[:, head + m : head + 2 * m] = np.sin(angle)
    parts = []
    for table in (cosine, sine):
        high = table.astype(jnp.bfloat16)
        parts += [high, (table - high.astype(np.float32)).astype(jnp.bfloat16)]
    return np.concatenate(parts, 1)


def slabs(rows, step, fn):
    def one(i, carry):
        fn(pl.ds(pl.multiple_of(i * step, step), step))
        return carry

    lax.fori_loop(0, rows // step, one, 0)


class Half:
    def __init__(self, name, one, one_dev, two, two_dev, rows):
        self.name, self.one, self.one_dev, self.two, self.two_dev, self.rows = name, one, one_dev, two, two_dev, rows


def unpack_small(packed, t):
    packed = packed.astype(BF)

    def pick(lanes, columns, owner):
        j = lax.broadcasted_iota(jnp.int32, (128, lanes), 0)
        at = lax.broadcasted_iota(jnp.int32, (128, lanes), 1)
        of_row = ((j >> 3) & 3) * 32 + (j >> 5) * 8 + (j & 7)
        select = jnp.zeros((128, lanes), F32)
        for column in columns(at):
            select = select + (j == column).astype(F32)
        rows = dot(packed, select.astype(BF))
        return jnp.sum(jnp.where(of_row == owner(at), rows, 0.0), 0, keepdims=True)

    eight = lambda *starts: pick(1024, lambda at: [s + (at & 7) for s in starts], lambda at: at >> 3)
    ln = [eight(8 * v) for v in range(4)]
    b_out = eight(88, 96)
    qkv_at = lambda at: (at >> 7) * 1024 + t * 128 + (at & 127)
    d24 = lambda c: (c * 2731) >> 16
    b_qkv = pick(384, lambda at: [32 + qkv_at(at) - 24 * d24(qkv_at(at))], lambda at: d24(qkv_at(at)))
    b_fc1 = pick(512, lambda at: [56 + (at & 31)], lambda at: t * 16 + (at >> 5))
    return ln, b_qkv, b_fc1, b_out


def rows_pass(x, dy, seg, w1_ref, w2_ref, ln_ref, bias_ref, table_ref):
    x = x.astype(F32)
    centre = x - jnp.mean(x, 1, keepdims=True)
    spread = jnp.mean(centre * centre, 1, keepdims=True)
    normed = centre * lax.rsqrt(spread + NORM_EPS)
    g1, g2 = ln_ref[0:1, :], ln_ref[2:3, :]
    a1 = (normed * g1 + ln_ref[1:2, :]).astype(BF)
    a2 = (normed * g2 + ln_ref[3:4, :]).astype(BF)
    joined = dot(a1, w1_ref[:, 0:384]) + bias_ref[0:1, 0:384]
    hidden = dot(a2, w1_ref[:, 384:896]) + bias_ref[0:1, 384:896]
    phi_cdf = 0.5 + 0.5 * lax.erf(hidden * math.sqrt(0.5))
    active = hidden * phi_cdf
    slope = phi_cdf + hidden * (jnp.exp(hidden * hidden * -0.5) * (1.0 / math.sqrt(2.0 * math.pi)))

    row = lax.broadcasted_iota(jnp.int32, (128, 128), 0)
    col = lax.broadcasted_iota(jnp.int32, (128, 128), 1)
    masks, lives, tables = [], [], []
    for b in range(2):
        seg_c = jnp.broadcast_to(seg[b : b + 1, :].astype(F32), (128, 128))
        seg_r = seg_c.T
        allowed = (seg_c == seg_r) & (col <= row)
        position = jnp.sum(allowed.astype(F32), 1, keepdims=True) - 1.0
        onehot = (col == position.astype(jnp.int32)).astype(BF)
        tables.append(dot(onehot, table_ref[...]))
        masks.append(allowed)
        lives.append((seg_r[:, 0:1] >= 0.0).astype(F32))
    live = jnp.concatenate(lives, 0)
    d_cat = dot_nt(dy, w2_ref[...]) * live
    d_hidden = d_cat[:, 128:640] * slope
    d_context = d_cat[:, 0:128].astype(BF)
    active = (active.astype(BF).astype(F32) * live).astype(BF)

    lane = lax.broadcasted_iota(jnp.int32, (128, 128), 1)
    low_lanes = (lane & 63) < 8
    head0 = lane < 64

    def stacked(u):
        zero = jnp.zeros_like(u)
        return jnp.concatenate([jnp.where(head0, u, zero), jnp.where(head0, zero, u)], 0)

    contexts, d_joined = [], []
    for b in range(2):
        part = slice(b * 128, b * 128 + 128)
        cosine = tables[b][:, 0:128] + tables[b][:, 128:256]
        sine = tables[b][:, 256:384] + tables[b][:, 384:512]
        q = turn(joined[part, 0:128], cosine, sine, low_lanes).astype(BF)
        k = turn(joined[part, 128:256], cosine, sine, low_lanes).astype(BF)
        v = joined[part, 256:384].astype(BF)
        q2 = stacked(q)
        allowed = jnp.concatenate([masks[b], masks[b]], 0)
        scores = jnp.where(allowed, dot_nt(q2, k) * 0.125, MASKED)
        e = jnp.exp(scores - jnp.max(scores, 1, keepdims=True))
        probs = e / jnp.sum(e, 1, keepdims=True)
        probs_b = probs.astype(BF)
        ctx = dot(probs_b, v)
        ctx = jnp.where(head0, ctx[0:128], ctx[128:256]).astype(BF).astype(F32)
        contexts.append((ctx * lives[b]).astype(BF))
        dc2 = stacked(d_context[part])
        d_probs = dot_nt(dc2, v)
        d_v = dot_tn(probs_b, dc2)
        d_scores = probs * (d_probs - jnp.sum(probs * d_probs, 1, keepdims=True))
        d_scores = d_scores.astype(BF)
        dq2 = dot(d_scores, k) * 0.125
        d_q = jnp.where(head0, dq2[0:128], dq2[128:256])
        d_k = dot_tn(d_scores, q2) * 0.125
        d_joined.append(
            jnp.concatenate(
                [turn(d_q, cosine, -sine, low_lanes), turn(d_k, cosine, -sine, low_lanes), d_v], 1
            )
        )
    cat = jnp.concatenate([jnp.concatenate(contexts, 0), active], 1)
    out = dot(cat, w2_ref[...])
    d_all = jnp.concatenate([jnp.concatenate(d_joined, 0), d_hidden], 1)
    column_sums = jnp.sum(d_all, 0, keepdims=True), jnp.sum(dy.astype(F32) * live, 0, keepdims=True)
    d_all_b = d_all.astype(BF)
    g = g1 * dot_nt(d_all_b[:, 0:384], w1_ref[:, 0:384]) + g2 * dot_nt(d_all_b[:, 384:896], w1_ref[:, 384:896])
    return out, g, normed.astype(BF), d_all_b, cat, column_sums


SCRATCH = dict(
    X=((8, 256, 1024), BF),
    DY=((8, 256, 1024), BF),
    SEG=((8, 2, 128), jnp.int32),
    SM=((8, 8, 128), F32),
    AW=((8, 8, 896), BF),
    WA=((4, 4, 64, 896), BF),
    WB=((4, 4, 48, 1024), BF),
    w1=((1024, 896), BF),
    w2=((640, 1024), BF),
    ln=((8, 1024), F32),
    bias=((8, 896), F32),
    OUT=((8, 256, 1024), BF),
    G=((8, 256, 1024), BF),
    NB=((8, 256, 1024), BF),
    DALL=((8, 256, 896), BF),
    CAT=((8, 256, 640), BF),
    sums=((8, 1024), F32),
    sib=((2, 4, 256, 1024), BF),
    from_y=((2, 3, 256, 1024), BF),
    ga=((4, 4, 64, 896), BF),
    gb=((4, 4, 48, 1024), BF),
    one_a=((3, 4, 64, 896), BF),
    one_b=((3, 4, 48, 1024), BF),
    held_one_a=((4, 64, 896), BF),
    held_one_b=((4, 48, 1024), BF),
    two_a=((3, 64, 896), BF),
    two_b=((3, 48, 1024), BF),
    held_two_a=((4, 64, 896), BF),
    held_two_b=((4, 48, 1024), BF),
    last_a=((64, 896), BF),
    last_b=((48, 1024), BF),
    fin_a=((8, 8, 896), F32),
    vec=((8, 256), F32),
    vec_one=((3, 8, 256), F32),
    vec_sum=((8, 256), F32),
    vec_two=((3, 8, 256), F32),
)
MESSAGES = 7 * 6 + 2 * 7 + 2 * (3 + 12) + 13 + 2 * (4 + 3) + 2 * 6 + 7


def whole_kernel(x_ref, dy_ref, seg_ref, wqkv_ref, wfc1_ref, dense_ref, fc2_ref, small_ref, table_ref,
                 out_sum, g_sum, n_all, own_b, vec_all, b_out, *scratch):
    m = dict(zip(SCRATCH, scratch))
    send_sem, recv_sem = scratch[len(SCRATCH) :]
    X, DY, SEG, SM, AW, WA, WB = (m[k] for k in ("X", "DY", "SEG", "SM", "AW", "WA", "WB"))
    x, z, y, core = coords()
    t = y * 2 + core
    ring_y, ring_x, ring_z = Ring(y, core), Ring(x, core), Ring(z, core)
    y_dev = lambda to: ident(x, z, to, core)
    x_dev = lambda to: ident(to, z, y, core)
    z_dev = lambda to: ident(x, to, y, core)
    sibling = ident(x, z, y, 1 - core)
    others = [lax.rem(t + k, 8) for k in range(1, 8)]
    x_others = [lax.rem(x + k, 4) for k in range(1, 4)]
    z_others = [lax.rem(z + k, 4) for k in range(1, 4)]
    mine = lambda at: at * 2 + core
    hers = lambda at: at * 2 + 1 - core
    halves = (
        Half("a", ring_x, x_dev, ring_z, z_dev, 64),
        Half("b", ring_z, z_dev, ring_x, x_dev, 48),
    )
    enter([group_member(x, z, o) for o in others] + [x_dev(o) for o in x_others] + [z_dev(o) for o in z_others])
    msgs = Messages(send_sem, recv_sem)

    for k, o in enumerate(others):
        dev = group_member(x, z, o)
        for sec in range(3):
            lanes = pl.ds(pl.multiple_of(sec * 1024 + o * 128, 128), 128)
            msgs.send(("w", k, sec), wqkv_ref.at[:, lanes], AW.at[t, :, pl.ds(sec * 128, 128)], dev)
        lanes = pl.ds(pl.multiple_of(o * 512, 512), 512)
        msgs.send(("w", k, 3), wfc1_ref.at[:, lanes], AW.at[t, :, pl.ds(384, 512)], dev)
        msgs.send(("w", k, 4), small_ref, SM.at[t], dev)
    rows = (("x", x_ref, X), ("d", dy_ref, DY))

    def own_rows(name, src, dst):
        msgs.send((name, 0), src, dst.at[t], y_dev(ring_y.fwd))
        msgs.send((name, 1), src, dst.at[t], y_dev(ring_y.bwd))
        msgs.send((name, 2), src, dst.at[t], sibling)

    own_rows(*rows[0])
    for k, o in enumerate(others):
        msgs.send(("s", k), seg_ref, SEG.at[t], group_member(x, z, o))
    own_rows(*rows[1])
    for sec in range(3):
        lanes = pl.ds(pl.multiple_of(sec * 1024 + t * 128, 128), 128)
        AW[t, :, sec * 128 : sec * 128 + 128] = wqkv_ref[:, lanes]
    AW[t, :, 384:896] = wfc1_ref[:, pl.ds(pl.multiple_of(t * 512, 512), 512)]
    SM[t] = small_ref[...]
    X[t] = x_ref[...]
    DY[t] = dy_ref[...]
    SEG[t] = seg_ref[...]
    for k in range(7):
        for sec in range(5):
            msgs.land(("w", k, sec))
    for pair in range(4):
        both = jnp.concatenate([AW[2 * pair].astype(F32), AW[2 * pair + 1].astype(F32)], 0)
        WA[x, z, 16 * pair : 16 * pair + 16, :] = both.astype(BF)
    member = lax.broadcasted_iota(jnp.int32, (8, 128), 0)
    small = jnp.zeros((8, 128), F32)
    for k in range(8):
        small = jnp.where(member == k, SM[k], small)
    small = jnp.concatenate([small, jnp.zeros((8, 896), F32)], 1)
    WB[z, x, 0:16, :] = jnp.concatenate([dense_ref[...].astype(F32), small], 0).astype(BF)
    WB[z, x, 16:48, :] = fc2_ref[...]

    gathered = {"a": WA, "b": WB}

    def first(h, k, at, to):
        ref = gathered[h.name].at[at, h.two.own]
        msgs.send((h.name, "p", k), ref, ref, h.one_dev(to))

    def second(h, sub, k, at, frm, to):
        ref = gathered[h.name].at[at, frm]
        msgs.send((h.name, sub, k), ref, ref, h.two_dev(to))

    def spread(h, sub):
        at = getattr(h.one, sub)
        second(h, sub, 0, at, h.two.own, h.two.fwd)
        second(h, sub, 1, at, h.two.own, h.two.bwd)

    def pass_on(h, sub):
        msgs.land((h.name, sub, 0))
        second(h, sub, 2, getattr(h.one, sub), h.two.bwd, h.two.fwd)

    for h in halves:
        first(h, 0, h.one.own, h.one.fwd)
        first(h, 1, h.one.own, h.one.bwd)
        spread(h, "own")
    for h in halves:
        msgs.land((h.name, "p", 0))
        first(h, 2, h.one.bwd, h.one.fwd)
        spread(h, "bwd")
    for h in halves:
        msgs.land((h.name, "p", 1))
        spread(h, "fwd")
    for h in halves:
        msgs.land((h.name, "p", 2))
        spread(h, "opp")
    for h in halves:
        pass_on(h, "own")

    def rows_on(name, dst):
        msgs.land((name, 0))
        ref = dst.at[mine(ring_y.bwd)]
        msgs.send((name, 3), ref, ref, y_dev(ring_y.fwd))
        msgs.send((name, 4), ref, ref, sibling)
        msgs.land((name, 1))
        ref = dst.at[mine(ring_y.fwd)]
        msgs.send((name, 5), ref, ref, sibling)

    def rows_last(name, dst):
        msgs.land((name, 3))
        ref = dst.at[mine(ring_y.opp)]
        msgs.send((name, 6), ref, ref, sibling)

    rows_on("x", X)
    for sub in ("bwd", "fwd", "opp"):
        for h in halves:
            pass_on(h, sub)
    rows_on("d", DY)
    rows_last("x", X)
    for k in range(7):
        msgs.land(("s", k))
    for h in halves:
        for sub in ("own", "bwd", "fwd", "opp"):
            msgs.land((h.name, sub, 1))
            msgs.land((h.name, sub, 2))

    w1, w2, ln, bias = m["w1"], m["w2"], m["ln"], m["bias"]
    w1[...] = WA[...].reshape(1024, 896)
    mixed = WB[:, :, 0:16, :].astype(F32)
    w2[0:128, :] = mixed[:, :, 0:8, :].reshape(128, 1024).astype(BF)
    w2[128:640, :] = WB[:, :, 16:48, :].reshape(512, 1024)
    norms, b_qkv, b_fc1, b_both = unpack_small(mixed[:, :, 8:16, 0:128].reshape(128, 128), t)
    for v in range(4):
        ln[v : v + 1, :] = norms[v]
    bias[0:1, 0:384] = b_qkv
    bias[0:1, 384:896] = b_fc1
    b_out[...] = jnp.broadcast_to(b_both, (8, 1024))
    sums = m["sums"]
    sums[...] = jnp.zeros_like(sums)

    OUT, G, NB, DALL, CAT, sib, from_y = (m[k] for k in ("OUT", "G", "NB", "DALL", "CAT", "sib", "from_y"))
    arrays = ((0, OUT, out_sum), (1, G, g_sum))
    chips = [lax.rem(y + k, 4) for k in (3, 1, 2, 0)]

    def join(a, src, at, extra=None):
        def add(r):
            v = src[mine(at), r, :].astype(F32) + sib[a, at, r, :].astype(F32)
            if extra is not None:
                v = v + from_y[a, extra, r, :].astype(F32)
            src[mine(at), r, :] = v.astype(BF)

        slabs(256, 32, add)

    ref = DY.at[mine(ring_y.opp)]
    msgs.plan(("d", 6), ref, ref, sibling)
    for a, src, _ in arrays:
        for k in range(4):
            msgs.plan(("sib", a, k), src.at[hers(chips[k])], sib.at[a, chips[k]], sibling)
        msgs.plan(("y", a, 1), src.at[mine(ring_y.bwd)], from_y.at[a, 1], y_dev(ring_y.bwd))
        msgs.plan(("y", a, 0), src.at[mine(ring_y.opp)], from_y.at[a, 0], y_dev(ring_y.fwd))

    def before(s):
        @pl.when(s == 0)
        def _():
            for name in "xd":
                msgs.land((name, 4))
                msgs.land((name, 5))

        @pl.when(s == 4)
        def _():
            msgs.land(("d", 3))
            msgs.sent["d", 6].start()
            msgs.land(("x", 6))
            msgs.land(("d", 6))

        @pl.when(s == 6)
        def _():
            msgs.land(("x", 2))
            msgs.land(("d", 2))

    def after(s):
        for k in range(4):

            @pl.when(s == 2 * k)
            def _(k=k):
                for a, src, _ in arrays:
                    msgs.sent["sib", a, k].start()

        @pl.when(s == 3)
        def _():
            for a, src, _ in arrays:
                msgs.land(("sib", a, 0))
                msgs.land(("sib", a, 1))
                join(a, src, ring_y.bwd)
                msgs.sent["y", a, 1].start()

        @pl.when(s == 5)
        def _():
            for a, src, _ in arrays:
                msgs.land(("sib", a, 2))
                join(a, src, ring_y.opp)
                msgs.sent["y", a, 0].start()

    def one_slot(s, carry):
        before(s)
        k = s // 2
        chip = jnp.where(k == 0, chips[0], jnp.where(k == 1, chips[1], jnp.where(k == 2, chips[2], chips[3])))
        slot = chip * 2 + jnp.where(s % 2 == 0, 1 - core, core)
        out, g, normed, d_all, cat, column_sums = rows_pass(
            X[slot], DY[slot], SEG[slot], w1, w2, ln, bias, table_ref
        )
        OUT[slot] = out.astype(BF)
        G[slot] = g.astype(BF)
        NB[slot] = normed
        DALL[slot] = d_all
        CAT[slot] = cat
        sums[0:1, 0:896] += column_sums[0]
        sums[1:2, :] += column_sums[1]
        after(s)
        return carry

    lax.fori_loop(0, 8, one_slot, 0)

    vec, vec_one, vec_sum, vec_two = (m[k] for k in ("vec", "vec_one", "vec_sum", "vec_two"))
    for i in range(8):
        vec[i : i + 1, :] = sums[i // 4 : i // 4 + 1, (i % 4) * 256 : (i % 4) * 256 + 256]
    for k, o in enumerate(x_others):
        msgs.send(("v1", k), vec, vec_one.at[k], x_dev(o))

    part = {"a": m["ga"], "b": m["gb"]}
    into_one = {"a": m["one_a"], "b": m["one_b"]}
    held_one = {"a": m["held_one_a"], "b": m["held_one_b"]}
    into_two = {"a": m["two_a"], "b": m["two_b"]}
    held_two = {"a": m["held_two_a"], "b": m["held_two_b"]}
    last = {"a": m["last_a"], "b": m["last_b"]}
    ha, hb = halves

    def grad_a(at):
        lanes = pl.ds(pl.multiple_of(at * 256, 256), 256)
        v = dot_tn(NB[:, :, lanes].reshape(2048, 256), DALL[...].reshape(2048, 896))
        part["a"][at] = v.reshape(4, 64, 896).astype(BF)

    def grad_b(first_at, second_at):
        cols = [
            CAT[:, :, pl.ds(pl.multiple_of(128 + at * 128, 128), 128)].reshape(2048, 128)
            for at in (first_at, second_at)
        ]
        v = dot_tn(jnp.concatenate(cols, 1), DY[...].reshape(2048, 1024))
        part["b"][first_at, :, 16:48, :] = v[0:128].reshape(4, 32, 1024).astype(BF)
        part["b"][second_at, :, 16:48, :] = v[128:256].reshape(4, 32, 1024).astype(BF)

    def send_one(h, k, at, to):
        msgs.send((h.name, "one", k), part[h.name].at[at], into_one[h.name].at[k], h.one_dev(to))

    v = dot_tn(CAT[:, :, 0:128].reshape(2048, 128), DY[...].reshape(2048, 1024)).reshape(4, 4, 8, 1024)
    part["b"][:, :, 0:16, :] = jnp.concatenate([v, jnp.zeros_like(v)], 2).astype(BF)
    grad_a(ring_x.opp)
    send_one(ha, 0, ring_x.opp, ring_x.fwd)
    grad_b(ring_z.opp, ring_z.bwd)
    send_one(hb, 0, ring_z.opp, ring_z.fwd)
    send_one(hb, 1, ring_z.bwd, ring_z.bwd)

    for a, src, _ in arrays:
        msgs.land(("y", a, 0))
        join(a, src, ring_y.fwd, extra=0)
        msgs.send(("y", a, 2), src.at[mine(ring_y.fwd)], from_y.at[a, 2], y_dev(ring_y.fwd))

    grad_a(ring_x.bwd)
    send_one(ha, 1, ring_x.bwd, ring_x.bwd)
    grad_a(ring_x.fwd)
    grad_b(ring_z.fwd, ring_z.own)

    for k in range(3):
        msgs.land(("v1", k))
    vec_sum[...] = vec[...] + vec_one[0] + vec_one[1] + vec_one[2]
    for k, o in enumerate(z_others):
        msgs.send(("v2", k), vec_sum, vec_two.at[k], z_dev(o))

    def slab_of(h):
        return h.rows // (4 if h.name == "a" else 3)

    def first_forward(h):
        msgs.land((h.name, "one", 0))

        def add(r):
            v = part[h.name][h.one.fwd, :, r, :].astype(F32) + into_one[h.name][0, :, r, :].astype(F32)
            held_one[h.name][:, r, :] = v.astype(BF)

        slabs(h.rows, slab_of(h), add)
        msgs.send((h.name, "one", 2), held_one[h.name], into_one[h.name].at[2], h.one_dev(h.one.fwd))

    for h in halves:
        first_forward(h)
    grad_a(ring_x.own)

    def first_total(h):
        msgs.land((h.name, "one", 1))
        msgs.land((h.name, "one", 2))

        def add(r):
            v = part[h.name][h.one.own, :, r, :].astype(F32) + into_one[h.name][1, :, r, :].astype(F32)
            held_two[h.name][:, r, :] = (v + into_one[h.name][2, :, r, :].astype(F32)).astype(BF)

        slabs(h.rows, slab_of(h), add)
        held = held_two[h.name]
        msgs.send((h.name, "two", 0), held.at[h.two.opp], into_two[h.name].at[0], h.two_dev(h.two.fwd))
        msgs.send((h.name, "two", 1), held.at[h.two.bwd], into_two[h.name].at[1], h.two_dev(h.two.bwd))

    for h in halves:
        first_total(h)

    for k in range(3):
        msgs.land(("v2", k))
    vec_all[t] = vec_sum[...] + vec_two[0] + vec_two[1] + vec_two[2]
    for k, o in enumerate(others):
        msgs.send(("v3", k), vec_all.at[t], vec_all.at[t], group_member(x, z, o))

    for h in halves:
        msgs.land((h.name, "two", 0))
        v = held_two[h.name][h.two.fwd].astype(F32) + into_two[h.name][0].astype(F32)
        last[h.name][...] = v.astype(BF)
        msgs.send((h.name, "two", 2), last[h.name], into_two[h.name].at[2], h.two_dev(h.two.fwd))

    for a, src, dst in arrays:
        msgs.land(("sib", a, 3))
        msgs.land(("y", a, 1))
        msgs.land(("y", a, 2))

        def add(r, a=a, src=src, dst=dst):
            v = src[mine(y), r, :].astype(F32) + sib[a, y, r, :].astype(F32)
            dst[r, :] = v + from_y[a, 1, r, :].astype(F32) + from_y[a, 2, r, :].astype(F32)

        slabs(256, 32, add)

    def second_total(h):
        msgs.land((h.name, "two", 1))
        msgs.land((h.name, "two", 2))
        two = into_two[h.name]
        return held_two[h.name][h.two.own].astype(F32) + two[1].astype(F32) + two[2].astype(F32)

    fin_a = m["fin_a"]
    fin_a[...] = second_total(ha).reshape(8, 8, 896)
    for k, o in enumerate(others):
        msgs.send(("n", k), fin_a.at[o], n_all.at[t], group_member(x, z, o))
    n_all[t] = fin_a[t]
    v = second_total(hb)
    own_b[0:8, :] = v[0:8]
    own_b[8:40, :] = v[16:48]
    msgs.finish()


def whole(*args):
    vmem = pl.BlockSpec(memory_space=pltpu.VMEM)
    return pl.pallas_call(
        whole_kernel,
        out_shape=(
            jax.ShapeDtypeStruct((256, 1024), F32),
            jax.ShapeDtypeStruct((256, 1024), F32),
            jax.ShapeDtypeStruct((8, 8, 896), F32),
            jax.ShapeDtypeStruct((40, 1024), F32),
            jax.ShapeDtypeStruct((8, 8, 256), F32),
            jax.ShapeDtypeStruct((8, 1024), F32),
        ),
        in_specs=[vmem] * len(args),
        out_specs=(vmem,) * 6,
        scratch_shapes=[pltpu.VMEM(*spec) for spec in SCRATCH.values()]
        + [pltpu.SemaphoreType.DMA((MESSAGES,)), pltpu.SemaphoreType.DMA((MESSAGES,))],
        compiler_params=pltpu.CompilerParams(
            collective_id=0, has_side_effects=True, vmem_limit_bytes=VMEM_LIMIT
        ),
        cost_estimate=pl.CostEstimate(flops=20_000_000_000, bytes_accessed=5_000_000, transcendentals=3_000_000),
        name="whole_block",
    )(*args)


def spread_owner(d):
    t, q = d // 16, d % 16
    return (q % 4) * 32 + (q // 4) * 8 + t


def body(tokens, segments, grad_out, ln1_gain, ln1_bias, ln2_gain, ln2_bias, w_qkv, b_qkv,
         w_dense, b_dense, w_fc1, b_fc1, w_fc2, b_fc2):
    me = lax.axis_index("fsdp")

    there = [(d, spread_owner(d)) for d in range(128)]
    back = [(b, a) for a, b in there]
    moved = lax.ppermute(jnp.concatenate([w_dense, w_fc2], 0), "fsdp", there)
    small = jnp.concatenate(
        [ln1_gain, ln1_bias, ln2_gain, ln2_bias, b_qkv, b_fc1, b_dense, b_fc2, jnp.zeros((24,), BF)]
    )
    small = jnp.broadcast_to(small.astype(F32), (8, 128))
    out_sum, g_sum, n_all, own_b, sums, b_out = whole(
        tokens, grad_out, segments, w_qkv, w_fc1, moved[0:8], moved[8:40], small, jnp.asarray(rotary_table())
    )
    grad_b = lax.ppermute(own_b, "fsdp", back)

    live = (segments.reshape(256, 1) >= 0).astype(F32)
    x = tokens.astype(F32)
    out = (x + live * (out_sum + b_out[0:1, :])).astype(BF)
    centre = x - jnp.mean(x, -1, keepdims=True)
    scale = lax.rsqrt(jnp.mean(centre * centre, -1, keepdims=True) + NORM_EPS)
    normed = centre * scale
    dx = (g_sum - jnp.mean(g_sum, -1, keepdims=True) - normed * jnp.mean(g_sum * normed, -1, keepdims=True)) * scale
    grad_tokens = (grad_out.astype(F32) + dx).astype(BF)

    sums = sums.reshape(8, 2, 1024)
    sum_qkv = sums[:, 0, 0:384].reshape(8, 3, 128).transpose(1, 0, 2).reshape(3072)
    sum_fc1 = sums[:, 0, 384:896].reshape(4096)
    n_qkv = n_all[:, :, 0:384].reshape(8, 8, 3, 128).transpose(1, 2, 0, 3).reshape(8, 3072)
    n_fc1 = n_all[:, :, 384:896].transpose(1, 0, 2).reshape(8, 4096)

    def norm_grads(weight, n, s, gain, bias_of):
        weight = weight.astype(F32)
        grad_w = gain.astype(F32)[:, None] * n + bias_of.astype(F32)[:, None] * s
        return jnp.sum(weight * n, 1), jnp.sum(weight * s, 1), grad_w

    g1_gain, g1_bias, grad_qkv = norm_grads(w_qkv, n_qkv, sum_qkv, ln1_gain, ln1_bias)
    g2_gain, g2_bias, grad_fc1 = norm_grads(w_fc1, n_fc1, sum_fc1, ln2_gain, ln2_bias)
    grad_b_qkv = lax.dynamic_slice(sum_qkv, (me * 24,), (24,))
    grad_b_fc1 = lax.dynamic_slice(sum_fc1, (me * 32,), (32,))
    grad_b_out = lax.dynamic_slice(sums[0, 1], (me * 8,), (8,))
    return (out, grad_tokens, g1_gain, g1_bias, g2_gain, g2_bias, grad_qkv, grad_b_qkv,
            grad_b[0:8], grad_b_out, grad_fc1, grad_b_fc1, grad_b[8:40], grad_b_out)


def solution(mesh):
    rows, flat = P("fsdp", None), P("fsdp")
    return jax.shard_map(
        body,
        mesh=mesh,
        in_specs=(rows, rows, rows, flat, flat, flat, flat, rows, flat, rows, flat, rows, flat, rows, flat),
        out_specs=(rows, rows, flat, flat, flat, flat, rows, flat, rows, flat, rows, flat, rows, flat),
        check_vma=False,
    )
```

```python
import functools
import math

import jax
import jax.numpy as jnp
import numpy as np
from jax import lax
from jax.experimental import pallas as pl
from jax.experimental.pallas import tpu as pltpu
from jax.sharding import PartitionSpec as P

NORM_EPS = 1e-05
MASKED = -1e30
MESH = pl.DeviceIdType.MESH
BF = jnp.bfloat16
F32 = jnp.float32
VMEM_LIMIT = 60 * 1024 * 1024


def coords():
    i = lax.axis_index("fsdp")
    core = lax.rem(i, 2)
    y = lax.rem(i // 2, 4)
    z = lax.rem(i // 8, 4)
    x = i // 32
    return x, z, y, core


def ident(x, z, y, core):
    return ((x * 4 + z) * 4 + y) * 2 + core


class Ring:
    def __init__(self, at, core):
        step = 1 + 2 * core
        self.own = at
        self.fwd = lax.rem(at + step, 4)
        self.bwd = lax.rem(at + 4 - step, 4)
        self.opp = lax.rem(at + 2, 4)


class Messages:
    def __init__(self, send_sem, recv_sem):
        self.send_sem, self.recv_sem = send_sem, recv_sem
        self.sent, self.landed, self.apart = {}, set(), set()

    def plan(self, name, src, dst, target, apart=False):
        n = len(self.sent)
        copy = pltpu.make_async_remote_copy(
            src_ref=src,
            dst_ref=dst,
            send_sem=self.send_sem.at[n],
            recv_sem=self.recv_sem.at[n],
            device_id=(target,),
            device_id_type=MESH,
        )
        self.sent[name] = copy
        if apart:
            self.apart.add(name)

    def send(self, name, src, dst, target):
        self.plan(name, src, dst, target)
        self.sent[name].start()

    def land(self, name):
        assert name not in self.landed
        self.landed.add(name)
        self.sent[name].wait_recv()

    def finish(self):
        for name, copy in self.sent.items():
            if name not in self.landed and name not in self.apart:
                copy.wait_recv()
        for name, copy in self.sent.items():
            if name not in self.apart:
                copy.wait_send()


def group_member(x, z, t):
    return ident(x, z, 0, 0) + t


def dot(a, b):
    return jnp.dot(a, b, preferred_element_type=F32)


def dot_nt(a, b):
    return lax.dot_general(a, b, (((1,), (1,)), ((), ())), preferred_element_type=F32)


def dot_tn(a, b):
    return lax.dot_general(a, b, (((0,), (0,)), ((), ())), preferred_element_type=F32)


def turn(u, cosine, sine, low_lanes):
    moved = jnp.where(low_lanes, pltpu.roll(u, 120, 1), pltpu.roll(u, 8, 1))
    return u * cosine + moved * sine


def rotary_table():
    m = 8
    angle = np.arange(128, dtype=np.float64)[:, None] * (10000.0 ** (-2.0 * np.arange(m) / 16.0))[None, :]
    cosine = np.ones((128, 128), np.float32)
    sine = np.zeros((128, 128), np.float32)
    for head in (0, 64):
        cosine[:, head : head + m] = np.cos(angle)
        cosine[:, head + m : head + 2 * m] = np.cos(angle)
        sine[:, head : head + m] = -np.sin(angle)
        sine[:, head + m : head + 2 * m] = np.sin(angle)
    parts = []
    for table in (cosine, sine):
        high = table.astype(jnp.bfloat16)
        parts += [high, (table - high.astype(np.float32)).astype(jnp.bfloat16)]
    return np.concatenate(parts, 1)


def slabs(rows, step, fn):
    def one(i, carry):
        fn(pl.ds(pl.multiple_of(i * step, step), step))
        return carry

    lax.fori_loop(0, rows // step, one, 0)


class Half:
    def __init__(self, name, one, one_dev, two, two_dev, rows):
        self.name, self.one, self.one_dev, self.two, self.two_dev, self.rows = name, one, one_dev, two, two_dev, rows


def unpack_small(packed, t):
    packed = packed.astype(BF)

    def pick(lanes, columns, owner):
        j = lax.broadcasted_iota(jnp.int32, (128, lanes), 0)
        at = lax.broadcasted_iota(jnp.int32, (128, lanes), 1)
        of_row = ((j >> 3) & 3) * 32 + (j >> 5) * 8 + (j & 7)
        select = jnp.zeros((128, lanes), F32)
        for column in columns(at):
            select = select + (j == column).astype(F32)
        rows = dot(packed, select.astype(BF))
        return jnp.sum(jnp.where(of_row == owner(at), rows, 0.0), 0, keepdims=True)

    eight = lambda *starts: pick(1024, lambda at: [s + (at & 7) for s in starts], lambda at: at >> 3)
    ln = [eight(8 * v) for v in range(4)]
    b_out = eight(88, 96)
    qkv_at = lambda at: (at >> 7) * 1024 + t * 128 + (at & 127)
    d24 = lambda c: (c * 2731) >> 16
    b_qkv = pick(384, lambda at: [32 + qkv_at(at) - 24 * d24(qkv_at(at))], lambda at: d24(qkv_at(at)))
    b_fc1 = pick(512, lambda at: [56 + (at & 31)], lambda at: ((at >> 5) & 3) * 32 + (at >> 7) * 8 + t)
    return ln, b_qkv, b_fc1, b_out


def rows_pass(x, dy, seg, w1_ref, w2_ref, ln_ref, bias_ref, table_ref):
    x = x.astype(F32)
    centre = x - jnp.mean(x, 1, keepdims=True)
    spread = jnp.mean(centre * centre, 1, keepdims=True)
    normed = centre * lax.rsqrt(spread + NORM_EPS)
    g1, g2 = ln_ref[0:1, :], ln_ref[2:3, :]
    a1 = (normed * g1 + ln_ref[1:2, :]).astype(BF)
    a2 = (normed * g2 + ln_ref[3:4, :]).astype(BF)
    joined = dot(a1, w1_ref[:, 0:384]) + bias_ref[0:1, 0:384]
    hidden = dot(a2, w1_ref[:, 384:896]) + bias_ref[0:1, 384:896]
    phi_cdf = 0.5 + 0.5 * lax.erf(hidden * math.sqrt(0.5))
    active = hidden * phi_cdf
    slope = phi_cdf + hidden * (jnp.exp(hidden * hidden * -0.5) * (1.0 / math.sqrt(2.0 * math.pi)))

    row = lax.broadcasted_iota(jnp.int32, (128, 128), 0)
    col = lax.broadcasted_iota(jnp.int32, (128, 128), 1)
    masks, lives, tables = [], [], []
    for b in range(2):
        seg_c = jnp.broadcast_to(seg[b : b + 1, :], (128, 128))
        seg_r = seg_c.T
        allowed = (seg_c == seg_r) & (col <= row)
        position = jnp.sum(allowed.astype(F32), 1, keepdims=True) - 1.0
        onehot = (col == position.astype(jnp.int32)).astype(BF)
        tables.append(dot(onehot, table_ref[...]))
        masks.append(allowed)
        lives.append((seg_r[:, 0:1] >= 0.0).astype(F32))
    live = jnp.concatenate(lives, 0)
    d_cat = dot_nt(dy, w2_ref[...]) * live
    d_hidden = d_cat[:, 128:640] * slope
    d_context = d_cat[:, 0:128].astype(BF)
    active = (active.astype(BF).astype(F32) * live).astype(BF)

    lane = lax.broadcasted_iota(jnp.int32, (128, 128), 1)
    low_lanes = (lane & 63) < 8
    head0 = lane < 64

    def stacked(u):
        zero = jnp.zeros_like(u)
        return jnp.concatenate([jnp.where(head0, u, zero), jnp.where(head0, zero, u)], 0)

    ones = jnp.ones((128, 128), BF)
    contexts, d_joined = [], []
    for b in range(2):
        part = slice(b * 128, b * 128 + 128)
        cosine = tables[b][:, 0:128] + tables[b][:, 128:256]
        sine = tables[b][:, 256:384] + tables[b][:, 384:512]
        q = turn(joined[part, 0:128], cosine, sine, low_lanes).astype(BF)
        k = turn(joined[part, 128:256], cosine, sine, low_lanes).astype(BF)
        v = joined[part, 256:384].astype(BF)
        q2 = stacked(q)
        allowed = jnp.concatenate([masks[b], masks[b]], 0)
        scores = jnp.where(allowed, dot_nt(q2, k) * 0.125, MASKED)
        e = jnp.exp(scores - jnp.max(scores, 1, keepdims=True))
        ctx = dot(e.astype(BF), jnp.concatenate([v, ones], 1))
        inverse = 1.0 / ctx[:, 128:256]
        probs = e * inverse
        probs_b = probs.astype(BF)
        ctx = ctx[:, 0:128] * inverse
        ctx = jnp.where(head0, ctx[0:128], ctx[128:256]).astype(BF).astype(F32)
        contexts.append((ctx * lives[b]).astype(BF))
        dc2 = stacked(d_context[part])
        d_probs = dot_nt(dc2, v)
        d_v = dot_tn(probs_b, dc2)
        d_scores = probs * (d_probs - jnp.sum(probs * d_probs, 1, keepdims=True))
        d_scores = d_scores.astype(BF)
        dq2 = dot(d_scores, k) * 0.125
        d_q = jnp.where(head0, dq2[0:128], dq2[128:256])
        d_k = dot_tn(d_scores, q2) * 0.125
        d_joined.append(
            jnp.concatenate(
                [turn(d_q, cosine, -sine, low_lanes), turn(d_k, cosine, -sine, low_lanes), d_v], 1
            )
        )
    cat = jnp.concatenate([jnp.concatenate(contexts, 0), active], 1)
    out = dot(cat, w2_ref[...])
    d_all = jnp.concatenate([jnp.concatenate(d_joined, 0), d_hidden], 1)
    column_sums = jnp.sum(d_all, 0, keepdims=True), jnp.sum(dy.astype(F32) * live, 0, keepdims=True)
    d_all_b = d_all.astype(BF)
    g = g1 * dot_nt(d_all_b[:, 0:384], w1_ref[:, 0:384]) + g2 * dot_nt(d_all_b[:, 384:896], w1_ref[:, 384:896])
    return out, g, normed.astype(BF), d_all_b, cat, column_sums


SCRATCH = dict(
    X=((8, 256, 1024), BF),
    DY=((8, 256, 1024), BF),
    qkv=((8, 3072), BF),
    fc1=((8, 4096), BF),
    small=((8, 128), BF),
    table=((128, 512), BF),
    dense=((8, 1024), BF),
    fc2=((32, 1024), BF),
    stage=((8, 8, 1024), BF),
    AW=((8, 8, 1024), BF),
    WA=((4, 4, 64, 896), BF),
    WB=((4, 4, 48, 1024), BF),
    w1=((1024, 896), BF),
    w2=((640, 1024), BF),
    ln=((8, 1024), F32),
    bias=((8, 896), F32),
    OUT=((8, 256, 1024), BF),
    G=((8, 256, 1024), BF),
    NB=((8, 256, 1024), BF),
    DALL=((8, 256, 896), BF),
    CAT=((8, 256, 640), BF),
    sums=((8, 1024), F32),
    sib=((2, 4, 256, 1024), BF),
    from_y=((2, 3, 256, 1024), BF),
    ga=((4, 4, 64, 896), BF),
    gb=((4, 4, 48, 1024), BF),
    one_a=((3, 4, 64, 896), BF),
    one_b=((3, 4, 48, 1024), BF),
    held_one_a=((4, 64, 896), BF),
    held_one_b=((4, 48, 1024), BF),
    two_a=((3, 64, 896), BF),
    two_b=((3, 48, 1024), BF),
    held_two_a=((3, 64, 896), BF),
    held_two_b=((3, 48, 1024), BF),
    fin_a=((8, 8, 896), F32),
    own_dense=((8, 1024), F32),
    vec=((8, 256), F32),
    vec_one=((3, 8, 256), F32),
    vec_sum=((8, 256), F32),
    vec_two=((3, 8, 256), F32),
)
MESSAGES = 7 + 1 + 2 * 7 + 2 * (3 + 12) + 13 + 2 * (4 + 3) + 2 * (12 + 3) + 7 + 1


def whole_kernel(x_ref, dy_ref, wqkv_ref, wfc1_ref, dense_ref, fc2_ref, small_ref, table_hbm,
                 out_sum, g_sum, n_all, grad_dense, grad_fc2, vec_all, b_out, *scratch):
    m = dict(zip(SCRATCH, scratch))
    send_sem, recv_sem, local_sem = scratch[len(SCRATCH) :]
    X, DY, AW, WA, WB, stage, table_ref = (m[k] for k in ("X", "DY", "AW", "WA", "WB", "stage", "table"))
    x, z, y, core = coords()
    t = y * 2 + core
    ring_y, ring_x, ring_z = Ring(y, core), Ring(x, core), Ring(z, core)
    y_dev = lambda to: ident(x, z, to, core)
    x_dev = lambda to: ident(to, z, y, core)
    z_dev = lambda to: ident(x, to, y, core)
    sibling = ident(x, z, y, 1 - core)
    others = [lax.rem(t + k, 8) for k in range(1, 8)]
    x_others = [lax.rem(x + k, 4) for k in range(1, 4)]
    z_others = [lax.rem(z + k, 4) for k in range(1, 4)]
    mine = lambda at: at * 2 + core
    hers = lambda at: at * 2 + 1 - core
    halves = (
        Half("a", ring_x, x_dev, ring_z, z_dev, 64),
        Half("b", ring_z, z_dev, ring_x, x_dev, 48),
    )
    owner = t * 16 + z * 4 + x
    me = ident(x, z, y, core)
    spreader = ident(lax.rem(me, 4), lax.rem(me // 4, 4), 0, 0) + me // 16
    moves = spreader != me

    local = [
        pltpu.make_async_copy(src, dst, local_sem.at[n])
        for n, (src, dst) in enumerate(
            (
                (wqkv_ref, m["qkv"]),
                (wfc1_ref, m["fc1"]),
                (small_ref, m["small"]),
                (fc2_ref, m["fc2"]),
                (table_hbm, table_ref),
                (x_ref, X.at[t]),
                (dy_ref, DY.at[t]),
            )
        )
    ]
    for copy in local:
        copy.start()
    barrier = pltpu.get_barrier_semaphore()
    near = [group_member(x, z, o) for o in others] + [x_dev(o) for o in x_others] + [z_dev(o) for o in z_others]
    for target in near:
        pl.semaphore_signal(barrier, inc=1, device_id=(target,), device_id_type=MESH)

    @pl.when(moves)
    def _():
        for target in (owner, spreader):
            pl.semaphore_signal(barrier, inc=1, device_id=(target,), device_id_type=MESH)

    for copy in local[:4]:
        copy.wait()
    fc1_rows = m["fc1"][...].astype(F32)
    for o in range(8):
        for sec in range(3):
            stage[o, :, sec * 128 : sec * 128 + 128] = m["qkv"][:, sec * 1024 + o * 128 : sec * 1024 + o * 128 + 128]
        columns = [fc1_rows[:, at : at + 32] for at in [p * 1024 + q * 256 + o * 32 for q in range(4) for p in range(4)]]
        stage[o, :, 384:896] = jnp.concatenate(columns, 1).astype(BF)
        stage[o, :, 896:1024] = m["small"][...]

    @pl.when(moves)
    def _():
        pl.semaphore_wait(barrier, len(near) + 2)

    @pl.when(jnp.logical_not(moves))
    def _():
        pl.semaphore_wait(barrier, len(near))

    msgs = Messages(send_sem, recv_sem)

    for k, o in enumerate(others):
        msgs.send(("w", k), stage.at[o], AW.at[t], group_member(x, z, o))
    lone = pltpu.make_async_copy(dense_ref, m["dense"], local_sem.at[7])
    msgs.plan("there", dense_ref, m["dense"], spreader, apart=True)
    msgs.plan("back", m["own_dense"], grad_dense, owner, apart=True)

    @pl.when(moves)
    def _():
        msgs.sent["there"].start()

    @pl.when(jnp.logical_not(moves))
    def _():
        lone.start()

    def own_rows(name, src, dst):
        msgs.send((name, 0), src, dst.at[t], y_dev(ring_y.fwd))
        msgs.send((name, 1), src, dst.at[t], y_dev(ring_y.bwd))
        msgs.send((name, 2), src, dst.at[t], sibling)

    own_rows("x", x_ref, X)
    own_rows("d", dy_ref, DY)
    AW[t] = stage[t]
    for k in range(7):
        msgs.land(("w", k))
    for pair in range(4):
        both = jnp.concatenate([AW[2 * pair].astype(F32), AW[2 * pair + 1].astype(F32)], 0)
        WA[x, z, 16 * pair : 16 * pair + 16, :] = both[:, 0:896].astype(BF)

    @pl.when(moves)
    def _():
        msgs.sent["there"].wait_recv()

    @pl.when(jnp.logical_not(moves))
    def _():
        lone.wait()

    member = lax.broadcasted_iota(jnp.int32, (8, 128), 0)
    small = jnp.zeros((8, 128), F32)
    for k in range(8):
        small = jnp.where(member == k, AW[k, :, 896:1024].astype(F32)[0:1], small)
    small = jnp.concatenate([small, jnp.zeros((8, 896), F32)], 1)
    WB[z, x, 0:16, :] = jnp.concatenate([m["dense"][...].astype(F32), small], 0).astype(BF)
    WB[z, x, 16:48, :] = m["fc2"][...]

    gathered = {"a": WA, "b": WB}

    def first(h, k, at, to):
        ref = gathered[h.name].at[at, h.two.own]
        msgs.send((h.name, "p", k), ref, ref, h.one_dev(to))

    def second(h, sub, k, at, frm, to):
        ref = gathered[h.name].at[at, frm]
        msgs.send((h.name, sub, k), ref, ref, h.two_dev(to))

    def spread(h, sub):
        at = getattr(h.one, sub)
        second(h, sub, 0, at, h.two.own, h.two.fwd)
        second(h, sub, 1, at, h.two.own, h.two.bwd)

    def pass_on(h, sub):
        msgs.land((h.name, sub, 0))
        second(h, sub, 2, getattr(h.one, sub), h.two.bwd, h.two.fwd)

    for h in halves:
        first(h, 0, h.one.own, h.one.fwd)
        first(h, 1, h.one.own, h.one.bwd)
        spread(h, "own")
    for h in halves:
        msgs.land((h.name, "p", 0))
        first(h, 2, h.one.bwd, h.one.fwd)
        spread(h, "bwd")
    for h in halves:
        msgs.land((h.name, "p", 1))
        spread(h, "fwd")
    for h in halves:
        msgs.land((h.name, "p", 2))
        spread(h, "opp")
    for h in halves:
        pass_on(h, "own")

    def rows_on(name, dst):
        msgs.land((name, 0))
        ref = dst.at[mine(ring_y.bwd)]
        msgs.send((name, 4), ref, ref, sibling)
        msgs.land((name, 1))
        ref = dst.at[mine(ring_y.fwd)]
        msgs.send((name, 5), ref, ref, sibling)

    def rows_far(name, dst):
        ref = dst.at[mine(ring_y.bwd)]
        msgs.send((name, 3), ref, ref, y_dev(ring_y.fwd))

    rows_on("x", X)
    for sub in ("bwd", "fwd", "opp"):
        for h in halves:
            pass_on(h, sub)
    rows_on("d", DY)
    rows_far("x", X)
    rows_far("d", DY)
    for h in halves:
        for sub in ("own", "bwd", "fwd", "opp"):
            msgs.land((h.name, sub, 1))
            msgs.land((h.name, sub, 2))
    for copy in local[4:]:
        copy.wait()

    w1, w2, ln, bias = m["w1"], m["w2"], m["ln"], m["bias"]
    w1[...] = WA[...].reshape(1024, 896)
    mixed = WB[:, :, 0:16, :].astype(F32)
    w2[0:128, :] = mixed[:, :, 0:8, :].reshape(128, 1024).astype(BF)
    w2[128:640, :] = WB[:, :, 16:48, :].reshape(512, 1024)
    norms, b_qkv, b_fc1, b_both = unpack_small(mixed[:, :, 8:16, 0:128].reshape(128, 128), t)
    for v in range(4):
        ln[v : v + 1, :] = norms[v]
    bias[0:1, 0:384] = b_qkv
    bias[0:1, 384:896] = b_fc1
    b_out[...] = jnp.broadcast_to(b_both, (8, 1024))
    sums = m["sums"]
    sums[...] = jnp.zeros_like(sums)

    OUT, G, NB, DALL, CAT, sib, from_y = (m[k] for k in ("OUT", "G", "NB", "DALL", "CAT", "sib", "from_y"))
    arrays = ((0, OUT, out_sum), (1, G, g_sum))
    chips = [lax.rem(y + k, 4) for k in (3, 1, 2, 0)]

    def join(a, src, at, extra=None):
        def add(r):
            v = src[mine(at), r, :].astype(F32) + sib[a, at, r, :].astype(F32)
            if extra is not None:
                v = v + from_y[a, extra, r, :].astype(F32)
            src[mine(at), r, :] = v.astype(BF)

        slabs(256, 32, add)

    for name, dst in (("x", X), ("d", DY)):
        ref = dst.at[mine(ring_y.opp)]
        msgs.plan((name, 6), ref, ref, sibling)
    for a, src, _ in arrays:
        for k in range(4):
            msgs.plan(("sib", a, k), src.at[hers(chips[k])], sib.at[a, chips[k]], sibling)
        msgs.plan(("y", a, 1), src.at[mine(ring_y.bwd)], from_y.at[a, 1], y_dev(ring_y.bwd))
        msgs.plan(("y", a, 0), src.at[mine(ring_y.opp)], from_y.at[a, 0], y_dev(ring_y.fwd))

    def before(s):
        @pl.when(s == 0)
        def _():
            for name in "xd":
                msgs.land((name, 4))
                msgs.land((name, 5))

        @pl.when(s == 2)
        def _():
            for name in "xd":
                msgs.land((name, 3))
                msgs.sent[name, 6].start()

        @pl.when(s == 4)
        def _():
            msgs.land(("x", 6))
            msgs.land(("d", 6))

        @pl.when(s == 6)
        def _():
            msgs.land(("x", 2))
            msgs.land(("d", 2))

    def after(s):
        for k in range(4):

            @pl.when(s == 2 * k)
            def _(k=k):
                for a, src, _ in arrays:
                    msgs.sent["sib", a, k].start()

        @pl.when(s == 3)
        def _():
            for a, src, _ in arrays:
                msgs.land(("sib", a, 0))
                msgs.land(("sib", a, 1))
                join(a, src, ring_y.bwd)
                msgs.sent["y", a, 1].start()

        @pl.when(s == 5)
        def _():
            for a, src, _ in arrays:
                msgs.land(("sib", a, 2))
                join(a, src, ring_y.opp)
                msgs.sent["y", a, 0].start()

    def one_slot(s, carry):
        before(s)
        k = s // 2
        chip = jnp.where(k == 0, chips[0], jnp.where(k == 1, chips[1], jnp.where(k == 2, chips[2], chips[3])))
        slot = chip * 2 + jnp.where(s % 2 == 0, 1 - core, core)
        out, g, normed, d_all, cat, column_sums = rows_pass(
            X[slot], DY[slot], AW[slot][:, 896:1024].astype(F32)[1:3], w1, w2, ln, bias, table_ref
        )
        OUT[slot] = out.astype(BF)
        G[slot] = g.astype(BF)
        NB[slot] = normed
        DALL[slot] = d_all
        CAT[slot] = cat
        sums[0:1, 0:896] += column_sums[0]
        sums[1:2, :] += column_sums[1]
        after(s)
        return carry

    lax.fori_loop(0, 8, one_slot, 0)

    vec, vec_one, vec_sum, vec_two = (m[k] for k in ("vec", "vec_one", "vec_sum", "vec_two"))
    for i in range(8):
        vec[i : i + 1, :] = sums[i // 4 : i // 4 + 1, (i % 4) * 256 : (i % 4) * 256 + 256]
    for k, o in enumerate(x_others):
        msgs.send(("v1", k), vec, vec_one.at[k], x_dev(o))

    part = {"a": m["ga"], "b": m["gb"]}
    into_one = {"a": m["one_a"], "b": m["one_b"]}
    held_one = {"a": m["held_one_a"], "b": m["held_one_b"]}
    into_two = {"a": m["two_a"], "b": m["two_b"]}
    held_two = {"a": m["held_two_a"], "b": m["held_two_b"]}
    ha, hb = halves

    def grad_a(at):
        lanes = pl.ds(pl.multiple_of(at * 256, 256), 256)
        v = dot_tn(NB[:, :, lanes].reshape(2048, 256), DALL[...].reshape(2048, 896))
        part["a"][at] = v.reshape(4, 64, 896).astype(BF)

    def grad_b(first_at, second_at):
        cols = [
            CAT[:, :, pl.ds(pl.multiple_of(128 + at * 128, 128), 128)].reshape(2048, 128)
            for at in (first_at, second_at)
        ]
        v = dot_tn(jnp.concatenate(cols, 1), DY[...].reshape(2048, 1024))
        part["b"][first_at, :, 16:48, :] = v[0:128].reshape(4, 32, 1024).astype(BF)
        part["b"][second_at, :, 16:48, :] = v[128:256].reshape(4, 32, 1024).astype(BF)

    subs = ("opp", "bwd", "fwd", "own")

    def send_one(h, k, at, to):
        for sub in subs:
            j = getattr(h.two, sub)
            msgs.send((h.name, "one", k, sub), part[h.name].at[at, j], into_one[h.name].at[k, j], h.one_dev(to))

    def send_forward(h, sub):
        j = getattr(h.two, sub)
        msgs.land((h.name, "one", 0, sub))
        v = part[h.name][h.one.fwd, j].astype(F32) + into_one[h.name][0, j].astype(F32)
        held_one[h.name][j] = v.astype(BF)
        msgs.send((h.name, "one", 2, sub), held_one[h.name].at[j], into_one[h.name].at[2, j], h.one_dev(h.one.fwd))

    def first_sum(h, sub):
        j = getattr(h.two, sub)
        msgs.land((h.name, "one", 1, sub))
        msgs.land((h.name, "one", 2, sub))
        v = part[h.name][h.one.own, j].astype(F32) + into_one[h.name][1, j].astype(F32)
        v = v + into_one[h.name][2, j].astype(F32)
        k = subs.index(sub)
        if sub == "fwd":
            msgs.land((h.name, "two", 0))
            v = v + into_two[h.name][0].astype(F32)
        if sub != "own":
            held_two[h.name][k] = v.astype(BF)
            to = h.two.bwd if sub == "bwd" else h.two.fwd
            msgs.send((h.name, "two", k), held_two[h.name].at[k], into_two[h.name].at[k], h.two_dev(to))
            return None
        msgs.land((h.name, "two", 1))
        msgs.land((h.name, "two", 2))
        return v + into_two[h.name][1].astype(F32) + into_two[h.name][2].astype(F32)

    v = dot_tn(CAT[:, :, 0:128].reshape(2048, 128), DY[...].reshape(2048, 1024)).reshape(4, 4, 8, 1024)
    part["b"][:, :, 0:16, :] = jnp.concatenate([v, jnp.zeros_like(v)], 2).astype(BF)
    grad_a(ring_x.opp)
    send_one(ha, 0, ring_x.opp, ring_x.fwd)
    grad_b(ring_z.opp, ring_z.bwd)
    send_one(hb, 0, ring_z.opp, ring_z.fwd)
    send_one(hb, 1, ring_z.bwd, ring_z.bwd)

    for a, src, _ in arrays:
        msgs.land(("y", a, 0))
        join(a, src, ring_y.fwd, extra=0)
        msgs.send(("y", a, 2), src.at[mine(ring_y.fwd)], from_y.at[a, 2], y_dev(ring_y.fwd))

    grad_a(ring_x.bwd)
    send_one(ha, 1, ring_x.bwd, ring_x.bwd)
    grad_a(ring_x.fwd)
    for sub in subs:
        send_forward(ha, sub)
    grad_b(ring_z.fwd, ring_z.own)
    for sub in subs:
        send_forward(hb, sub)
    grad_a(ring_x.own)

    for k in range(3):
        msgs.land(("v1", k))
    vec_sum[...] = vec[...] + vec_one[0] + vec_one[1] + vec_one[2]
    for k, o in enumerate(z_others):
        msgs.send(("v2", k), vec_sum, vec_two.at[k], z_dev(o))

    for sub in ("opp", "bwd"):
        for h in halves:
            first_sum(h, sub)

    for k in range(3):
        msgs.land(("v2", k))
    vec_all[t] = vec_sum[...] + vec_two[0] + vec_two[1] + vec_two[2]
    for k, o in enumerate(others):
        msgs.send(("v3", k), vec_all.at[t], vec_all.at[t], group_member(x, z, o))

    for h in halves:
        first_sum(h, "fwd")

    for a, src, dst in arrays:
        msgs.land(("sib", a, 3))
        msgs.land(("y", a, 1))
        msgs.land(("y", a, 2))

        def add(r, a=a, src=src, dst=dst):
            v = src[mine(y), r, :].astype(F32) + sib[a, y, r, :].astype(F32)
            dst[r, :] = v + from_y[a, 1, r, :].astype(F32) + from_y[a, 2, r, :].astype(F32)

        slabs(256, 32, add)

    fin_a = m["fin_a"]
    fin_a[...] = first_sum(ha, "own").reshape(8, 8, 896)
    for k, o in enumerate(others):
        msgs.send(("n", k), fin_a.at[o], n_all.at[t], group_member(x, z, o))
    n_all[t] = fin_a[t]
    v = first_sum(hb, "own")
    m["own_dense"][...] = v[0:8]
    grad_fc2[...] = v[16:48]

    @pl.when(moves)
    def _():
        msgs.sent["back"].start()
        msgs.sent["there"].wait_send()
        msgs.sent["back"].wait()

    @pl.when(jnp.logical_not(moves))
    def _():
        grad_dense[...] = m["own_dense"][...]

    msgs.finish()


def whole(*args):
    vmem = pl.BlockSpec(memory_space=pltpu.VMEM)
    hbm = pl.BlockSpec(memory_space=pl.ANY)
    return pl.pallas_call(
        whole_kernel,
        out_shape=(
            jax.ShapeDtypeStruct((256, 1024), F32),
            jax.ShapeDtypeStruct((256, 1024), F32),
            jax.ShapeDtypeStruct((8, 8, 896), F32),
            jax.ShapeDtypeStruct((8, 1024), F32),
            jax.ShapeDtypeStruct((32, 1024), F32),
            jax.ShapeDtypeStruct((8, 8, 256), F32),
            jax.ShapeDtypeStruct((8, 1024), F32),
        ),
        in_specs=[hbm] * len(args),
        out_specs=(vmem,) * 7,
        scratch_shapes=[pltpu.VMEM(*spec) for spec in SCRATCH.values()]
        + [pltpu.SemaphoreType.DMA((MESSAGES,)), pltpu.SemaphoreType.DMA((MESSAGES,)), pltpu.SemaphoreType.DMA((8,))],
        compiler_params=pltpu.CompilerParams(
            collective_id=0, has_side_effects=True, vmem_limit_bytes=VMEM_LIMIT
        ),
        cost_estimate=pl.CostEstimate(flops=20_000_000_000, bytes_accessed=5_000_000, transcendentals=3_000_000),
        name="whole_block",
    )(*args)


def body(tokens, segments, grad_out, ln1_gain, ln1_bias, ln2_gain, ln2_bias, w_qkv, b_qkv,
         w_dense, b_dense, w_fc1, b_fc1, w_fc2, b_fc2):
    me = lax.axis_index("fsdp")

    small = jnp.pad(segments.astype(BF), ((1, 5), (0, 0)))
    at = 0
    for vector in (ln1_gain, ln1_bias, ln2_gain, ln2_bias, b_qkv, b_fc1, b_dense, b_fc2):
        small = small + jnp.pad(vector[None], ((0, 7), (at, 128 - at - vector.shape[0])))
        at += vector.shape[0]
    out_sum, g_sum, n_all, grad_dense, grad_fc2, sums, b_out = whole(
        tokens, grad_out, w_qkv, w_fc1, w_dense, w_fc2, small, jnp.asarray(rotary_table())
    )

    live = (segments.reshape(256, 1) >= 0).astype(F32)
    x = tokens.astype(F32)
    out = (x + live * (out_sum + b_out[0:1, :])).astype(BF)
    centre = x - jnp.mean(x, -1, keepdims=True)
    scale = lax.rsqrt(jnp.mean(centre * centre, -1, keepdims=True) + NORM_EPS)
    normed = centre * scale
    dx = (g_sum - jnp.mean(g_sum, -1, keepdims=True) - normed * jnp.mean(g_sum * normed, -1, keepdims=True)) * scale
    grad_tokens = (grad_out.astype(F32) + dx).astype(BF)

    sums = sums.reshape(8, 2, 1024)
    sum_qkv = sums[:, 0, 0:384].reshape(8, 3, 128).transpose(1, 0, 2).reshape(3072)
    sum_fc1 = sums[:, 0, 384:896].reshape(8, 4, 4, 32).transpose(2, 1, 0, 3).reshape(4096)
    n_qkv = n_all[:, :, 0:384].reshape(8, 8, 3, 128).transpose(1, 2, 0, 3).reshape(8, 3072)
    n_fc1 = n_all[:, :, 384:896].reshape(8, 8, 4, 4, 32).transpose(1, 3, 2, 0, 4).reshape(8, 4096)

    def norm_grads(weight, n, s, gain, bias_of):
        weight = weight.astype(F32)
        grad_w = gain.astype(F32)[:, None] * n + bias_of.astype(F32)[:, None] * s
        return jnp.sum(weight * n, 1), jnp.sum(weight * s, 1), grad_w

    g1_gain, g1_bias, grad_qkv = norm_grads(w_qkv, n_qkv, sum_qkv, ln1_gain, ln1_bias)
    g2_gain, g2_bias, grad_fc1 = norm_grads(w_fc1, n_fc1, sum_fc1, ln2_gain, ln2_bias)
    grad_b_qkv = lax.dynamic_slice(sum_qkv, (me * 24,), (24,))
    grad_b_fc1 = lax.dynamic_slice(sum_fc1, (me * 32,), (32,))
    grad_b_out = lax.dynamic_slice(sums[0, 1], (me * 8,), (8,))
    return (out, grad_tokens, g1_gain, g1_bias, g2_gain, g2_bias, grad_qkv, grad_b_qkv,
            grad_dense, grad_b_out, grad_fc1, grad_b_fc1, grad_fc2, grad_b_out)


def solution(mesh):
    rows, flat = P("fsdp", None), P("fsdp")
    return jax.shard_map(
        body,
        mesh=mesh,
        in_specs=(rows, rows, rows, flat, flat, flat, flat, rows, flat, rows, flat, rows, flat, rows, flat),
        out_specs=(rows, rows, flat, flat, flat, flat, rows, flat, rows, flat, rows, flat, rows, flat),
        check_vma=False,
    )
```

```python
import functools
import math

import jax
import jax.numpy as jnp
import numpy as np
from jax import lax
from jax.experimental import pallas as pl
from jax.experimental.pallas import tpu as pltpu
from jax.sharding import PartitionSpec as P

NORM_EPS = 1e-05
MASKED = -1e30
MESH = pl.DeviceIdType.MESH
BF = jnp.bfloat16
F32 = jnp.float32
VMEM_LIMIT = 60 * 1024 * 1024


def coords():
    i = lax.axis_index("fsdp")
    core = lax.rem(i, 2)
    y = lax.rem(i // 2, 4)
    z = lax.rem(i // 8, 4)
    x = i // 32
    return x, z, y, core


def ident(x, z, y, core):
    return ((x * 4 + z) * 4 + y) * 2 + core


class Ring:
    def __init__(self, at, core):
        step = 1 + 2 * core
        self.own = at
        self.fwd = lax.rem(at + step, 4)
        self.bwd = lax.rem(at + 4 - step, 4)
        self.opp = lax.rem(at + 2, 4)


class Messages:
    def __init__(self, send_sem, recv_sem):
        self.send_sem, self.recv_sem = send_sem, recv_sem
        self.sent, self.landed, self.apart = {}, set(), set()

    def plan(self, name, src, dst, target, apart=False):
        n = len(self.sent)
        copy = pltpu.make_async_remote_copy(
            src_ref=src,
            dst_ref=dst,
            send_sem=self.send_sem.at[n],
            recv_sem=self.recv_sem.at[n],
            device_id=(target,),
            device_id_type=MESH,
        )
        self.sent[name] = copy
        if apart:
            self.apart.add(name)

    def send(self, name, src, dst, target):
        self.plan(name, src, dst, target)
        self.sent[name].start()

    def land(self, name):
        assert name not in self.landed
        self.landed.add(name)
        self.sent[name].wait_recv()

    def finish(self):
        for name, copy in self.sent.items():
            if name not in self.landed and name not in self.apart:
                copy.wait_recv()
        for name, copy in self.sent.items():
            if name not in self.apart:
                copy.wait_send()


def group_member(x, z, t):
    return ident(x, z, 0, 0) + t


def dot(a, b):
    return jnp.dot(a, b, preferred_element_type=F32)


def dot_nt(a, b):
    return lax.dot_general(a, b, (((1,), (1,)), ((), ())), preferred_element_type=F32)


def dot_tn(a, b):
    return lax.dot_general(a, b, (((0,), (0,)), ((), ())), preferred_element_type=F32)


def turn(u, cosine, sine, low_lanes):
    moved = jnp.where(low_lanes, pltpu.roll(u, 120, 1), pltpu.roll(u, 8, 1))
    return u * cosine + moved * sine


def rotary_table():
    m = 8
    angle = np.arange(128, dtype=np.float64)[:, None] * (10000.0 ** (-2.0 * np.arange(m) / 16.0))[None, :]
    cosine = np.ones((128, 128), np.float32)
    sine = np.zeros((128, 128), np.float32)
    for head in (0, 64):
        cosine[:, head : head + m] = np.cos(angle)
        cosine[:, head + m : head + 2 * m] = np.cos(angle)
        sine[:, head : head + m] = -np.sin(angle)
        sine[:, head + m : head + 2 * m] = np.sin(angle)
    parts = []
    for table in (cosine, sine):
        high = table.astype(jnp.bfloat16)
        parts += [high, (table - high.astype(np.float32)).astype(jnp.bfloat16)]
    return np.concatenate(parts, 1)


def slabs(rows, step, fn):
    def one(i, carry):
        fn(pl.ds(pl.multiple_of(i * step, step), step))
        return carry

    lax.fori_loop(0, rows // step, one, 0)


class Half:
    def __init__(self, name, one, one_dev, two, two_dev, rows):
        self.name, self.one, self.one_dev, self.two, self.two_dev, self.rows = name, one, one_dev, two, two_dev, rows


def unpack_small(packed, t):
    packed = packed.astype(BF)

    def pick(lanes, columns, owner):
        j = lax.broadcasted_iota(jnp.int32, (128, lanes), 0)
        at = lax.broadcasted_iota(jnp.int32, (128, lanes), 1)
        of_row = ((j >> 3) & 3) * 32 + (j >> 5) * 8 + (j & 7)
        select = jnp.zeros((128, lanes), F32)
        for column in columns(at):
            select = select + (j == column).astype(F32)
        rows = dot(packed, select.astype(BF))
        return jnp.sum(jnp.where(of_row == owner(at), rows, 0.0), 0, keepdims=True)

    eight = lambda *starts: pick(1024, lambda at: [s + (at & 7) for s in starts], lambda at: at >> 3)
    ln = [eight(8 * v) for v in range(4)]
    b_out = eight(88, 96)
    qkv_at = lambda at: (at >> 7) * 1024 + t * 128 + (at & 127)
    d24 = lambda c: (c * 2731) >> 16
    b_qkv = pick(384, lambda at: [32 + qkv_at(at) - 24 * d24(qkv_at(at))], lambda at: d24(qkv_at(at)))
    b_fc1 = pick(512, lambda at: [56 + (at & 31)], lambda at: ((at >> 5) & 3) * 32 + (at >> 7) * 8 + t)
    return ln, b_qkv, b_fc1, b_out


def rows_pass(x, dy, seg, w1_ref, w2_ref, ln_ref, bias_ref, table_ref):
    x = x.astype(F32)
    centre = x - jnp.mean(x, 1, keepdims=True)
    spread = jnp.mean(centre * centre, 1, keepdims=True)
    normed = centre * lax.rsqrt(spread + NORM_EPS)
    g1, g2 = ln_ref[0:1, :], ln_ref[2:3, :]
    a1 = (normed * g1 + ln_ref[1:2, :]).astype(BF)
    a2 = (normed * g2 + ln_ref[3:4, :]).astype(BF)
    joined = dot(a1, w1_ref[:, 0:384]) + bias_ref[0:1, 0:384]

    row = lax.broadcasted_iota(jnp.int32, (128, 128), 0)
    col = lax.broadcasted_iota(jnp.int32, (128, 128), 1)
    low_lanes = (col & 63) < 8
    head0 = col < 64
    ones = jnp.ones((128, 128), BF)
    blocks = range(2)
    parts = [slice(b * 128, b * 128 + 128) for b in blocks]

    def stacked(u):
        zero = jnp.zeros_like(u)
        return jnp.concatenate([jnp.where(head0, u, zero), jnp.where(head0, zero, u)], 0)

    def folded(u):
        return jnp.where(head0, u[0:128], u[128:256])

    masks, lives, tables = [], [], []
    for b in blocks:
        seg_c = jnp.broadcast_to(seg[b : b + 1, :], (128, 128))
        seg_r = seg_c.T
        allowed = (seg_c == seg_r) & (col <= row)
        position = jnp.sum(allowed.astype(F32), 1, keepdims=True) - 1.0
        onehot = (col == position.astype(jnp.int32)).astype(BF)
        tables.append(dot(onehot, table_ref[...]))
        masks.append(jnp.concatenate([allowed, allowed], 0))
        lives.append((seg_r[:, 0:1] >= 0.0).astype(F32))
    live = jnp.concatenate(lives, 0)
    cosine = [u[:, 0:128] + u[:, 128:256] for u in tables]
    sine = [u[:, 256:384] + u[:, 384:512] for u in tables]
    q = [turn(joined[parts[b], 0:128], cosine[b], sine[b], low_lanes).astype(BF) for b in blocks]
    k = [turn(joined[parts[b], 128:256], cosine[b], sine[b], low_lanes).astype(BF) for b in blocks]
    v = [joined[parts[b], 256:384].astype(BF) for b in blocks]
    q2 = [stacked(u) for u in q]
    scores = [jnp.where(masks[b], dot_nt(q2[b], k[b]) * 0.125, MASKED) for b in blocks]
    d_cat = dot_nt(dy, w2_ref[...]) * live
    e = [jnp.exp(u - jnp.max(u, 1, keepdims=True)) for u in scores]
    hidden = dot(a2, w1_ref[:, 384:896]) + bias_ref[0:1, 384:896]
    weighted = [dot(e[b].astype(BF), jnp.concatenate([v[b], ones], 1)) for b in blocks]
    d_context = d_cat[:, 0:128].astype(BF)
    dc2 = [stacked(d_context[p]) for p in parts]
    d_probs = [dot_nt(dc2[b], v[b]) for b in blocks]
    inverse = [1.0 / u[:, 128:256] for u in weighted]
    probs = [e[b] * inverse[b] for b in blocks]
    along = [jnp.sum(probs[b] * d_probs[b], 1, keepdims=True) for b in blocks]
    phi_cdf = 0.5 + 0.5 * lax.erf(hidden * math.sqrt(0.5))
    active = ((hidden * phi_cdf).astype(BF).astype(F32) * live).astype(BF)
    slope = phi_cdf + hidden * (jnp.exp(hidden * hidden * -0.5) * (1.0 / math.sqrt(2.0 * math.pi)))
    d_hidden = d_cat[:, 128:640] * slope
    d_scores = [(probs[b] * (d_probs[b] - along[b])).astype(BF) for b in blocks]
    contexts = [
        (folded(weighted[b][:, 0:128] * inverse[b]).astype(BF).astype(F32) * lives[b]).astype(BF) for b in blocks
    ]
    d_v = [dot_tn(probs[b].astype(BF), dc2[b]) for b in blocks]
    d_q = [folded(dot(d_scores[b], k[b]) * 0.125) for b in blocks]
    d_k = [dot_tn(d_scores[b], q2[b]) * 0.125 for b in blocks]
    d_joined = [
        jnp.concatenate(
            [turn(d_q[b], cosine[b], -sine[b], low_lanes), turn(d_k[b], cosine[b], -sine[b], low_lanes), d_v[b]], 1
        )
        for b in blocks
    ]
    cat = jnp.concatenate([jnp.concatenate(contexts, 0), active], 1)
    out = dot(cat, w2_ref[...])
    d_all = jnp.concatenate([jnp.concatenate(d_joined, 0), d_hidden], 1)
    column_sums = jnp.sum(d_all, 0, keepdims=True), jnp.sum(dy.astype(F32) * live, 0, keepdims=True)
    d_all_b = d_all.astype(BF)
    g = g1 * dot_nt(d_all_b[:, 0:384], w1_ref[:, 0:384]) + g2 * dot_nt(d_all_b[:, 384:896], w1_ref[:, 384:896])
    return out, g, normed.astype(BF), d_all_b, cat, column_sums


SCRATCH = dict(
    X=((8, 256, 1024), BF),
    DY=((8, 256, 1024), BF),
    qkv=((8, 3072), BF),
    fc1=((8, 4096), BF),
    small=((8, 128), BF),
    table=((128, 512), BF),
    dense=((8, 1024), BF),
    fc2=((32, 1024), BF),
    stage=((8, 8, 1024), BF),
    AW=((8, 8, 1024), BF),
    WA=((4, 4, 64, 896), BF),
    WB=((4, 4, 48, 1024), BF),
    w1=((1024, 896), BF),
    w2=((640, 1024), BF),
    ln=((8, 1024), F32),
    bias=((8, 896), F32),
    OUT=((8, 256, 1024), BF),
    G=((8, 256, 1024), BF),
    NB=((8, 256, 1024), BF),
    DALL=((8, 256, 896), BF),
    CAT=((8, 256, 640), BF),
    sums=((8, 1024), F32),
    sib=((2, 4, 256, 1024), BF),
    from_y=((2, 3, 256, 1024), BF),
    ga=((4, 4, 64, 896), BF),
    gb=((4, 4, 48, 1024), BF),
    one_a=((3, 4, 64, 896), BF),
    one_b=((3, 4, 48, 1024), BF),
    held_one_a=((4, 64, 896), BF),
    held_one_b=((4, 48, 1024), BF),
    two_a=((3, 64, 896), BF),
    two_b=((3, 48, 1024), BF),
    held_two_a=((3, 64, 896), BF),
    held_two_b=((3, 48, 1024), BF),
    fin_a=((8, 8, 896), F32),
    own_dense=((8, 1024), F32),
    vec=((8, 256), F32),
    vec_one=((3, 8, 256), F32),
    vec_sum=((8, 256), F32),
    vec_two=((3, 8, 256), F32),
)
MESSAGES = 7 + 1 + 2 * 7 + 2 * (3 + 12) + 13 + 2 * (4 + 3) + 2 * (12 + 3) + 7 + 1


def whole_kernel(x_ref, dy_ref, wqkv_ref, wfc1_ref, dense_ref, fc2_ref, small_ref, table_hbm,
                 out_sum, g_sum, n_all, grad_dense, grad_fc2, vec_all, b_out, *scratch):
    m = dict(zip(SCRATCH, scratch))
    send_sem, recv_sem, local_sem = scratch[len(SCRATCH) :]
    X, DY, AW, WA, WB, stage, table_ref = (m[k] for k in ("X", "DY", "AW", "WA", "WB", "stage", "table"))
    x, z, y, core = coords()
    t = y * 2 + core
    ring_y, ring_x, ring_z = Ring(y, core), Ring(x, core), Ring(z, core)
    y_dev = lambda to: ident(x, z, to, core)
    x_dev = lambda to: ident(to, z, y, core)
    z_dev = lambda to: ident(x, to, y, core)
    sibling = ident(x, z, y, 1 - core)
    others = [lax.rem(t + k, 8) for k in range(1, 8)]
    x_others = [lax.rem(x + k, 4) for k in range(1, 4)]
    z_others = [lax.rem(z + k, 4) for k in range(1, 4)]
    mine = lambda at: at * 2 + core
    hers = lambda at: at * 2 + 1 - core
    halves = (
        Half("a", ring_x, x_dev, ring_z, z_dev, 64),
        Half("b", ring_z, z_dev, ring_x, x_dev, 48),
    )
    owner = t * 16 + z * 4 + x
    me = ident(x, z, y, core)
    spreader = ident(lax.rem(me, 4), lax.rem(me // 4, 4), 0, 0) + me // 16
    moves = spreader != me

    local = [
        pltpu.make_async_copy(src, dst, local_sem.at[n])
        for n, (src, dst) in enumerate(
            (
                (wqkv_ref, m["qkv"]),
                (wfc1_ref, m["fc1"]),
                (small_ref, m["small"]),
                (fc2_ref, m["fc2"]),
                (table_hbm, table_ref),
                (x_ref, X.at[t]),
                (dy_ref, DY.at[t]),
            )
        )
    ]
    for copy in local:
        copy.start()
    barrier = pltpu.get_barrier_semaphore()
    near = [group_member(x, z, o) for o in others] + [x_dev(o) for o in x_others] + [z_dev(o) for o in z_others]
    for target in near:
        pl.semaphore_signal(barrier, inc=1, device_id=(target,), device_id_type=MESH)

    @pl.when(moves)
    def _():
        for target in (owner, spreader):
            pl.semaphore_signal(barrier, inc=1, device_id=(target,), device_id_type=MESH)

    for copy in local[:4]:
        copy.wait()
    fc1_rows = m["fc1"][...].astype(F32)
    for o in range(8):
        for sec in range(3):
            stage[o, :, sec * 128 : sec * 128 + 128] = m["qkv"][:, sec * 1024 + o * 128 : sec * 1024 + o * 128 + 128]
        columns = [fc1_rows[:, at : at + 32] for at in [p * 1024 + q * 256 + o * 32 for q in range(4) for p in range(4)]]
        stage[o, :, 384:896] = jnp.concatenate(columns, 1).astype(BF)
        stage[o, :, 896:1024] = m["small"][...]

    @pl.when(moves)
    def _():
        pl.semaphore_wait(barrier, len(near) + 2)

    @pl.when(jnp.logical_not(moves))
    def _():
        pl.semaphore_wait(barrier, len(near))

    msgs = Messages(send_sem, recv_sem)

    for k, o in enumerate(others):
        msgs.send(("w", k), stage.at[o], AW.at[t], group_member(x, z, o))
    lone = pltpu.make_async_copy(dense_ref, m["dense"], local_sem.at[7])
    msgs.plan("there", dense_ref, m["dense"], spreader, apart=True)
    msgs.plan("back", m["own_dense"], grad_dense, owner, apart=True)

    @pl.when(moves)
    def _():
        msgs.sent["there"].start()

    @pl.when(jnp.logical_not(moves))
    def _():
        lone.start()

    def own_rows(name, src, dst):
        msgs.send((name, 0), src, dst.at[t], y_dev(ring_y.fwd))
        msgs.send((name, 1), src, dst.at[t], y_dev(ring_y.bwd))
        msgs.send((name, 2), src, dst.at[t], sibling)

    own_rows("x", x_ref, X)
    own_rows("d", dy_ref, DY)
    AW[t] = stage[t]
    for k in range(7):
        msgs.land(("w", k))
    for pair in range(4):
        both = jnp.concatenate([AW[2 * pair].astype(F32), AW[2 * pair + 1].astype(F32)], 0)
        WA[x, z, 16 * pair : 16 * pair + 16, :] = both[:, 0:896].astype(BF)

    @pl.when(moves)
    def _():
        msgs.sent["there"].wait_recv()

    @pl.when(jnp.logical_not(moves))
    def _():
        lone.wait()

    member = lax.broadcasted_iota(jnp.int32, (8, 128), 0)
    small = jnp.zeros((8, 128), F32)
    for k in range(8):
        small = jnp.where(member == k, AW[k, :, 896:1024].astype(F32)[0:1], small)
    small = jnp.concatenate([small, jnp.zeros((8, 896), F32)], 1)
    WB[z, x, 0:16, :] = jnp.concatenate([m["dense"][...].astype(F32), small], 0).astype(BF)
    WB[z, x, 16:48, :] = m["fc2"][...]

    gathered = {"a": WA, "b": WB}

    def first(h, k, at, to):
        ref = gathered[h.name].at[at, h.two.own]
        msgs.send((h.name, "p", k), ref, ref, h.one_dev(to))

    def second(h, sub, k, at, frm, to):
        ref = gathered[h.name].at[at, frm]
        msgs.send((h.name, sub, k), ref, ref, h.two_dev(to))

    def spread(h, sub):
        at = getattr(h.one, sub)
        second(h, sub, 0, at, h.two.own, h.two.fwd)
        second(h, sub, 1, at, h.two.own, h.two.bwd)

    def pass_on(h, sub):
        msgs.land((h.name, sub, 0))
        second(h, sub, 2, getattr(h.one, sub), h.two.bwd, h.two.fwd)

    for h in halves:
        first(h, 0, h.one.own, h.one.fwd)
        first(h, 1, h.one.own, h.one.bwd)
        spread(h, "own")
    for h in halves:
        msgs.land((h.name, "p", 0))
        first(h, 2, h.one.bwd, h.one.fwd)
        spread(h, "bwd")
    for h in halves:
        msgs.land((h.name, "p", 1))
        spread(h, "fwd")
    for h in halves:
        msgs.land((h.name, "p", 2))
        spread(h, "opp")
    for h in halves:
        pass_on(h, "own")

    def rows_on(name, dst):
        msgs.land((name, 0))
        ref = dst.at[mine(ring_y.bwd)]
        msgs.send((name, 4), ref, ref, sibling)
        msgs.land((name, 1))
        ref = dst.at[mine(ring_y.fwd)]
        msgs.send((name, 5), ref, ref, sibling)

    def rows_far(name, dst):
        ref = dst.at[mine(ring_y.bwd)]
        msgs.send((name, 3), ref, ref, y_dev(ring_y.fwd))

    for sub in ("bwd", "fwd", "opp"):
        for h in halves:
            pass_on(h, sub)
    rows_on("x", X)
    rows_on("d", DY)
    rows_far("x", X)
    rows_far("d", DY)
    for h in halves:
        for sub in ("own", "bwd", "fwd", "opp"):
            msgs.land((h.name, sub, 1))
            msgs.land((h.name, sub, 2))
    for copy in local[4:]:
        copy.wait()

    w1, w2, ln, bias = m["w1"], m["w2"], m["ln"], m["bias"]
    w1[...] = WA[...].reshape(1024, 896)
    mixed = WB[:, :, 0:16, :].astype(F32)
    w2[0:128, :] = mixed[:, :, 0:8, :].reshape(128, 1024).astype(BF)
    w2[128:640, :] = WB[:, :, 16:48, :].reshape(512, 1024)
    norms, b_qkv, b_fc1, b_both = unpack_small(mixed[:, :, 8:16, 0:128].reshape(128, 128), t)
    for v in range(4):
        ln[v : v + 1, :] = norms[v]
    bias[0:1, 0:384] = b_qkv
    bias[0:1, 384:896] = b_fc1
    b_out[...] = jnp.broadcast_to(b_both, (8, 1024))
    sums = m["sums"]
    sums[...] = jnp.zeros_like(sums)

    OUT, G, NB, DALL, CAT, sib, from_y = (m[k] for k in ("OUT", "G", "NB", "DALL", "CAT", "sib", "from_y"))
    arrays = ((0, OUT, out_sum), (1, G, g_sum))
    chips = [lax.rem(y + k, 4) for k in (0, 3, 1, 2)]

    def join(a, src, at, extra=None):
        def add(r):
            v = src[mine(at), r, :].astype(F32) + sib[a, at, r, :].astype(F32)
            if extra is not None:
                v = v + from_y[a, extra, r, :].astype(F32)
            src[mine(at), r, :] = v.astype(BF)

        slabs(256, 32, add)

    for name, dst in (("x", X), ("d", DY)):
        ref = dst.at[mine(ring_y.opp)]
        msgs.plan((name, 6), ref, ref, sibling)
    for a, src, _ in arrays:
        for k in range(4):
            msgs.plan(("sib", a, k), src.at[hers(chips[k])], sib.at[a, chips[k]], sibling)
        msgs.plan(("y", a, 1), src.at[mine(ring_y.bwd)], from_y.at[a, 1], y_dev(ring_y.bwd))
        msgs.plan(("y", a, 0), src.at[mine(ring_y.opp)], from_y.at[a, 0], y_dev(ring_y.fwd))

    def before(s):
        @pl.when(s == 0)
        def _():
            for name in "xd":
                msgs.land((name, 2))

        @pl.when(s == 2)
        def _():
            for name in "xd":
                msgs.land((name, 4))
                msgs.land((name, 5))

        @pl.when(s == 4)
        def _():
            for name in "xd":
                msgs.land((name, 3))
                msgs.sent[name, 6].start()

        @pl.when(s == 6)
        def _():
            for name in "xd":
                msgs.land((name, 6))

    def after(s):
        for k in range(4):

            @pl.when(s == 2 * k)
            def _(k=k):
                for a, src, _ in arrays:
                    msgs.sent["sib", a, k].start()

        @pl.when(s == 5)
        def _():
            for a, src, _ in arrays:
                msgs.land(("sib", a, 1))
                msgs.land(("sib", a, 2))
                join(a, src, ring_y.bwd)
                msgs.sent["y", a, 1].start()

    def one_slot(s, carry):
        before(s)
        k = s // 2
        chip = jnp.where(k == 0, chips[0], jnp.where(k == 1, chips[1], jnp.where(k == 2, chips[2], chips[3])))
        slot = chip * 2 + jnp.where(s % 2 == 0, 1 - core, core)
        out, g, normed, d_all, cat, column_sums = rows_pass(
            X[slot], DY[slot], AW[slot][:, 896:1024].astype(F32)[1:3], w1, w2, ln, bias, table_ref
        )
        OUT[slot] = out.astype(BF)
        G[slot] = g.astype(BF)
        NB[slot] = normed
        DALL[slot] = d_all
        CAT[slot] = cat
        sums[0:1, 0:896] += column_sums[0]
        sums[1:2, :] += column_sums[1]
        after(s)
        return carry

    lax.fori_loop(0, 8, one_slot, 0)

    vec, vec_one, vec_sum, vec_two = (m[k] for k in ("vec", "vec_one", "vec_sum", "vec_two"))
    for i in range(8):
        vec[i : i + 1, :] = sums[i // 4 : i // 4 + 1, (i % 4) * 256 : (i % 4) * 256 + 256]
    for k, o in enumerate(x_others):
        msgs.send(("v1", k), vec, vec_one.at[k], x_dev(o))

    part = {"a": m["ga"], "b": m["gb"]}
    into_one = {"a": m["one_a"], "b": m["one_b"]}
    held_one = {"a": m["held_one_a"], "b": m["held_one_b"]}
    into_two = {"a": m["two_a"], "b": m["two_b"]}
    held_two = {"a": m["held_two_a"], "b": m["held_two_b"]}
    ha, hb = halves

    def grad_a(at):
        lanes = pl.ds(pl.multiple_of(at * 256, 256), 256)
        v = dot_tn(NB[:, :, lanes].reshape(2048, 256), DALL[...].reshape(2048, 896))
        part["a"][at] = v.reshape(4, 64, 896).astype(BF)

    def grad_b(first_at, second_at):
        cols = [
            CAT[:, :, pl.ds(pl.multiple_of(128 + at * 128, 128), 128)].reshape(2048, 128)
            for at in (first_at, second_at)
        ]
        v = dot_tn(jnp.concatenate(cols, 1), DY[...].reshape(2048, 1024))
        part["b"][first_at, :, 16:48, :] = v[0:128].reshape(4, 32, 1024).astype(BF)
        part["b"][second_at, :, 16:48, :] = v[128:256].reshape(4, 32, 1024).astype(BF)

    subs = ("opp", "bwd", "fwd", "own")

    def send_one(h, k, at, to):
        for sub in subs:
            j = getattr(h.two, sub)
            msgs.send((h.name, "one", k, sub), part[h.name].at[at, j], into_one[h.name].at[k, j], h.one_dev(to))

    def send_forward(h, sub):
        j = getattr(h.two, sub)
        msgs.land((h.name, "one", 0, sub))
        v = part[h.name][h.one.fwd, j].astype(F32) + into_one[h.name][0, j].astype(F32)
        held_one[h.name][j] = v.astype(BF)
        msgs.send((h.name, "one", 2, sub), held_one[h.name].at[j], into_one[h.name].at[2, j], h.one_dev(h.one.fwd))

    def first_sum(h, sub):
        j = getattr(h.two, sub)
        msgs.land((h.name, "one", 1, sub))
        msgs.land((h.name, "one", 2, sub))
        v = part[h.name][h.one.own, j].astype(F32) + into_one[h.name][1, j].astype(F32)
        v = v + into_one[h.name][2, j].astype(F32)
        k = subs.index(sub)
        if sub == "fwd":
            msgs.land((h.name, "two", 0))
            v = v + into_two[h.name][0].astype(F32)
        if sub != "own":
            held_two[h.name][k] = v.astype(BF)
            to = h.two.bwd if sub == "bwd" else h.two.fwd
            msgs.send((h.name, "two", k), held_two[h.name].at[k], into_two[h.name].at[k], h.two_dev(to))
            return None
        msgs.land((h.name, "two", 1))
        msgs.land((h.name, "two", 2))
        return v + into_two[h.name][1].astype(F32) + into_two[h.name][2].astype(F32)

    grad_a(ring_x.opp)
    send_one(ha, 0, ring_x.opp, ring_x.fwd)

    for a, src, _ in arrays:
        msgs.land(("sib", a, 3))
        join(a, src, ring_y.opp)
        msgs.sent["y", a, 0].start()

    grad_a(ring_x.bwd)
    send_one(ha, 1, ring_x.bwd, ring_x.bwd)
    v = dot_tn(CAT[:, :, 0:128].reshape(2048, 128), DY[...].reshape(2048, 1024)).reshape(4, 4, 8, 1024)
    part["b"][:, :, 0:16, :] = jnp.concatenate([v, jnp.zeros_like(v)], 2).astype(BF)
    grad_b(ring_z.opp, ring_z.bwd)
    send_one(hb, 0, ring_z.opp, ring_z.fwd)
    send_one(hb, 1, ring_z.bwd, ring_z.bwd)
    grad_a(ring_x.fwd)
    for sub in subs:
        send_forward(ha, sub)
    grad_b(ring_z.fwd, ring_z.own)
    for sub in subs:
        send_forward(hb, sub)

    for a, src, _ in arrays:
        msgs.land(("y", a, 0))
        join(a, src, ring_y.fwd, extra=0)
        msgs.send(("y", a, 2), src.at[mine(ring_y.fwd)], from_y.at[a, 2], y_dev(ring_y.fwd))
    grad_a(ring_x.own)

    for k in range(3):
        msgs.land(("v1", k))
    vec_sum[...] = vec[...] + vec_one[0] + vec_one[1] + vec_one[2]
    for k, o in enumerate(z_others):
        msgs.send(("v2", k), vec_sum, vec_two.at[k], z_dev(o))

    for sub in ("opp", "bwd"):
        for h in halves:
            first_sum(h, sub)

    for k in range(3):
        msgs.land(("v2", k))
    vec_all[t] = vec_sum[...] + vec_two[0] + vec_two[1] + vec_two[2]
    for k, o in enumerate(others):
        msgs.send(("v3", k), vec_all.at[t], vec_all.at[t], group_member(x, z, o))

    for h in halves:
        first_sum(h, "fwd")

    v = first_sum(hb, "own")
    m["own_dense"][...] = v[0:8]
    grad_fc2[...] = v[16:48]

    @pl.when(moves)
    def _():
        msgs.sent["back"].start()

    @pl.when(jnp.logical_not(moves))
    def _():
        grad_dense[...] = m["own_dense"][...]

    fin_a = m["fin_a"]
    fin_a[...] = first_sum(ha, "own").reshape(8, 8, 896)
    for k, o in enumerate(others):
        msgs.send(("n", k), fin_a.at[o], n_all.at[t], group_member(x, z, o))
    n_all[t] = fin_a[t]

    for a, src, dst in arrays:
        msgs.land(("sib", a, 0))
        msgs.land(("y", a, 1))
        msgs.land(("y", a, 2))

        def add(r, a=a, src=src, dst=dst):
            v = src[mine(y), r, :].astype(F32) + sib[a, y, r, :].astype(F32)
            dst[r, :] = v + from_y[a, 1, r, :].astype(F32) + from_y[a, 2, r, :].astype(F32)

        slabs(256, 32, add)

    @pl.when(moves)
    def _():
        msgs.sent["there"].wait_send()
        msgs.sent["back"].wait()

    msgs.finish()


def whole(*args):
    vmem = pl.BlockSpec(memory_space=pltpu.VMEM)
    hbm = pl.BlockSpec(memory_space=pl.ANY)
    return pl.pallas_call(
        whole_kernel,
        out_shape=(
            jax.ShapeDtypeStruct((256, 1024), F32),
            jax.ShapeDtypeStruct((256, 1024), F32),
            jax.ShapeDtypeStruct((8, 8, 896), F32),
            jax.ShapeDtypeStruct((8, 1024), F32),
            jax.ShapeDtypeStruct((32, 1024), F32),
            jax.ShapeDtypeStruct((8, 8, 256), F32),
            jax.ShapeDtypeStruct((8, 1024), F32),
        ),
        in_specs=[hbm] * len(args),
        out_specs=(vmem,) * 7,
        scratch_shapes=[pltpu.VMEM(*spec) for spec in SCRATCH.values()]
        + [pltpu.SemaphoreType.DMA((MESSAGES,)), pltpu.SemaphoreType.DMA((MESSAGES,)), pltpu.SemaphoreType.DMA((8,))],
        compiler_params=pltpu.CompilerParams(
            collective_id=0, has_side_effects=True, vmem_limit_bytes=VMEM_LIMIT
        ),
        cost_estimate=pl.CostEstimate(flops=20_000_000_000, bytes_accessed=5_000_000, transcendentals=3_000_000),
        name="whole_block",
    )(*args)


def finish_kernel(*refs):
    given, results, held, sems = refs[:12], refs[12:26], refs[26:38], refs[38]
    copies = [pltpu.make_async_copy(src, dst, sems.at[n]) for n, (src, dst) in enumerate(zip(given, held))]
    for copy in copies:
        copy.start()
    for copy in copies:
        copy.wait()
    x_ref, dy_ref, out_sum, g_sum, n_all, dense_in, fc2_in, vec_all, b_out, small_ref, wqkv_ref, wfc1_ref = held
    (out_ref, dx_ref, g1_gain, g1_bias, g2_gain, g2_bias, grad_qkv, grad_b_qkv,
     grad_dense, grad_b_out, grad_fc1, grad_b_fc1, grad_fc2, grad_b_last) = results
    me = lax.axis_index("fsdp")
    small = small_ref[...].astype(F32)
    lives = [jnp.broadcast_to(small[b : b + 1, :], (128, 128)).T[:, 0:1] >= 0.0 for b in (1, 2)]
    live = jnp.concatenate([u.astype(F32) for u in lives], 0)
    x = x_ref[...].astype(F32)
    out_ref[...] = (x + live * (out_sum[...] + b_out[0:1, :])).astype(BF)
    centre = x - jnp.mean(x, 1, keepdims=True)
    scale = lax.rsqrt(jnp.mean(centre * centre, 1, keepdims=True) + NORM_EPS)
    normed = centre * scale
    g = g_sum[...]
    dx = (g - jnp.mean(g, 1, keepdims=True) - normed * jnp.mean(g * normed, 1, keepdims=True)) * scale
    dx_ref[...] = (dy_ref[...].astype(F32) + dx).astype(BF)

    row = lax.broadcasted_iota(jnp.int32, (8, 128), 0)
    lane = lax.broadcasted_iota(jnp.int32, (8, 128), 1)

    def column(start):
        return jnp.sum(jnp.where(lane == row + start, small[0:1, :], 0.0), 1, keepdims=True)

    def as_lanes(u):
        return jnp.sum(jnp.where(lane == row, u, 0.0), 0, keepdims=True)

    def write(ref, u, count):
        ref[...] = u[0:1, 0:count]

    def shifted(u, by):
        width = u.shape[1]
        return pltpu.roll(jnp.broadcast_to(u, (8, width)), lax.rem(width - by, width), 1)

    n_qkv = jnp.concatenate([n_all[t, :, c * 128 : c * 128 + 128] for c in range(3) for t in range(8)], 1)
    at = ((0, 0), (0, 128), (1, 0))
    s_qkv = jnp.concatenate([vec_all[t, r : r + 1, lo : lo + 128] for r, lo in at for t in range(8)], 1)
    both = []
    for t in range(8):
        sums = jnp.concatenate([vec_all[t, 1:2, 128:256], vec_all[t, 2:3, :], vec_all[t, 3:4, 0:128]], 1)
        both.append(jnp.concatenate([n_all[t, :, 384:896], jnp.broadcast_to(sums, (8, 512))], 0))
    fc1 = jnp.concatenate(
        [both[t][:, (q * 4 + p) * 32 : (q * 4 + p) * 32 + 32] for p in range(4) for q in range(4) for t in range(8)], 1
    )

    def norm_grads(weight, n, s, start, gain_ref, bias_ref, grad_ref):
        weight = weight.astype(F32)
        grad_ref[...] = column(start) * n + column(start + 8) * s
        write(gain_ref, as_lanes(jnp.sum(weight * n, 1, keepdims=True)), 8)
        write(bias_ref, as_lanes(jnp.sum(weight * s, 1, keepdims=True)), 8)

    s_fc1 = fc1[8:9]
    norm_grads(wqkv_ref[...], n_qkv, s_qkv, 0, g1_gain, g1_bias, grad_qkv)
    norm_grads(wfc1_ref[...], fc1[0:8], s_fc1, 16, g2_gain, g2_bias, grad_fc1)
    write(grad_b_qkv, shifted(s_qkv, me * 24), 24)
    write(grad_b_fc1, shifted(s_fc1, me * 32), 32)
    branch = jnp.concatenate([vec_all[0, r : r + 1, :] for r in range(4, 8)], 1)
    branch = shifted(branch, me * 8)
    write(grad_b_out, branch, 8)
    write(grad_b_last, branch, 8)
    grad_dense[...] = dense_in[...]
    grad_fc2[...] = fc2_in[...]


def finish(*args):
    flat = lambda count: jax.ShapeDtypeStruct((1, count), F32)
    full = lambda *shape: jax.ShapeDtypeStruct(shape, F32)
    rows = jax.ShapeDtypeStruct((256, 1024), BF)
    outs = pl.pallas_call(
        finish_kernel,
        out_shape=(rows, rows, flat(8), flat(8), flat(8), flat(8), full(8, 3072), flat(24), full(8, 1024), flat(8),
                   full(8, 4096), flat(32), full(32, 1024), flat(8)),
        in_specs=[pl.BlockSpec(memory_space=pl.ANY)] * len(args),
        scratch_shapes=[pltpu.VMEM(u.shape, u.dtype) for u in args] + [pltpu.SemaphoreType.DMA((len(args),))],
        compiler_params=pltpu.CompilerParams(vmem_limit_bytes=VMEM_LIMIT),
        cost_estimate=pl.CostEstimate(flops=20_000_000, bytes_accessed=6_000_000, transcendentals=0),
        name="finish",
    )(*args)
    return tuple(u.reshape(-1) if u.shape[0] == 1 else u for u in outs)


def body(tokens, segments, grad_out, ln1_gain, ln1_bias, ln2_gain, ln2_bias, w_qkv, b_qkv,
         w_dense, b_dense, w_fc1, b_fc1, w_fc2, b_fc2):
    small = jnp.pad(segments.astype(BF), ((1, 5), (0, 0)))
    at = 0
    for vector in (ln1_gain, ln1_bias, ln2_gain, ln2_bias, b_qkv, b_fc1, b_dense, b_fc2):
        small = small + jnp.pad(vector[None], ((0, 7), (at, 128 - at - vector.shape[0])))
        at += vector.shape[0]
    out_sum, g_sum, n_all, grad_dense, grad_fc2, sums, b_out = whole(
        tokens, grad_out, w_qkv, w_fc1, w_dense, w_fc2, small, jnp.asarray(rotary_table())
    )

    return finish(
        tokens, grad_out, out_sum, g_sum, n_all, grad_dense, grad_fc2, sums, b_out, small, w_qkv, w_fc1
    )


def solution(mesh):
    rows, flat = P("fsdp", None), P("fsdp")
    return jax.shard_map(
        body,
        mesh=mesh,
        in_specs=(rows, rows, rows, flat, flat, flat, flat, rows, flat, rows, flat, rows, flat, rows, flat),
        out_specs=(rows, rows, flat, flat, flat, flat, rows, flat, rows, flat, rows, flat, rows, flat),
        check_vma=False,
    )
```

```python
import functools
import math

import jax
import jax.numpy as jnp
import numpy as np
from jax import lax
from jax.experimental import pallas as pl
from jax.experimental.pallas import tpu as pltpu
from jax.sharding import PartitionSpec as P

NORM_EPS = 1e-05
MASKED = -1e30
MESH = pl.DeviceIdType.MESH
BF = jnp.bfloat16
F32 = jnp.float32
VMEM_LIMIT = 60 * 1024 * 1024


def coords():
    i = lax.axis_index("fsdp")
    core = lax.rem(i, 2)
    y = lax.rem(i // 2, 4)
    z = lax.rem(i // 8, 4)
    x = i // 32
    return x, z, y, core


def ident(x, z, y, core):
    return ((x * 4 + z) * 4 + y) * 2 + core


class Ring:
    def __init__(self, at, core):
        step = 1 + 2 * core
        self.own = at
        self.fwd = lax.rem(at + step, 4)
        self.bwd = lax.rem(at + 4 - step, 4)
        self.opp = lax.rem(at + 2, 4)


class Messages:
    def __init__(self, send_sem, recv_sem):
        self.send_sem, self.recv_sem = send_sem, recv_sem
        self.sent, self.landed, self.apart = {}, set(), set()

    def plan(self, name, src, dst, target, apart=False):
        n = len(self.sent)
        copy = pltpu.make_async_remote_copy(
            src_ref=src,
            dst_ref=dst,
            send_sem=self.send_sem.at[n],
            recv_sem=self.recv_sem.at[n],
            device_id=(target,),
            device_id_type=MESH,
        )
        self.sent[name] = copy
        if apart:
            self.apart.add(name)

    def send(self, name, src, dst, target):
        self.plan(name, src, dst, target)
        self.sent[name].start()

    def land(self, name):
        assert name not in self.landed
        self.landed.add(name)
        self.sent[name].wait_recv()

    def finish(self):
        for name, copy in self.sent.items():
            if name not in self.landed and name not in self.apart:
                copy.wait_recv()
        for name, copy in self.sent.items():
            if name not in self.apart:
                copy.wait_send()


def group_member(x, z, t):
    return ident(x, z, 0, 0) + t


def dot(a, b):
    return jnp.dot(a, b, preferred_element_type=F32)


def dot_nt(a, b):
    return lax.dot_general(a, b, (((1,), (1,)), ((), ())), preferred_element_type=F32)


def dot_tn(a, b):
    return lax.dot_general(a, b, (((0,), (0,)), ((), ())), preferred_element_type=F32)


def turn(u, cosine, sine, low_lanes):
    moved = jnp.where(low_lanes, pltpu.roll(u, 120, 1), pltpu.roll(u, 8, 1))
    return u * cosine + moved * sine


def rotary_table():
    m = 8
    angle = np.arange(128, dtype=np.float64)[:, None] * (10000.0 ** (-2.0 * np.arange(m) / 16.0))[None, :]
    cosine = np.ones((128, 128), np.float32)
    sine = np.zeros((128, 128), np.float32)
    for head in (0, 64):
        cosine[:, head : head + m] = np.cos(angle)
        cosine[:, head + m : head + 2 * m] = np.cos(angle)
        sine[:, head : head + m] = -np.sin(angle)
        sine[:, head + m : head + 2 * m] = np.sin(angle)
    parts = []
    for table in (cosine, sine):
        high = table.astype(jnp.bfloat16)
        parts += [high, (table - high.astype(np.float32)).astype(jnp.bfloat16)]
    return np.concatenate(parts, 1)


def slabs(rows, step, fn):
    def one(i, carry):
        fn(pl.ds(pl.multiple_of(i * step, step), step))
        return carry

    lax.fori_loop(0, rows // step, one, 0)


class Half:
    def __init__(self, name, one, one_dev, two, two_dev, rows):
        self.name, self.one, self.one_dev, self.two, self.two_dev, self.rows = name, one, one_dev, two, two_dev, rows


def unpack_small(packed, t):
    packed = packed.astype(BF)

    def pick(lanes, columns, owner):
        j = lax.broadcasted_iota(jnp.int32, (128, lanes), 0)
        at = lax.broadcasted_iota(jnp.int32, (128, lanes), 1)
        of_row = ((j >> 3) & 3) * 32 + (j >> 5) * 8 + (j & 7)
        select = jnp.zeros((128, lanes), F32)
        for column in columns(at):
            select = select + (j == column).astype(F32)
        rows = dot(packed, select.astype(BF))
        return jnp.sum(jnp.where(of_row == owner(at), rows, 0.0), 0, keepdims=True)

    eight = lambda *starts: pick(1024, lambda at: [s + (at & 7) for s in starts], lambda at: at >> 3)
    ln = [eight(8 * v) for v in range(4)]
    b_out = eight(88, 96)
    qkv_at = lambda at: (at >> 7) * 1024 + t * 128 + (at & 127)
    d24 = lambda c: (c * 2731) >> 16
    b_qkv = pick(384, lambda at: [32 + qkv_at(at) - 24 * d24(qkv_at(at))], lambda at: d24(qkv_at(at)))
    b_fc1 = pick(512, lambda at: [56 + (at & 31)], lambda at: ((at >> 5) & 3) * 32 + (at >> 7) * 8 + t)
    return ln, b_qkv, b_fc1, b_out


def rows_pass(x, dy, seg, w1_ref, w2_ref, ln_ref, bias_ref, table_ref):
    x = x.astype(F32)
    centre = x - jnp.mean(x, 1, keepdims=True)
    spread = jnp.mean(centre * centre, 1, keepdims=True)
    normed = centre * lax.rsqrt(spread + NORM_EPS)
    g1, g2 = ln_ref[0:1, :], ln_ref[2:3, :]
    a1 = (normed * g1 + ln_ref[1:2, :]).astype(BF)
    a2 = (normed * g2 + ln_ref[3:4, :]).astype(BF)
    joined = dot(a1, w1_ref[:, 0:384]) + bias_ref[0:1, 0:384]

    row = lax.broadcasted_iota(jnp.int32, (128, 128), 0)
    col = lax.broadcasted_iota(jnp.int32, (128, 128), 1)
    low_lanes = (col & 63) < 8
    head0 = col < 64
    ones = jnp.ones((128, 128), BF)
    blocks = range(2)
    parts = [slice(b * 128, b * 128 + 128) for b in blocks]

    def stacked(u):
        zero = jnp.zeros_like(u)
        return jnp.concatenate([jnp.where(head0, u, zero), jnp.where(head0, zero, u)], 0)

    def folded(u):
        return jnp.where(head0, u[0:128], u[128:256])

    masks, lives, tables = [], [], []
    for b in blocks:
        seg_c = jnp.broadcast_to(seg[b : b + 1, :], (128, 128))
        seg_r = seg_c.T
        allowed = (seg_c == seg_r) & (col <= row)
        position = jnp.sum(allowed.astype(F32), 1, keepdims=True) - 1.0
        onehot = (col == position.astype(jnp.int32)).astype(BF)
        tables.append(dot(onehot, table_ref[...]))
        masks.append(jnp.concatenate([allowed, allowed], 0))
        lives.append((seg_r[:, 0:1] >= 0.0).astype(F32))
    live = jnp.concatenate(lives, 0)
    cosine = [u[:, 0:128] + u[:, 128:256] for u in tables]
    sine = [u[:, 256:384] + u[:, 384:512] for u in tables]
    q = [turn(joined[parts[b], 0:128], cosine[b], sine[b], low_lanes).astype(BF) for b in blocks]
    k = [turn(joined[parts[b], 128:256], cosine[b], sine[b], low_lanes).astype(BF) for b in blocks]
    v = [joined[parts[b], 256:384].astype(BF) for b in blocks]
    q2 = [stacked(u) for u in q]
    scores = [jnp.where(masks[b], dot_nt(q2[b], k[b]) * 0.125, MASKED) for b in blocks]
    d_cat = dot_nt(dy, w2_ref[...]) * live
    e = [jnp.exp(u - jnp.max(u, 1, keepdims=True)) for u in scores]
    hidden = dot(a2, w1_ref[:, 384:896]) + bias_ref[0:1, 384:896]
    weighted = [dot(e[b].astype(BF), jnp.concatenate([v[b], ones], 1)) for b in blocks]
    d_context = d_cat[:, 0:128].astype(BF)
    dc2 = [stacked(d_context[p]) for p in parts]
    d_probs = [dot_nt(dc2[b], v[b]) for b in blocks]
    inverse = [1.0 / u[:, 128:256] for u in weighted]
    probs = [e[b] * inverse[b] for b in blocks]
    along = [jnp.sum(probs[b] * d_probs[b], 1, keepdims=True) for b in blocks]
    phi_cdf = 0.5 + 0.5 * lax.erf(hidden * math.sqrt(0.5))
    active = ((hidden * phi_cdf).astype(BF).astype(F32) * live).astype(BF)
    slope = phi_cdf + hidden * (jnp.exp(hidden * hidden * -0.5) * (1.0 / math.sqrt(2.0 * math.pi)))
    d_hidden = d_cat[:, 128:640] * slope
    d_scores = [(probs[b] * (d_probs[b] - along[b])).astype(BF) for b in blocks]
    contexts = [
        (folded(weighted[b][:, 0:128] * inverse[b]).astype(BF).astype(F32) * lives[b]).astype(BF) for b in blocks
    ]
    d_v = [dot_tn(probs[b].astype(BF), dc2[b]) for b in blocks]
    d_q = [folded(dot(d_scores[b], k[b]) * 0.125) for b in blocks]
    d_k = [dot_tn(d_scores[b], q2[b]) * 0.125 for b in blocks]
    d_joined = [
        jnp.concatenate(
            [turn(d_q[b], cosine[b], -sine[b], low_lanes), turn(d_k[b], cosine[b], -sine[b], low_lanes), d_v[b]], 1
        )
        for b in blocks
    ]
    cat = jnp.concatenate([jnp.concatenate(contexts, 0), active], 1)
    out = dot(cat, w2_ref[...])
    d_all = jnp.concatenate([jnp.concatenate(d_joined, 0), d_hidden], 1)
    column_sums = jnp.sum(d_all, 0, keepdims=True), jnp.sum(dy.astype(F32) * live, 0, keepdims=True)
    d_all_b = d_all.astype(BF)
    g = g1 * dot_nt(d_all_b[:, 0:384], w1_ref[:, 0:384]) + g2 * dot_nt(d_all_b[:, 384:896], w1_ref[:, 384:896])
    return out, g, normed.astype(BF), d_all_b, cat, column_sums


SCRATCH = dict(
    X=((8, 256, 1024), BF),
    DY=((8, 256, 1024), BF),
    qkv=((8, 3072), BF),
    fc1=((8, 4096), BF),
    small=((8, 128), BF),
    table=((128, 512), BF),
    dense=((8, 1024), BF),
    fc2=((32, 1024), BF),
    stage=((8, 8, 1024), BF),
    AW=((8, 8, 1024), BF),
    WA=((4, 4, 64, 896), BF),
    WB=((4, 4, 48, 1024), BF),
    w1=((1024, 896), BF),
    w2=((640, 1024), BF),
    ln=((8, 1024), F32),
    bias=((8, 896), F32),
    OUT=((8, 256, 1024), BF),
    G=((8, 256, 1024), BF),
    NB=((8, 256, 1024), BF),
    DALL=((8, 256, 896), BF),
    CAT=((8, 256, 640), BF),
    sums=((8, 1024), F32),
    sib=((2, 4, 256, 1024), BF),
    from_y=((2, 3, 256, 1024), BF),
    ga=((4, 4, 64, 896), BF),
    gb=((4, 4, 48, 1024), BF),
    one_a=((3, 4, 64, 896), BF),
    one_b=((3, 4, 48, 1024), BF),
    held_one_a=((4, 64, 896), BF),
    held_one_b=((4, 48, 1024), BF),
    two_a=((3, 64, 896), BF),
    two_b=((3, 48, 1024), BF),
    held_two_a=((3, 64, 896), BF),
    held_two_b=((3, 48, 1024), BF),
    fin_a=((8, 8, 896), F32),
    own_dense=((8, 1024), F32),
    vec=((8, 256), F32),
    vec_one=((3, 8, 256), F32),
    vec_sum=((8, 256), F32),
    vec_two=((3, 8, 256), F32),
)
MESSAGES = 7 + 1 + 2 * 7 + 2 * (3 + 12) + 13 + 2 * (4 + 3) + 2 * (12 + 3) + 7 + 1


def whole_kernel(x_ref, dy_ref, wqkv_ref, wfc1_ref, dense_ref, fc2_ref, small_ref, table_hbm,
                 out_sum, g_sum, n_all, grad_dense, grad_fc2, vec_all, b_out, *scratch):
    m = dict(zip(SCRATCH, scratch))
    send_sem, recv_sem, local_sem = scratch[len(SCRATCH) :]
    X, DY, AW, WA, WB, stage, table_ref = (m[k] for k in ("X", "DY", "AW", "WA", "WB", "stage", "table"))
    x, z, y, core = coords()
    t = y * 2 + core
    ring_y, ring_x, ring_z = Ring(y, core), Ring(x, core), Ring(z, core)
    y_dev = lambda to: ident(x, z, to, core)
    x_dev = lambda to: ident(to, z, y, core)
    z_dev = lambda to: ident(x, to, y, core)
    sibling = ident(x, z, y, 1 - core)
    others = [lax.rem(t + k, 8) for k in range(1, 8)]
    x_others = [lax.rem(x + k, 4) for k in range(1, 4)]
    z_others = [lax.rem(z + k, 4) for k in range(1, 4)]
    mine = lambda at: at * 2 + core
    hers = lambda at: at * 2 + 1 - core
    halves = (
        Half("a", ring_x, x_dev, ring_z, z_dev, 64),
        Half("b", ring_z, z_dev, ring_x, x_dev, 48),
    )
    owner = t * 16 + z * 4 + x
    me = ident(x, z, y, core)
    spreader = ident(lax.rem(me, 4), lax.rem(me // 4, 4), 0, 0) + me // 16
    moves = spreader != me

    local = [
        pltpu.make_async_copy(src, dst, local_sem.at[n])
        for n, (src, dst) in enumerate(
            (
                (wqkv_ref, m["qkv"]),
                (wfc1_ref, m["fc1"]),
                (small_ref, m["small"]),
                (fc2_ref, m["fc2"]),
                (table_hbm, table_ref),
                (x_ref, X.at[t]),
                (dy_ref, DY.at[t]),
            )
        )
    ]
    for copy in local:
        copy.start()
    barrier = pltpu.get_barrier_semaphore()
    near = [group_member(x, z, o) for o in others] + [x_dev(o) for o in x_others] + [z_dev(o) for o in z_others]
    for target in near:
        pl.semaphore_signal(barrier, inc=1, device_id=(target,), device_id_type=MESH)

    @pl.when(moves)
    def _():
        for target in (owner, spreader):
            pl.semaphore_signal(barrier, inc=1, device_id=(target,), device_id_type=MESH)

    for copy in local[:4]:
        copy.wait()
    fc1_rows = m["fc1"][...].astype(F32)
    for o in range(8):
        for sec in range(3):
            stage[o, :, sec * 128 : sec * 128 + 128] = m["qkv"][:, sec * 1024 + o * 128 : sec * 1024 + o * 128 + 128]
        columns = [fc1_rows[:, at : at + 32] for at in [p * 1024 + q * 256 + o * 32 for q in range(4) for p in range(4)]]
        stage[o, :, 384:896] = jnp.concatenate(columns, 1).astype(BF)
        stage[o, :, 896:1024] = m["small"][...]

    @pl.when(moves)
    def _():
        pl.semaphore_wait(barrier, len(near) + 2)

    @pl.when(jnp.logical_not(moves))
    def _():
        pl.semaphore_wait(barrier, len(near))

    msgs = Messages(send_sem, recv_sem)

    for k, o in enumerate(others):
        msgs.send(("w", k), stage.at[o], AW.at[t], group_member(x, z, o))
    lone = pltpu.make_async_copy(dense_ref, m["dense"], local_sem.at[7])
    msgs.plan("there", dense_ref, m["dense"], spreader, apart=True)
    msgs.plan("back", m["own_dense"], grad_dense, owner, apart=True)

    @pl.when(moves)
    def _():
        msgs.sent["there"].start()

    @pl.when(jnp.logical_not(moves))
    def _():
        lone.start()

    def own_rows(name, src, dst):
        msgs.send((name, 0), src, dst.at[t], y_dev(ring_y.fwd))
        msgs.send((name, 1), src, dst.at[t], y_dev(ring_y.bwd))
        msgs.send((name, 2), src, dst.at[t], sibling)

    own_rows("x", x_ref, X)
    own_rows("d", dy_ref, DY)
    AW[t] = stage[t]
    for k in range(7):
        msgs.land(("w", k))
    for pair in range(4):
        both = jnp.concatenate([AW[2 * pair].astype(F32), AW[2 * pair + 1].astype(F32)], 0)
        WA[x, z, 16 * pair : 16 * pair + 16, :] = both[:, 0:896].astype(BF)

    @pl.when(moves)
    def _():
        msgs.sent["there"].wait_recv()

    @pl.when(jnp.logical_not(moves))
    def _():
        lone.wait()

    member = lax.broadcasted_iota(jnp.int32, (8, 128), 0)
    small = jnp.zeros((8, 128), F32)
    for k in range(8):
        small = jnp.where(member == k, AW[k, :, 896:1024].astype(F32)[0:1], small)
    small = jnp.concatenate([small, jnp.zeros((8, 896), F32)], 1)
    WB[z, x, 0:16, :] = jnp.concatenate([m["dense"][...].astype(F32), small], 0).astype(BF)
    WB[z, x, 16:48, :] = m["fc2"][...]

    gathered = {"a": WA, "b": WB}

    def first(h, k, at, to):
        ref = gathered[h.name].at[at, h.two.own]
        msgs.send((h.name, "p", k), ref, ref, h.one_dev(to))

    def second(h, sub, k, at, frm, to):
        ref = gathered[h.name].at[at, frm]
        msgs.send((h.name, sub, k), ref, ref, h.two_dev(to))

    def spread(h, sub):
        at = getattr(h.one, sub)
        second(h, sub, 0, at, h.two.own, h.two.fwd)
        second(h, sub, 1, at, h.two.own, h.two.bwd)

    def pass_on(h, sub):
        msgs.land((h.name, sub, 0))
        second(h, sub, 2, getattr(h.one, sub), h.two.bwd, h.two.fwd)

    for h in halves:
        first(h, 0, h.one.own, h.one.fwd)
        first(h, 1, h.one.own, h.one.bwd)
        spread(h, "own")
    for h in halves:
        msgs.land((h.name, "p", 0))
        first(h, 2, h.one.bwd, h.one.fwd)
        spread(h, "bwd")
    for h in halves:
        msgs.land((h.name, "p", 1))
        spread(h, "fwd")
    for h in halves:
        msgs.land((h.name, "p", 2))
        spread(h, "opp")
    for h in halves:
        pass_on(h, "own")

    def rows_on(name, dst):
        msgs.land((name, 0))
        ref = dst.at[mine(ring_y.bwd)]
        msgs.send((name, 4), ref, ref, sibling)
        msgs.land((name, 1))
        ref = dst.at[mine(ring_y.fwd)]
        msgs.send((name, 5), ref, ref, sibling)

    def rows_far(name, dst):
        ref = dst.at[mine(ring_y.bwd)]
        msgs.send((name, 3), ref, ref, y_dev(ring_y.fwd))

    for sub in ("bwd", "fwd", "opp"):
        for h in halves:
            pass_on(h, sub)
    rows_on("x", X)
    rows_on("d", DY)
    rows_far("x", X)
    rows_far("d", DY)
    for h in halves:
        for sub in ("own", "bwd", "fwd", "opp"):
            msgs.land((h.name, sub, 1))
            msgs.land((h.name, sub, 2))
    for copy in local[4:]:
        copy.wait()

    w1, w2, ln, bias = m["w1"], m["w2"], m["ln"], m["bias"]
    w1[...] = WA[...].reshape(1024, 896)
    mixed = WB[:, :, 0:16, :].astype(F32)
    w2[0:128, :] = mixed[:, :, 0:8, :].reshape(128, 1024).astype(BF)
    w2[128:640, :] = WB[:, :, 16:48, :].reshape(512, 1024)
    norms, b_qkv, b_fc1, b_both = unpack_small(mixed[:, :, 8:16, 0:128].reshape(128, 128), t)
    for v in range(4):
        ln[v : v + 1, :] = norms[v]
    bias[0:1, 0:384] = b_qkv
    bias[0:1, 384:896] = b_fc1
    b_out[...] = jnp.broadcast_to(b_both, (8, 1024))
    sums = m["sums"]
    sums[...] = jnp.zeros_like(sums)

    OUT, G, NB, DALL, CAT, sib, from_y = (m[k] for k in ("OUT", "G", "NB", "DALL", "CAT", "sib", "from_y"))
    arrays = ((0, OUT, out_sum), (1, G, g_sum))
    chips = [lax.rem(y + k, 4) for k in (0, 3, 1, 2)]

    def join(a, src, at, extra=None):
        def add(r):
            v = src[mine(at), r, :].astype(F32) + sib[a, at, r, :].astype(F32)
            if extra is not None:
                v = v + from_y[a, extra, r, :].astype(F32)
            src[mine(at), r, :] = v.astype(BF)

        slabs(256, 32, add)

    for name, dst in (("x", X), ("d", DY)):
        ref = dst.at[mine(ring_y.opp)]
        msgs.plan((name, 6), ref, ref, sibling)
    for a, src, _ in arrays:
        for k in range(4):
            msgs.plan(("sib", a, k), src.at[hers(chips[k])], sib.at[a, chips[k]], sibling)
        msgs.plan(("y", a, 1), src.at[mine(ring_y.bwd)], from_y.at[a, 1], y_dev(ring_y.bwd))
        msgs.plan(("y", a, 0), src.at[mine(ring_y.opp)], from_y.at[a, 0], y_dev(ring_y.fwd))

    def before(s):
        @pl.when(s == 0)
        def _():
            for name in "xd":
                msgs.land((name, 2))

        @pl.when(s == 2)
        def _():
            for name in "xd":
                msgs.land((name, 4))
                msgs.land((name, 5))

        @pl.when(s == 5)
        def _():
            for name in "xd":
                msgs.land((name, 3))
                msgs.sent[name, 6].start()

        @pl.when(s == 6)
        def _():
            for name in "xd":
                msgs.land((name, 6))

    def after(s):
        for k in range(4):

            @pl.when(s == 2 * k)
            def _(k=k):
                for a, src, _ in arrays:
                    msgs.sent["sib", a, k].start()

        @pl.when(s == 5)
        def _():
            for a, src, _ in arrays:
                msgs.land(("sib", a, 1))
                msgs.land(("sib", a, 2))
                join(a, src, ring_y.bwd)
                msgs.sent["y", a, 1].start()

    def one_slot(s, carry):
        before(s)
        k = s // 2
        chip = jnp.where(k == 0, chips[0], jnp.where(k == 1, chips[1], jnp.where(k == 2, chips[2], chips[3])))
        slot = chip * 2 + jnp.where(s % 2 == 0, 1 - core, core)
        out, g, normed, d_all, cat, column_sums = rows_pass(
            X[slot], DY[slot], AW[slot][:, 896:1024].astype(F32)[1:3], w1, w2, ln, bias, table_ref
        )
        OUT[slot] = out.astype(BF)
        G[slot] = g.astype(BF)
        NB[slot] = normed
        DALL[slot] = d_all
        CAT[slot] = cat
        sums[0:1, 0:896] += column_sums[0]
        sums[1:2, :] += column_sums[1]
        after(s)
        return carry

    lax.fori_loop(0, 8, one_slot, 0)

    vec, vec_one, vec_sum, vec_two = (m[k] for k in ("vec", "vec_one", "vec_sum", "vec_two"))
    for i in range(8):
        vec[i : i + 1, :] = sums[i // 4 : i // 4 + 1, (i % 4) * 256 : (i % 4) * 256 + 256]
    for k, o in enumerate(x_others):
        msgs.send(("v1", k), vec, vec_one.at[k], x_dev(o))

    part = {"a": m["ga"], "b": m["gb"]}
    into_one = {"a": m["one_a"], "b": m["one_b"]}
    held_one = {"a": m["held_one_a"], "b": m["held_one_b"]}
    into_two = {"a": m["two_a"], "b": m["two_b"]}
    held_two = {"a": m["held_two_a"], "b": m["held_two_b"]}
    ha, hb = halves

    def grad_a(at):
        lanes = pl.ds(pl.multiple_of(at * 256, 256), 256)
        v = dot_tn(NB[:, :, lanes].reshape(2048, 256), DALL[...].reshape(2048, 896))
        part["a"][at] = v.reshape(4, 64, 896).astype(BF)

    def grad_b(first_at, second_at):
        cols = [
            CAT[:, :, pl.ds(pl.multiple_of(128 + at * 128, 128), 128)].reshape(2048, 128)
            for at in (first_at, second_at)
        ]
        v = dot_tn(jnp.concatenate(cols, 1), DY[...].reshape(2048, 1024))
        part["b"][first_at, :, 16:48, :] = v[0:128].reshape(4, 32, 1024).astype(BF)
        part["b"][second_at, :, 16:48, :] = v[128:256].reshape(4, 32, 1024).astype(BF)

    subs = ("opp", "bwd", "fwd", "own")

    def send_one(h, k, at, to):
        for sub in subs:
            j = getattr(h.two, sub)
            msgs.send((h.name, "one", k, sub), part[h.name].at[at, j], into_one[h.name].at[k, j], h.one_dev(to))

    def send_forward(h, sub):
        j = getattr(h.two, sub)
        msgs.land((h.name, "one", 0, sub))
        v = part[h.name][h.one.fwd, j].astype(F32) + into_one[h.name][0, j].astype(F32)
        held_one[h.name][j] = v.astype(BF)
        msgs.send((h.name, "one", 2, sub), held_one[h.name].at[j], into_one[h.name].at[2, j], h.one_dev(h.one.fwd))

    def first_sum(h, sub):
        j = getattr(h.two, sub)
        msgs.land((h.name, "one", 1, sub))
        msgs.land((h.name, "one", 2, sub))
        v = part[h.name][h.one.own, j].astype(F32) + into_one[h.name][1, j].astype(F32)
        v = v + into_one[h.name][2, j].astype(F32)
        k = subs.index(sub)
        if sub == "fwd":
            msgs.land((h.name, "two", 0))
            v = v + into_two[h.name][0].astype(F32)
        if sub != "own":
            held_two[h.name][k] = v.astype(BF)
            to = h.two.bwd if sub == "bwd" else h.two.fwd
            msgs.send((h.name, "two", k), held_two[h.name].at[k], into_two[h.name].at[k], h.two_dev(to))
            return None
        msgs.land((h.name, "two", 1))
        msgs.land((h.name, "two", 2))
        return v + into_two[h.name][1].astype(F32) + into_two[h.name][2].astype(F32)

    grad_a(ring_x.opp)
    send_one(ha, 0, ring_x.opp, ring_x.fwd)

    for a, src, _ in arrays:
        msgs.land(("sib", a, 3))
        join(a, src, ring_y.opp)
        msgs.sent["y", a, 0].start()

    grad_a(ring_x.bwd)
    send_one(ha, 1, ring_x.bwd, ring_x.bwd)
    v = dot_tn(CAT[:, :, 0:128].reshape(2048, 128), DY[...].reshape(2048, 1024)).reshape(4, 4, 8, 1024)
    part["b"][:, :, 0:16, :] = jnp.concatenate([v, jnp.zeros_like(v)], 2).astype(BF)
    grad_b(ring_z.opp, ring_z.bwd)
    send_one(hb, 0, ring_z.opp, ring_z.fwd)
    send_one(hb, 1, ring_z.bwd, ring_z.bwd)
    grad_a(ring_x.fwd)
    for sub in subs:
        send_forward(ha, sub)
    grad_b(ring_z.fwd, ring_z.own)
    for sub in subs:
        send_forward(hb, sub)

    for a, src, _ in arrays:
        msgs.land(("y", a, 0))
        join(a, src, ring_y.fwd, extra=0)
        msgs.send(("y", a, 2), src.at[mine(ring_y.fwd)], from_y.at[a, 2], y_dev(ring_y.fwd))
    grad_a(ring_x.own)

    for k in range(3):
        msgs.land(("v1", k))
    vec_sum[...] = vec[...] + vec_one[0] + vec_one[1] + vec_one[2]
    for k, o in enumerate(z_others):
        msgs.send(("v2", k), vec_sum, vec_two.at[k], z_dev(o))

    for sub in ("opp", "bwd"):
        for h in halves:
            first_sum(h, sub)

    for k in range(3):
        msgs.land(("v2", k))
    vec_all[t] = vec_sum[...] + vec_two[0] + vec_two[1] + vec_two[2]
    for k, o in enumerate(others):
        msgs.send(("v3", k), vec_all.at[t], vec_all.at[t], group_member(x, z, o))

    for h in halves:
        first_sum(h, "fwd")

    v = first_sum(hb, "own")
    m["own_dense"][...] = v[0:8]
    grad_fc2[...] = v[16:48]

    @pl.when(moves)
    def _():
        msgs.sent["back"].start()

    @pl.when(jnp.logical_not(moves))
    def _():
        grad_dense[...] = m["own_dense"][...]

    fin_a = m["fin_a"]
    fin_a[...] = first_sum(ha, "own").reshape(8, 8, 896)
    for k, o in enumerate(others):
        msgs.send(("n", k), fin_a.at[o], n_all.at[t], group_member(x, z, o))
    n_all[t] = fin_a[t]

    for a, src, dst in arrays:
        msgs.land(("sib", a, 0))
        msgs.land(("y", a, 1))
        msgs.land(("y", a, 2))

        def add(r, a=a, src=src, dst=dst):
            v = src[mine(y), r, :].astype(F32) + sib[a, y, r, :].astype(F32)
            dst[r, :] = v + from_y[a, 1, r, :].astype(F32) + from_y[a, 2, r, :].astype(F32)

        slabs(256, 32, add)

    @pl.when(moves)
    def _():
        msgs.sent["there"].wait_send()
        msgs.sent["back"].wait()

    msgs.finish()


def whole(*args):
    vmem = pl.BlockSpec(memory_space=pltpu.VMEM)
    hbm = pl.BlockSpec(memory_space=pl.ANY)
    return pl.pallas_call(
        whole_kernel,
        out_shape=(
            jax.ShapeDtypeStruct((256, 1024), F32),
            jax.ShapeDtypeStruct((256, 1024), F32),
            jax.ShapeDtypeStruct((8, 8, 896), F32),
            jax.ShapeDtypeStruct((8, 1024), F32),
            jax.ShapeDtypeStruct((32, 1024), F32),
            jax.ShapeDtypeStruct((8, 8, 256), F32),
            jax.ShapeDtypeStruct((8, 1024), F32),
        ),
        in_specs=[hbm] * len(args),
        out_specs=(vmem,) * 7,
        scratch_shapes=[pltpu.VMEM(*spec) for spec in SCRATCH.values()]
        + [pltpu.SemaphoreType.DMA((MESSAGES,)), pltpu.SemaphoreType.DMA((MESSAGES,)), pltpu.SemaphoreType.DMA((8,))],
        compiler_params=pltpu.CompilerParams(
            collective_id=0, has_side_effects=True, vmem_limit_bytes=VMEM_LIMIT
        ),
        cost_estimate=pl.CostEstimate(flops=20_000_000_000, bytes_accessed=5_000_000, transcendentals=3_000_000),
        name="whole_block",
    )(*args)


def finish_kernel(*refs):
    given, results, held, sems = refs[:12], refs[12:26], refs[26:38], refs[38]
    copies = [pltpu.make_async_copy(src, dst, sems.at[n]) for n, (src, dst) in enumerate(zip(given, held))]
    for copy in copies:
        copy.start()
    x_ref, dy_ref, out_sum, g_sum, n_all, dense_in, fc2_in, vec_all, b_out, small_ref, wqkv_ref, wfc1_ref = held
    (out_ref, dx_ref, g1_gain, g1_bias, g2_gain, g2_bias, grad_qkv, grad_b_qkv,
     grad_dense, grad_b_out, grad_fc1, grad_b_fc1, grad_fc2, grad_b_last) = results
    me = lax.axis_index("fsdp")
    for n in (0, 2, 8, 9):
        copies[n].wait()
    small = small_ref[...].astype(F32)
    lives = [jnp.broadcast_to(small[b : b + 1, :], (128, 128)).T[:, 0:1] >= 0.0 for b in (1, 2)]
    live = jnp.concatenate([u.astype(F32) for u in lives], 0)
    x = x_ref[...].astype(F32)
    out_ref[...] = (x + live * (out_sum[...] + b_out[0:1, :])).astype(BF)
    centre = x - jnp.mean(x, 1, keepdims=True)
    scale = lax.rsqrt(jnp.mean(centre * centre, 1, keepdims=True) + NORM_EPS)
    normed = centre * scale
    for n in (1, 3):
        copies[n].wait()
    g = g_sum[...]
    dx = (g - jnp.mean(g, 1, keepdims=True) - normed * jnp.mean(g * normed, 1, keepdims=True)) * scale
    dx_ref[...] = (dy_ref[...].astype(F32) + dx).astype(BF)

    row = lax.broadcasted_iota(jnp.int32, (8, 128), 0)
    lane = lax.broadcasted_iota(jnp.int32, (8, 128), 1)

    def column(start):
        return jnp.sum(jnp.where(lane == row + start, small[0:1, :], 0.0), 1, keepdims=True)

    def as_lanes(u):
        return jnp.sum(jnp.where(lane == row, u, 0.0), 0, keepdims=True)

    def write(ref, u, count):
        ref[...] = u[0:1, 0:count]

    def shifted(u, by):
        width = u.shape[1]
        return pltpu.roll(jnp.broadcast_to(u, (8, width)), lax.rem(width - by, width), 1)

    for n in (4, 5, 6, 7, 10, 11):
        copies[n].wait()
    n_qkv = jnp.concatenate([n_all[t, :, c * 128 : c * 128 + 128] for c in range(3) for t in range(8)], 1)
    at = ((0, 0), (0, 128), (1, 0))
    s_qkv = jnp.concatenate([vec_all[t, r : r + 1, lo : lo + 128] for r, lo in at for t in range(8)], 1)
    both = []
    for t in range(8):
        sums = jnp.concatenate([vec_all[t, 1:2, 128:256], vec_all[t, 2:3, :], vec_all[t, 3:4, 0:128]], 1)
        both.append(jnp.concatenate([n_all[t, :, 384:896], jnp.broadcast_to(sums, (8, 512))], 0))
    fc1 = jnp.concatenate(
        [both[t][:, (q * 4 + p) * 32 : (q * 4 + p) * 32 + 32] for p in range(4) for q in range(4) for t in range(8)], 1
    )

    def norm_grads(weight, n, s, start, gain_ref, bias_ref, grad_ref):
        weight = weight.astype(F32)
        grad_ref[...] = column(start) * n + column(start + 8) * s
        write(gain_ref, as_lanes(jnp.sum(weight * n, 1, keepdims=True)), 8)
        write(bias_ref, as_lanes(jnp.sum(weight * s, 1, keepdims=True)), 8)

    s_fc1 = fc1[8:9]
    norm_grads(wqkv_ref[...], n_qkv, s_qkv, 0, g1_gain, g1_bias, grad_qkv)
    norm_grads(wfc1_ref[...], fc1[0:8], s_fc1, 16, g2_gain, g2_bias, grad_fc1)
    write(grad_b_qkv, shifted(s_qkv, me * 24), 24)
    write(grad_b_fc1, shifted(s_fc1, me * 32), 32)
    branch = jnp.concatenate([vec_all[0, r : r + 1, :] for r in range(4, 8)], 1)
    branch = shifted(branch, me * 8)
    write(grad_b_out, branch, 8)
    write(grad_b_last, branch, 8)
    grad_dense[...] = dense_in[...]
    grad_fc2[...] = fc2_in[...]


def finish(*args):
    flat = lambda count: jax.ShapeDtypeStruct((1, count), F32)
    full = lambda *shape: jax.ShapeDtypeStruct(shape, F32)
    rows = jax.ShapeDtypeStruct((256, 1024), BF)
    outs = pl.pallas_call(
        finish_kernel,
        out_shape=(rows, rows, flat(8), flat(8), flat(8), flat(8), full(8, 3072), flat(24), full(8, 1024), flat(8),
                   full(8, 4096), flat(32), full(32, 1024), flat(8)),
        in_specs=[pl.BlockSpec(memory_space=pl.ANY)] * len(args),
        scratch_shapes=[pltpu.VMEM(u.shape, u.dtype) for u in args] + [pltpu.SemaphoreType.DMA((len(args),))],
        compiler_params=pltpu.CompilerParams(vmem_limit_bytes=VMEM_LIMIT),
        cost_estimate=pl.CostEstimate(flops=20_000_000, bytes_accessed=6_000_000, transcendentals=0),
        name="finish",
    )(*args)
    return tuple(u.reshape(-1) if u.shape[0] == 1 else u for u in outs)


def body(tokens, segments, grad_out, ln1_gain, ln1_bias, ln2_gain, ln2_bias, w_qkv, b_qkv,
         w_dense, b_dense, w_fc1, b_fc1, w_fc2, b_fc2):
    small = jnp.pad(segments.astype(BF), ((1, 5), (0, 0)))
    at = 0
    for vector in (ln1_gain, ln1_bias, ln2_gain, ln2_bias, b_qkv, b_fc1, b_dense, b_fc2):
        small = small + jnp.pad(vector[None], ((0, 7), (at, 128 - at - vector.shape[0])))
        at += vector.shape[0]
    out_sum, g_sum, n_all, grad_dense, grad_fc2, sums, b_out = whole(
        tokens, grad_out, w_qkv, w_fc1, w_dense, w_fc2, small, jnp.asarray(rotary_table())
    )

    return finish(
        tokens, grad_out, out_sum, g_sum, n_all, grad_dense, grad_fc2, sums, b_out, small, w_qkv, w_fc1
    )


def solution(mesh):
    rows, flat = P("fsdp", None), P("fsdp")
    return jax.shard_map(
        body,
        mesh=mesh,
        in_specs=(rows, rows, rows, flat, flat, flat, flat, rows, flat, rows, flat, rows, flat, rows, flat),
        out_specs=(rows, rows, flat, flat, flat, flat, rows, flat, rows, flat, rows, flat, rows, flat),
        check_vma=False,
    )
```

```python
import functools
import math

import jax
import jax.numpy as jnp
import numpy as np
from jax import lax
from jax.experimental import pallas as pl
from jax.experimental.pallas import tpu as pltpu
from jax.sharding import PartitionSpec as P

NORM_EPS = 1e-05
MASKED = -1e30
MESH = pl.DeviceIdType.MESH
BF = jnp.bfloat16
F32 = jnp.float32
VMEM_LIMIT = 60 * 1024 * 1024


def coords():
    i = lax.axis_index("fsdp")
    core = lax.rem(i, 2)
    y = lax.rem(i // 2, 4)
    z = lax.rem(i // 8, 4)
    x = i // 32
    return x, z, y, core


def ident(x, z, y, core):
    return ((x * 4 + z) * 4 + y) * 2 + core


class Ring:
    def __init__(self, at, core):
        step = 1 + 2 * core
        self.own = at
        self.fwd = lax.rem(at + step, 4)
        self.bwd = lax.rem(at + 4 - step, 4)
        self.opp = lax.rem(at + 2, 4)


class Messages:
    def __init__(self, send_sem, recv_sem):
        self.send_sem, self.recv_sem = send_sem, recv_sem
        self.sent, self.landed, self.apart = {}, set(), set()

    def plan(self, name, src, dst, target, apart=False):
        n = len(self.sent)
        copy = pltpu.make_async_remote_copy(
            src_ref=src,
            dst_ref=dst,
            send_sem=self.send_sem.at[n],
            recv_sem=self.recv_sem.at[n],
            device_id=(target,),
            device_id_type=MESH,
        )
        self.sent[name] = copy
        if apart:
            self.apart.add(name)

    def send(self, name, src, dst, target):
        self.plan(name, src, dst, target)
        self.sent[name].start()

    def land(self, name):
        assert name not in self.landed
        self.landed.add(name)
        self.sent[name].wait_recv()

    def finish(self):
        for name, copy in self.sent.items():
            if name not in self.landed and name not in self.apart:
                copy.wait_recv()
        for name, copy in self.sent.items():
            if name not in self.apart:
                copy.wait_send()


def group_member(x, z, t):
    return ident(x, z, 0, 0) + t


def dot(a, b):
    return jnp.dot(a, b, preferred_element_type=F32)


def dot_nt(a, b):
    return lax.dot_general(a, b, (((1,), (1,)), ((), ())), preferred_element_type=F32)


def dot_tn(a, b):
    return lax.dot_general(a, b, (((0,), (0,)), ((), ())), preferred_element_type=F32)


def turn(u, cosine, sine, low_lanes):
    moved = jnp.where(low_lanes, pltpu.roll(u, 120, 1), pltpu.roll(u, 8, 1))
    return u * cosine + moved * sine


def rotary_table():
    m = 8
    angle = np.arange(128, dtype=np.float64)[:, None] * (10000.0 ** (-2.0 * np.arange(m) / 16.0))[None, :]
    cosine = np.ones((128, 128), np.float32)
    sine = np.zeros((128, 128), np.float32)
    for head in (0, 64):
        cosine[:, head : head + m] = np.cos(angle)
        cosine[:, head + m : head + 2 * m] = np.cos(angle)
        sine[:, head : head + m] = -np.sin(angle)
        sine[:, head + m : head + 2 * m] = np.sin(angle)
    parts = []
    for table in (cosine, sine):
        high = table.astype(jnp.bfloat16)
        parts += [high, (table - high.astype(np.float32)).astype(jnp.bfloat16)]
    return np.concatenate(parts, 1)


def slabs(rows, step, fn):
    def one(i, carry):
        fn(pl.ds(pl.multiple_of(i * step, step), step))
        return carry

    lax.fori_loop(0, rows // step, one, 0)


class Half:
    def __init__(self, name, one, one_dev, two, two_dev, rows):
        self.name, self.one, self.one_dev, self.two, self.two_dev, self.rows = name, one, one_dev, two, two_dev, rows


def unpack_small(packed, t):
    packed = packed.astype(BF)

    def pick(lanes, columns, owner):
        j = lax.broadcasted_iota(jnp.int32, (128, lanes), 0)
        at = lax.broadcasted_iota(jnp.int32, (128, lanes), 1)
        of_row = ((j >> 3) & 3) * 32 + (j >> 5) * 8 + (j & 7)
        select = jnp.zeros((128, lanes), F32)
        for column in columns(at):
            select = select + (j == column).astype(F32)
        rows = dot(packed, select.astype(BF))
        return jnp.sum(jnp.where(of_row == owner(at), rows, 0.0), 0, keepdims=True)

    eight = lambda *starts: pick(1024, lambda at: [s + (at & 7) for s in starts], lambda at: at >> 3)
    ln = [eight(8 * v) for v in range(4)]
    b_out = eight(88, 96)
    qkv_at = lambda at: (at >> 7) * 1024 + t * 128 + (at & 127)
    d24 = lambda c: (c * 2731) >> 16
    b_qkv = pick(384, lambda at: [32 + qkv_at(at) - 24 * d24(qkv_at(at))], lambda at: d24(qkv_at(at)))
    b_fc1 = pick(512, lambda at: [56 + (at & 31)], lambda at: ((at >> 5) & 3) * 32 + (at >> 7) * 8 + t)
    return ln, b_qkv, b_fc1, b_out


def rows_pass(x, dy, seg, w1_ref, w2_ref, ln_ref, bias_ref, table_ref):
    x = x.astype(F32)
    centre = x - jnp.mean(x, 1, keepdims=True)
    spread = jnp.mean(centre * centre, 1, keepdims=True)
    normed = centre * lax.rsqrt(spread + NORM_EPS)
    g1, g2 = ln_ref[0:1, :], ln_ref[2:3, :]
    a1 = (normed * g1 + ln_ref[1:2, :]).astype(BF)
    a2 = (normed * g2 + ln_ref[3:4, :]).astype(BF)
    joined = dot(a1, w1_ref[:, 0:384]) + bias_ref[0:1, 0:384]

    row = lax.broadcasted_iota(jnp.int32, (128, 128), 0)
    col = lax.broadcasted_iota(jnp.int32, (128, 128), 1)
    low_lanes = (col & 63) < 8
    head0 = col < 64
    ones = jnp.ones((128, 128), BF)
    blocks = range(2)
    parts = [slice(b * 128, b * 128 + 128) for b in blocks]

    def stacked(u):
        zero = jnp.zeros_like(u)
        return jnp.concatenate([jnp.where(head0, u, zero), jnp.where(head0, zero, u)], 0)

    def folded(u):
        return jnp.where(head0, u[0:128], u[128:256])

    masks, lives, tables = [], [], []
    for b in blocks:
        seg_c = jnp.broadcast_to(seg[b : b + 1, :], (128, 128))
        seg_r = seg_c.T
        allowed = (seg_c == seg_r) & (col <= row)
        position = jnp.sum(allowed.astype(F32), 1, keepdims=True) - 1.0
        onehot = (col == position.astype(jnp.int32)).astype(BF)
        tables.append(dot(onehot, table_ref[...]))
        masks.append(jnp.concatenate([allowed, allowed], 0))
        lives.append((seg_r[:, 0:1] >= 0.0).astype(F32))
    live = jnp.concatenate(lives, 0)
    cosine = [u[:, 0:128] + u[:, 128:256] for u in tables]
    sine = [u[:, 256:384] + u[:, 384:512] for u in tables]
    q = [turn(joined[parts[b], 0:128], cosine[b], sine[b], low_lanes).astype(BF) for b in blocks]
    k = [turn(joined[parts[b], 128:256], cosine[b], sine[b], low_lanes).astype(BF) for b in blocks]
    v = [joined[parts[b], 256:384].astype(BF) for b in blocks]
    q2 = [stacked(u) for u in q]
    scores = [jnp.where(masks[b], dot_nt(q2[b], k[b]) * 0.125, MASKED) for b in blocks]
    d_cat = dot_nt(dy, w2_ref[...]) * live
    e = [jnp.exp(u - jnp.max(u, 1, keepdims=True)) for u in scores]
    hidden = dot(a2, w1_ref[:, 384:896]) + bias_ref[0:1, 384:896]
    weighted = [dot(e[b].astype(BF), jnp.concatenate([v[b], ones], 1)) for b in blocks]
    d_context = d_cat[:, 0:128].astype(BF)
    dc2 = [stacked(d_context[p]) for p in parts]
    d_probs = [dot_nt(dc2[b], v[b]) for b in blocks]
    inverse = [1.0 / u[:, 128:256] for u in weighted]
    probs = [e[b] * inverse[b] for b in blocks]
    along = [jnp.sum(probs[b] * d_probs[b], 1, keepdims=True) for b in blocks]
    phi_cdf = 0.5 + 0.5 * lax.erf(hidden * math.sqrt(0.5))
    active = ((hidden * phi_cdf).astype(BF).astype(F32) * live).astype(BF)
    slope = phi_cdf + hidden * (jnp.exp(hidden * hidden * -0.5) * (1.0 / math.sqrt(2.0 * math.pi)))
    d_hidden = d_cat[:, 128:640] * slope
    d_scores = [(probs[b] * (d_probs[b] - along[b])).astype(BF) for b in blocks]
    contexts = [
        (folded(weighted[b][:, 0:128] * inverse[b]).astype(BF).astype(F32) * lives[b]).astype(BF) for b in blocks
    ]
    d_v = [dot_tn(probs[b].astype(BF), dc2[b]) for b in blocks]
    d_q = [folded(dot(d_scores[b], k[b]) * 0.125) for b in blocks]
    d_k = [dot_tn(d_scores[b], q2[b]) * 0.125 for b in blocks]
    d_joined = [
        jnp.concatenate(
            [turn(d_q[b], cosine[b], -sine[b], low_lanes), turn(d_k[b], cosine[b], -sine[b], low_lanes), d_v[b]], 1
        )
        for b in blocks
    ]
    cat = jnp.concatenate([jnp.concatenate(contexts, 0), active], 1)
    out = dot(cat, w2_ref[...])
    d_all = jnp.concatenate([jnp.concatenate(d_joined, 0), d_hidden], 1)
    column_sums = jnp.sum(d_all, 0, keepdims=True), jnp.sum(dy.astype(F32) * live, 0, keepdims=True)
    d_all_b = d_all.astype(BF)
    g = g1 * dot_nt(d_all_b[:, 0:384], w1_ref[:, 0:384]) + g2 * dot_nt(d_all_b[:, 384:896], w1_ref[:, 384:896])
    return out, g, normed.astype(BF), d_all_b, cat, column_sums


SCRATCH = dict(
    X=((8, 256, 1024), BF),
    DY=((8, 256, 1024), BF),
    qkv=((8, 3072), BF),
    fc1=((8, 4096), BF),
    small=((8, 128), BF),
    table=((128, 512), BF),
    dense=((8, 1024), BF),
    fc2=((32, 1024), BF),
    stage=((8, 8, 1024), BF),
    AW=((8, 8, 1024), BF),
    WA=((4, 4, 64, 896), BF),
    WB=((4, 4, 48, 1024), BF),
    w1=((1024, 896), BF),
    w2=((640, 1024), BF),
    ln=((8, 1024), F32),
    bias=((8, 896), F32),
    OUT=((8, 256, 1024), BF),
    G=((8, 256, 1024), BF),
    NB=((8, 256, 1024), BF),
    DALL=((8, 256, 896), BF),
    CAT=((8, 256, 640), BF),
    sums=((8, 1024), F32),
    sib=((2, 4, 256, 1024), BF),
    from_y=((2, 3, 256, 1024), BF),
    ga=((4, 4, 64, 896), BF),
    gb=((4, 4, 48, 1024), BF),
    one_a=((3, 4, 64, 896), BF),
    one_b=((3, 4, 48, 1024), BF),
    held_one_a=((4, 64, 896), BF),
    held_one_b=((4, 48, 1024), BF),
    two_a=((3, 64, 896), BF),
    two_b=((3, 48, 1024), BF),
    held_two_a=((3, 64, 896), BF),
    held_two_b=((3, 48, 1024), BF),
    fin_a=((8, 8, 896), F32),
    own_dense=((8, 1024), F32),
    vec=((8, 256), F32),
    vec_one=((3, 8, 256), F32),
    vec_sum=((8, 256), F32),
    vec_two=((3, 8, 256), F32),
)
MESSAGES = 7 + 1 + 2 * 7 + 2 * (3 + 12) + 13 + 2 * (4 + 3) + 2 * (12 + 3) + 7 + 1


def whole_kernel(x_ref, dy_ref, wqkv_ref, wfc1_ref, dense_ref, fc2_ref, small_ref, table_hbm,
                 out_sum, g_sum, n_all, grad_dense, grad_fc2, vec_all, b_out, *scratch):
    m = dict(zip(SCRATCH, scratch))
    send_sem, recv_sem, local_sem = scratch[len(SCRATCH) :]
    X, DY, AW, WA, WB, stage, table_ref = (m[k] for k in ("X", "DY", "AW", "WA", "WB", "stage", "table"))
    x, z, y, core = coords()
    t = y * 2 + core
    ring_y, ring_x, ring_z = Ring(y, core), Ring(x, core), Ring(z, core)
    y_dev = lambda to: ident(x, z, to, core)
    x_dev = lambda to: ident(to, z, y, core)
    z_dev = lambda to: ident(x, to, y, core)
    sibling = ident(x, z, y, 1 - core)
    others = [lax.rem(t + k, 8) for k in range(1, 8)]
    x_others = [lax.rem(x + k, 4) for k in range(1, 4)]
    z_others = [lax.rem(z + k, 4) for k in range(1, 4)]
    mine = lambda at: at * 2 + core
    hers = lambda at: at * 2 + 1 - core
    halves = (
        Half("a", ring_x, x_dev, ring_z, z_dev, 64),
        Half("b", ring_z, z_dev, ring_x, x_dev, 48),
    )
    owner = t * 16 + z * 4 + x
    me = ident(x, z, y, core)
    spreader = ident(lax.rem(me, 4), lax.rem(me // 4, 4), 0, 0) + me // 16
    moves = spreader != me

    local = [
        pltpu.make_async_copy(src, dst, local_sem.at[n])
        for n, (src, dst) in enumerate(
            (
                (wqkv_ref, m["qkv"]),
                (wfc1_ref, m["fc1"]),
                (small_ref, m["small"]),
                (fc2_ref, m["fc2"]),
                (table_hbm, table_ref),
                (x_ref, X.at[t]),
                (dy_ref, DY.at[t]),
            )
        )
    ]
    for copy in local:
        copy.start()
    barrier = pltpu.get_barrier_semaphore()
    near = [group_member(x, z, o) for o in others] + [x_dev(o) for o in x_others] + [z_dev(o) for o in z_others]
    for target in near:
        pl.semaphore_signal(barrier, inc=1, device_id=(target,), device_id_type=MESH)

    @pl.when(moves)
    def _():
        for target in (owner, spreader):
            pl.semaphore_signal(barrier, inc=1, device_id=(target,), device_id_type=MESH)

    for copy in local[:4]:
        copy.wait()
    fc1_rows = m["fc1"][...].astype(F32)
    for o in range(8):
        for sec in range(3):
            stage[o, :, sec * 128 : sec * 128 + 128] = m["qkv"][:, sec * 1024 + o * 128 : sec * 1024 + o * 128 + 128]
        columns = [fc1_rows[:, at : at + 32] for at in [p * 1024 + q * 256 + o * 32 for q in range(4) for p in range(4)]]
        stage[o, :, 384:896] = jnp.concatenate(columns, 1).astype(BF)
        stage[o, :, 896:1024] = m["small"][...]

    @pl.when(moves)
    def _():
        pl.semaphore_wait(barrier, len(near) + 2)

    @pl.when(jnp.logical_not(moves))
    def _():
        pl.semaphore_wait(barrier, len(near))

    msgs = Messages(send_sem, recv_sem)

    for k, o in enumerate(others):
        msgs.send(("w", k), stage.at[o], AW.at[t], group_member(x, z, o))
    lone = pltpu.make_async_copy(dense_ref, m["dense"], local_sem.at[7])
    msgs.plan("there", dense_ref, m["dense"], spreader, apart=True)
    msgs.plan("back", m["own_dense"], grad_dense, owner, apart=True)

    @pl.when(moves)
    def _():
        msgs.sent["there"].start()

    @pl.when(jnp.logical_not(moves))
    def _():
        lone.start()

    def own_rows(name, src, dst):
        msgs.send((name, 0), src, dst.at[t], y_dev(ring_y.fwd))
        msgs.send((name, 1), src, dst.at[t], y_dev(ring_y.bwd))
        msgs.send((name, 2), src, dst.at[t], sibling)

    own_rows("x", x_ref, X)
    own_rows("d", dy_ref, DY)
    AW[t] = stage[t]
    for k in range(7):
        msgs.land(("w", k))
    for pair in range(4):
        both = jnp.concatenate([AW[2 * pair].astype(F32), AW[2 * pair + 1].astype(F32)], 0)
        WA[x, z, 16 * pair : 16 * pair + 16, :] = both[:, 0:896].astype(BF)

    @pl.when(moves)
    def _():
        msgs.sent["there"].wait_recv()

    @pl.when(jnp.logical_not(moves))
    def _():
        lone.wait()

    member = lax.broadcasted_iota(jnp.int32, (8, 128), 0)
    small = jnp.zeros((8, 128), F32)
    for k in range(8):
        small = jnp.where(member == k, AW[k, :, 896:1024].astype(F32)[0:1], small)
    small = jnp.concatenate([small, jnp.zeros((8, 896), F32)], 1)
    WB[z, x, 0:16, :] = jnp.concatenate([m["dense"][...].astype(F32), small], 0).astype(BF)
    WB[z, x, 16:48, :] = m["fc2"][...]

    gathered = {"a": WA, "b": WB}

    def first(h, k, at, to):
        ref = gathered[h.name].at[at, h.two.own]
        msgs.send((h.name, "p", k), ref, ref, h.one_dev(to))

    def second(h, sub, k, at, frm, to):
        ref = gathered[h.name].at[at, frm]
        msgs.send((h.name, sub, k), ref, ref, h.two_dev(to))

    def spread(h, sub):
        at = getattr(h.one, sub)
        second(h, sub, 0, at, h.two.own, h.two.fwd)
        second(h, sub, 1, at, h.two.own, h.two.bwd)

    def pass_on(h, sub):
        msgs.land((h.name, sub, 0))
        second(h, sub, 2, getattr(h.one, sub), h.two.bwd, h.two.fwd)

    for h in halves:
        first(h, 0, h.one.own, h.one.fwd)
        first(h, 1, h.one.own, h.one.bwd)
        spread(h, "own")
    for h in halves:
        msgs.land((h.name, "p", 0))
        first(h, 2, h.one.bwd, h.one.fwd)
        spread(h, "bwd")
    for h in halves:
        msgs.land((h.name, "p", 1))
        spread(h, "fwd")
    for h in halves:
        msgs.land((h.name, "p", 2))
        spread(h, "opp")
    for h in halves:
        pass_on(h, "own")

    def rows_on(name, dst):
        msgs.land((name, 0))
        ref = dst.at[mine(ring_y.bwd)]
        msgs.send((name, 4), ref, ref, sibling)
        msgs.land((name, 1))
        ref = dst.at[mine(ring_y.fwd)]
        msgs.send((name, 5), ref, ref, sibling)

    def rows_far(name, dst):
        ref = dst.at[mine(ring_y.bwd)]
        msgs.send((name, 3), ref, ref, y_dev(ring_y.fwd))

    for sub in ("bwd", "fwd", "opp"):
        for h in halves:
            pass_on(h, sub)
    rows_on("x", X)
    rows_far("x", X)
    rows_on("d", DY)
    rows_far("d", DY)
    for h in halves:
        for sub in ("own", "bwd", "fwd", "opp"):
            msgs.land((h.name, sub, 1))
            msgs.land((h.name, sub, 2))
    for copy in local[4:]:
        copy.wait()

    w1, w2, ln, bias = m["w1"], m["w2"], m["ln"], m["bias"]
    w1[...] = WA[...].reshape(1024, 896)
    mixed = WB[:, :, 0:16, :].astype(F32)
    w2[0:128, :] = mixed[:, :, 0:8, :].reshape(128, 1024).astype(BF)
    w2[128:640, :] = WB[:, :, 16:48, :].reshape(512, 1024)
    norms, b_qkv, b_fc1, b_both = unpack_small(mixed[:, :, 8:16, 0:128].reshape(128, 128), t)
    for v in range(4):
        ln[v : v + 1, :] = norms[v]
    bias[0:1, 0:384] = b_qkv
    bias[0:1, 384:896] = b_fc1
    b_out[...] = jnp.broadcast_to(b_both, (8, 1024))
    sums = m["sums"]
    sums[...] = jnp.zeros_like(sums)

    OUT, G, NB, DALL, CAT, sib, from_y = (m[k] for k in ("OUT", "G", "NB", "DALL", "CAT", "sib", "from_y"))
    arrays = ((0, OUT, out_sum), (1, G, g_sum))
    chips = [lax.rem(y + k, 4) for k in (0, 3, 1, 2)]

    def join(a, src, at, extra=None):
        def add(r):
            v = src[mine(at), r, :].astype(F32) + sib[a, at, r, :].astype(F32)
            if extra is not None:
                v = v + from_y[a, extra, r, :].astype(F32)
            src[mine(at), r, :] = v.astype(BF)

        slabs(256, 32, add)

    for name, dst in (("x", X), ("d", DY)):
        ref = dst.at[mine(ring_y.opp)]
        msgs.plan((name, 6), ref, ref, sibling)
    for a, src, _ in arrays:
        for k in range(4):
            msgs.plan(("sib", a, k), src.at[hers(chips[k])], sib.at[a, chips[k]], sibling)
        msgs.plan(("y", a, 1), src.at[mine(ring_y.bwd)], from_y.at[a, 1], y_dev(ring_y.bwd))
        msgs.plan(("y", a, 0), src.at[mine(ring_y.opp)], from_y.at[a, 0], y_dev(ring_y.fwd))

    def before(s):
        @pl.when(s == 0)
        def _():
            for name in "xd":
                msgs.land((name, 2))

        @pl.when(s == 2)
        def _():
            for name in "xd":
                msgs.land((name, 4))
                msgs.land((name, 5))

        @pl.when(s == 4)
        def _():
            for name in "xd":
                msgs.land((name, 3))
                msgs.sent[name, 6].start()

        @pl.when(s == 6)
        def _():
            for name in "xd":
                msgs.land((name, 6))

    def after(s):
        for k in range(4):

            @pl.when(s == 2 * k)
            def _(k=k):
                for a, src, _ in arrays:
                    msgs.sent["sib", a, k].start()

        @pl.when(s == 5)
        def _():
            for a, src, _ in arrays:
                msgs.land(("sib", a, 1))
                msgs.land(("sib", a, 2))
                join(a, src, ring_y.bwd)
                msgs.sent["y", a, 1].start()

    def one_slot(s, carry):
        before(s)
        k = s // 2
        chip = jnp.where(k == 0, chips[0], jnp.where(k == 1, chips[1], jnp.where(k == 2, chips[2], chips[3])))
        slot = chip * 2 + jnp.where(s % 2 == 0, 1 - core, core)
        out, g, normed, d_all, cat, column_sums = rows_pass(
            X[slot], DY[slot], AW[slot][:, 896:1024].astype(F32)[1:3], w1, w2, ln, bias, table_ref
        )
        OUT[slot] = out.astype(BF)
        G[slot] = g.astype(BF)
        NB[slot] = normed
        DALL[slot] = d_all
        CAT[slot] = cat
        sums[0:1, 0:896] += column_sums[0]
        sums[1:2, :] += column_sums[1]
        after(s)
        return carry

    lax.fori_loop(0, 8, one_slot, 0)

    vec, vec_one, vec_sum, vec_two = (m[k] for k in ("vec", "vec_one", "vec_sum", "vec_two"))
    for i in range(8):
        vec[i : i + 1, :] = sums[i // 4 : i // 4 + 1, (i % 4) * 256 : (i % 4) * 256 + 256]
    for k, o in enumerate(x_others):
        msgs.send(("v1", k), vec, vec_one.at[k], x_dev(o))

    part = {"a": m["ga"], "b": m["gb"]}
    into_one = {"a": m["one_a"], "b": m["one_b"]}
    held_one = {"a": m["held_one_a"], "b": m["held_one_b"]}
    into_two = {"a": m["two_a"], "b": m["two_b"]}
    held_two = {"a": m["held_two_a"], "b": m["held_two_b"]}
    ha, hb = halves

    def grad_a(at):
        lanes = pl.ds(pl.multiple_of(at * 256, 256), 256)
        v = dot_tn(NB[:, :, lanes].reshape(2048, 256), DALL[...].reshape(2048, 896))
        part["a"][at] = v.reshape(4, 64, 896).astype(BF)

    def grad_b(first_at, second_at):
        cols = [
            CAT[:, :, pl.ds(pl.multiple_of(128 + at * 128, 128), 128)].reshape(2048, 128)
            for at in (first_at, second_at)
        ]
        v = dot_tn(jnp.concatenate(cols, 1), DY[...].reshape(2048, 1024))
        part["b"][first_at, :, 16:48, :] = v[0:128].reshape(4, 32, 1024).astype(BF)
        part["b"][second_at, :, 16:48, :] = v[128:256].reshape(4, 32, 1024).astype(BF)

    subs = ("opp", "bwd", "fwd", "own")

    def send_one(h, k, at, to):
        for sub in subs:
            j = getattr(h.two, sub)
            msgs.send((h.name, "one", k, sub), part[h.name].at[at, j], into_one[h.name].at[k, j], h.one_dev(to))

    def send_forward(h, sub):
        j = getattr(h.two, sub)
        msgs.land((h.name, "one", 0, sub))
        v = part[h.name][h.one.fwd, j].astype(F32) + into_one[h.name][0, j].astype(F32)
        held_one[h.name][j] = v.astype(BF)
        msgs.send((h.name, "one", 2, sub), held_one[h.name].at[j], into_one[h.name].at[2, j], h.one_dev(h.one.fwd))

    def first_sum(h, sub):
        j = getattr(h.two, sub)
        msgs.land((h.name, "one", 1, sub))
        msgs.land((h.name, "one", 2, sub))
        v = part[h.name][h.one.own, j].astype(F32) + into_one[h.name][1, j].astype(F32)
        v = v + into_one[h.name][2, j].astype(F32)
        k = subs.index(sub)
        if sub == "fwd":
            msgs.land((h.name, "two", 0))
            v = v + into_two[h.name][0].astype(F32)
        if sub != "own":
            held_two[h.name][k] = v.astype(BF)
            to = h.two.bwd if sub == "bwd" else h.two.fwd
            msgs.send((h.name, "two", k), held_two[h.name].at[k], into_two[h.name].at[k], h.two_dev(to))
            return None
        msgs.land((h.name, "two", 1))
        msgs.land((h.name, "two", 2))
        return v + into_two[h.name][1].astype(F32) + into_two[h.name][2].astype(F32)

    grad_a(ring_x.opp)
    send_one(ha, 0, ring_x.opp, ring_x.fwd)

    for a, src, _ in arrays:
        msgs.land(("sib", a, 3))
        join(a, src, ring_y.opp)
        msgs.sent["y", a, 0].start()

    grad_a(ring_x.bwd)
    send_one(ha, 1, ring_x.bwd, ring_x.bwd)
    v = dot_tn(CAT[:, :, 0:128].reshape(2048, 128), DY[...].reshape(2048, 1024)).reshape(4, 4, 8, 1024)
    part["b"][:, :, 0:16, :] = jnp.concatenate([v, jnp.zeros_like(v)], 2).astype(BF)
    grad_b(ring_z.opp, ring_z.bwd)
    send_one(hb, 0, ring_z.opp, ring_z.fwd)
    send_one(hb, 1, ring_z.bwd, ring_z.bwd)
    grad_a(ring_x.fwd)
    for sub in subs:
        send_forward(ha, sub)
    grad_b(ring_z.fwd, ring_z.own)
    for sub in subs:
        send_forward(hb, sub)

    for a, src, _ in arrays:
        msgs.land(("y", a, 0))
        join(a, src, ring_y.fwd, extra=0)
        msgs.send(("y", a, 2), src.at[mine(ring_y.fwd)], from_y.at[a, 2], y_dev(ring_y.fwd))
    grad_a(ring_x.own)

    for k in range(3):
        msgs.land(("v1", k))
    vec_sum[...] = vec[...] + vec_one[0] + vec_one[1] + vec_one[2]
    for k, o in enumerate(z_others):
        msgs.send(("v2", k), vec_sum, vec_two.at[k], z_dev(o))

    for sub in ("opp", "bwd"):
        for h in halves:
            first_sum(h, sub)

    for k in range(3):
        msgs.land(("v2", k))
    vec_all[t] = vec_sum[...] + vec_two[0] + vec_two[1] + vec_two[2]
    for k, o in enumerate(others):
        msgs.send(("v3", k), vec_all.at[t], vec_all.at[t], group_member(x, z, o))

    for h in halves:
        first_sum(h, "fwd")

    v = first_sum(hb, "own")
    m["own_dense"][...] = v[0:8]
    grad_fc2[...] = v[16:48]

    @pl.when(moves)
    def _():
        msgs.sent["back"].start()

    @pl.when(jnp.logical_not(moves))
    def _():
        grad_dense[...] = m["own_dense"][...]

    fin_a = m["fin_a"]
    fin_a[...] = first_sum(ha, "own").reshape(8, 8, 896)
    for k, o in enumerate(others):
        msgs.send(("n", k), fin_a.at[o], n_all.at[t], group_member(x, z, o))
    n_all[t] = fin_a[t]

    for a, src, dst in arrays:
        msgs.land(("sib", a, 0))
        msgs.land(("y", a, 1))
        msgs.land(("y", a, 2))

        def add(r, a=a, src=src, dst=dst):
            v = src[mine(y), r, :].astype(F32) + sib[a, y, r, :].astype(F32)
            dst[r, :] = v + from_y[a, 1, r, :].astype(F32) + from_y[a, 2, r, :].astype(F32)

        slabs(256, 32, add)

    @pl.when(moves)
    def _():
        msgs.sent["there"].wait_send()
        msgs.sent["back"].wait()

    msgs.finish()


def whole(*args):
    vmem = pl.BlockSpec(memory_space=pltpu.VMEM)
    hbm = pl.BlockSpec(memory_space=pl.ANY)
    return pl.pallas_call(
        whole_kernel,
        out_shape=(
            jax.ShapeDtypeStruct((256, 1024), F32),
            jax.ShapeDtypeStruct((256, 1024), F32),
            jax.ShapeDtypeStruct((8, 8, 896), F32),
            jax.ShapeDtypeStruct((8, 1024), F32),
            jax.ShapeDtypeStruct((32, 1024), F32),
            jax.ShapeDtypeStruct((8, 8, 256), F32),
            jax.ShapeDtypeStruct((8, 1024), F32),
        ),
        in_specs=[hbm] * len(args),
        out_specs=(vmem,) * 7,
        scratch_shapes=[pltpu.VMEM(*spec) for spec in SCRATCH.values()]
        + [pltpu.SemaphoreType.DMA((MESSAGES,)), pltpu.SemaphoreType.DMA((MESSAGES,)), pltpu.SemaphoreType.DMA((8,))],
        compiler_params=pltpu.CompilerParams(
            collective_id=0, has_side_effects=True, vmem_limit_bytes=VMEM_LIMIT
        ),
        cost_estimate=pl.CostEstimate(flops=20_000_000_000, bytes_accessed=5_000_000, transcendentals=3_000_000),
        name="whole_block",
    )(*args)


def finish_kernel(*refs):
    given, results, held, sems = refs[:12], refs[12:26], refs[26:38], refs[38]
    copies = [pltpu.make_async_copy(src, dst, sems.at[n]) for n, (src, dst) in enumerate(zip(given, held))]
    for copy in copies:
        copy.start()
    for copy in copies:
        copy.wait()
    x_ref, dy_ref, out_sum, g_sum, n_all, dense_in, fc2_in, vec_all, b_out, small_ref, wqkv_ref, wfc1_ref = held
    (out_ref, dx_ref, g1_gain, g1_bias, g2_gain, g2_bias, grad_qkv, grad_b_qkv,
     grad_dense, grad_b_out, grad_fc1, grad_b_fc1, grad_fc2, grad_b_last) = results
    me = lax.axis_index("fsdp")
    small = small_ref[...].astype(F32)
    lives = [jnp.broadcast_to(small[b : b + 1, :], (128, 128)).T[:, 0:1] >= 0.0 for b in (1, 2)]
    live = jnp.concatenate([u.astype(F32) for u in lives], 0)
    x = x_ref[...].astype(F32)
    out_ref[...] = (x + live * (out_sum[...] + b_out[0:1, :])).astype(BF)
    centre = x - jnp.mean(x, 1, keepdims=True)
    scale = lax.rsqrt(jnp.mean(centre * centre, 1, keepdims=True) + NORM_EPS)
    normed = centre * scale
    g = g_sum[...]
    dx = (g - jnp.mean(g, 1, keepdims=True) - normed * jnp.mean(g * normed, 1, keepdims=True)) * scale
    dx_ref[...] = (dy_ref[...].astype(F32) + dx).astype(BF)

    row = lax.broadcasted_iota(jnp.int32, (8, 128), 0)
    lane = lax.broadcasted_iota(jnp.int32, (8, 128), 1)

    def column(start):
        return jnp.sum(jnp.where(lane == row + start, small[0:1, :], 0.0), 1, keepdims=True)

    def as_lanes(u):
        return jnp.sum(jnp.where(lane == row, u, 0.0), 0, keepdims=True)

    def write(ref, u, count):
        ref[...] = u[0:1, 0:count]

    def shifted(u, by):
        width = u.shape[1]
        return pltpu.roll(jnp.broadcast_to(u, (8, width)), lax.rem(width - by, width), 1)

    n_qkv = jnp.concatenate([n_all[t, :, c * 128 : c * 128 + 128] for c in range(3) for t in range(8)], 1)
    at = ((0, 0), (0, 128), (1, 0))
    s_qkv = jnp.concatenate([vec_all[t, r : r + 1, lo : lo + 128] for r, lo in at for t in range(8)], 1)
    both = []
    for t in range(8):
        sums = jnp.concatenate([vec_all[t, 1:2, 128:256], vec_all[t, 2:3, :], vec_all[t, 3:4, 0:128]], 1)
        both.append(jnp.concatenate([n_all[t, :, 384:896], jnp.broadcast_to(sums, (8, 512))], 0))
    fc1 = jnp.concatenate(
        [both[t][:, (q * 4 + p) * 32 : (q * 4 + p) * 32 + 32] for p in range(4) for q in range(4) for t in range(8)], 1
    )

    def norm_grads(weight, n, s, start, gain_ref, bias_ref, grad_ref):
        weight = weight.astype(F32)
        grad_ref[...] = column(start) * n + column(start + 8) * s
        write(gain_ref, as_lanes(jnp.sum(weight * n, 1, keepdims=True)), 8)
        write(bias_ref, as_lanes(jnp.sum(weight * s, 1, keepdims=True)), 8)

    s_fc1 = fc1[8:9]
    norm_grads(wqkv_ref[...], n_qkv, s_qkv, 0, g1_gain, g1_bias, grad_qkv)
    norm_grads(wfc1_ref[...], fc1[0:8], s_fc1, 16, g2_gain, g2_bias, grad_fc1)
    write(grad_b_qkv, shifted(s_qkv, me * 24), 24)
    write(grad_b_fc1, shifted(s_fc1, me * 32), 32)
    branch = jnp.concatenate([vec_all[0, r : r + 1, :] for r in range(4, 8)], 1)
    branch = shifted(branch, me * 8)
    write(grad_b_out, branch, 8)
    write(grad_b_last, branch, 8)
    grad_dense[...] = dense_in[...]
    grad_fc2[...] = fc2_in[...]


def finish(*args):
    flat = lambda count: jax.ShapeDtypeStruct((1, count), F32)
    full = lambda *shape: jax.ShapeDtypeStruct(shape, F32)
    rows = jax.ShapeDtypeStruct((256, 1024), BF)
    outs = pl.pallas_call(
        finish_kernel,
        out_shape=(rows, rows, flat(8), flat(8), flat(8), flat(8), full(8, 3072), flat(24), full(8, 1024), flat(8),
                   full(8, 4096), flat(32), full(32, 1024), flat(8)),
        in_specs=[pl.BlockSpec(memory_space=pl.ANY)] * len(args),
        scratch_shapes=[pltpu.VMEM(u.shape, u.dtype) for u in args] + [pltpu.SemaphoreType.DMA((len(args),))],
        compiler_params=pltpu.CompilerParams(vmem_limit_bytes=VMEM_LIMIT),
        cost_estimate=pl.CostEstimate(flops=20_000_000, bytes_accessed=6_000_000, transcendentals=0),
        name="finish",
    )(*args)
    return tuple(u.reshape(-1) if u.shape[0] == 1 else u for u in outs)


def body(tokens, segments, grad_out, ln1_gain, ln1_bias, ln2_gain, ln2_bias, w_qkv, b_qkv,
         w_dense, b_dense, w_fc1, b_fc1, w_fc2, b_fc2):
    small = jnp.pad(segments.astype(BF), ((1, 5), (0, 0)))
    at = 0
    for vector in (ln1_gain, ln1_bias, ln2_gain, ln2_bias, b_qkv, b_fc1, b_dense, b_fc2):
        small = small + jnp.pad(vector[None], ((0, 7), (at, 128 - at - vector.shape[0])))
        at += vector.shape[0]
    out_sum, g_sum, n_all, grad_dense, grad_fc2, sums, b_out = whole(
        tokens, grad_out, w_qkv, w_fc1, w_dense, w_fc2, small, jnp.asarray(rotary_table())
    )

    return finish(
        tokens, grad_out, out_sum, g_sum, n_all, grad_dense, grad_fc2, sums, b_out, small, w_qkv, w_fc1
    )


def solution(mesh):
    rows, flat = P("fsdp", None), P("fsdp")
    return jax.shard_map(
        body,
        mesh=mesh,
        in_specs=(rows, rows, rows, flat, flat, flat, flat, rows, flat, rows, flat, rows, flat, rows, flat),
        out_specs=(rows, rows, flat, flat, flat, flat, rows, flat, rows, flat, rows, flat, rows, flat),
        check_vma=False,
    )
```
